32 devices in a mesh: rows: 4 (over y, core), chan: 8 (over z, x).
Axes of the slice: x: 2, y: 2, z: 4, core: 2. Of those that a mesh axis runs over, the one named last changes fastest.
Arguments:
- activations: bfloat16 [5120, 1536], P(('rows', 'chan')), may hold values from -6 to 6
- condition: bfloat16 [8, 1536], P('rows'), may hold values from -6 to 6
- seq_lengths: int32 [4, 2], P('rows'), may hold values from 1 to 1024, 1280 in all within a row
- w_ada: bfloat16 [3, 1536, 1536], P(None, 'chan'), may hold values from -0.15625 to 0.15625
- b_ada: float32 [3, 1536], P(None, 'chan'), may hold values from -3 to 3
- norm_gain: float32 [1536], P('chan'), may hold values from 0.25 to 1.75
- w_in_x: bfloat16 [3072, 1536], P('chan'), may hold values from -0.15625 to 0.15625
- w_in_z: bfloat16 [3072, 1536], P('chan'), may hold values from -0.15625 to 0.15625
- conv_weight: float32 [3072, 4], P('chan'), may hold values from -3 to 3
- conv_bias: float32 [3072], P('chan'), may hold values from -1 to 1
- w_xproj: bfloat16 [3072, 128], P('chan'), may hold values from -0.109375 to 0.109375
- w_dt: bfloat16 [96, 3072], P(None, 'chan'), may hold values from -0.625 to 0.625
- dt_bias: float32 [3072], P('chan'), may hold values from -6.9 to -2.3
- a_log: float32 [3072, 16], P('chan'), may hold values from 0 to 2.77
- d_skip: float32 [3072], P('chan'), may hold values from 0.5 to 1.5
- w_out: bfloat16 [3072, 1536], P('chan'), may hold values from -0.3125 to 0.3125
- grad_out: bfloat16 [5120, 1536], P(('rows', 'chan')), may hold values from -6 to 6
Outputs:
- block_out: bfloat16 [5120, 1536], P(('rows', 'chan'))
- grad_input: bfloat16 [5120, 1536], P(('rows', 'chan'))
- grad_w_ada: float32 [3, 1536, 1536], P(None, 'chan')
- grad_b_ada: float32 [3, 1536], P(None, 'chan')
- grad_gain: float32 [1536], P('chan')
- grad_w_in_x: float32 [3072, 1536], P('chan')
- grad_w_in_z: float32 [3072, 1536], P('chan')
- grad_conv_weight: float32 [3072, 4], P('chan')
- grad_conv_bias: float32 [3072], P('chan')
- grad_w_xproj: float32 [3072, 128], P('chan')
- grad_w_dt: float32 [96, 3072], P(None, 'chan')
- grad_dt_bias: float32 [3072], P('chan')
- grad_a_log: float32 [3072, 16], P('chan')
- grad_d_skip: float32 [3072], P('chan')
- grad_w_out: float32 [3072, 1536], P('chan')
The draws below stay inside these ranges and needn't reach their ends.
Inputs may be any that keep to these rules, and one draw needn't show every extreme that they name: `seq_lengths`: row r lists, in order, the lengths of the 2 sequences packed into the 1280 tokens of index r of rows; they sum to 1280.
All inputs are finite; a program needn't handle non-finite values.
Results may differ from the reference program's by a relative error of at most 0.012.
The reference program's roundings to bfloat16 on the way count: a program that leaves them out, or rounds other values in their place, can miss the bound.
Values may be sent and summed in bfloat16 or wider, within the bound.
No kernel may reach another device: no remote copies, remote signals or barrier semaphores. Data moves between devices by JAX's collectives and lax.ppermute only.
A program may use at most 576 MiB of HBM per device.

```python
import math
import jax
import jax.numpy as jnp
import numpy as np
from jax import lax

D = 1536
E = 3072
N = 16
R = 96
K = 4
SEQ_MAX = 1024
TOK_DEV = 1280
SEQ_DEV = 2
TOKENS = 5120
NSEQ = 8
N_ROWS = 4


def block_levels(key, shape, cuts, low, high):
    factor_of, own = 1.0, jax.random.fold_in(key, 6)
    for dim, blocks in cuts:
        steps = jnp.exp(jax.random.uniform(jax.random.fold_in(own, dim), (blocks,), jnp.float32, low / len(cuts), high / len(cuts)))
        factor_of = factor_of * jnp.repeat(steps, shape[dim] // blocks).reshape([-1 if axis == dim else 1 for axis in range(len(shape))])
    return factor_of


def split_up(number_of, total, bound, skew):
    portions = [(1 << 20) // math.isqrt(grade ** skew) + 1 for grade in range(2, number_of + 1)]
    surplus, holding = total - bound - (number_of - 1), [1] * (number_of - 1)
    while surplus > 0:
        movable = [i for i in range(number_of - 1) if holding[i] < bound]
        pool, remaining = sum([portions[i] for i in movable]), surplus
        for i in movable:
            more = min(bound - holding[i], max(1, remaining * portions[i] // pool), surplus)
            holding[i] = holding[i] + more
            surplus = surplus - more
    return np.array([bound] + holding)


def uneven(rng, number_of, total, limit, lean):
    if number_of == 2:
        one = jax.random.randint(rng, (), max(1, total - limit), min(limit, total - 1) + 1)
        return jnp.stack([one, total - one])
    sizes = jnp.asarray(split_up(number_of, total, limit, lean), jnp.int32)
    couples = (number_of - 1) // 2
    source_of, sink = sizes[1:1 + 2 * couples:2], sizes[2:2 + 2 * couples:2]
    room = jnp.minimum(source_of - 1, limit - sink)
    passed = jax.random.randint(jax.random.fold_in(rng, 1), (couples,), 0, 1 << 20) % (room + 1)
    sizes = sizes.at[1:1 + 2 * couples:2].set(source_of - passed).at[2:2 + 2 * couples:2].set(sink + passed)
    return sizes[jax.random.permutation(jax.random.fold_in(rng, 2), number_of)]


def gaussian(key, dims, width, most, split=(), kind=jnp.bfloat16):
    drawn = jax.random.normal(key, dims, jnp.float32) * width
    if len(split) > 0:
        drawn = block_levels(key, dims, split, -0.22, 0.18) * drawn
    return jnp.clip(drawn, min=-most, max=most).astype(kind)


def setup_inputs(seed: int = 0) -> dict:
    arg_keys = jax.random.split(jax.random.key(seed), 18)
    return {
        "activations": gaussian(arg_keys[0], (TOKENS, D), 1.0, 6.0, ((0, 32),)),
        "condition": gaussian(arg_keys[1], (NSEQ, D), 1.0, 6.0, ((0, 4),)),
        "seq_lengths": jax.vmap(lambda own: uneven(own, SEQ_DEV, TOK_DEV, SEQ_MAX, 2))(jax.random.split(arg_keys[2], N_ROWS)).reshape((N_ROWS, SEQ_DEV)).astype(jnp.int32),
        "w_ada": gaussian(arg_keys[3], (3, D, D), D ** -0.5, 0.15625, ((1, 8),)),
        "b_ada": gaussian(arg_keys[4], (3, D), 0.5, 3.0, ((1, 8),), jnp.float32),
        "norm_gain": jnp.clip(1.0 + 0.15 * jax.random.normal(arg_keys[5], (D,), jnp.float32), 0.25, 1.75),
        "w_in_x": gaussian(arg_keys[6], (E, D), D ** -0.5, 0.15625, ((0, 8),)),
        "w_in_z": gaussian(arg_keys[7], (E, D), D ** -0.5, 0.15625, ((0, 8),)),
        "conv_weight": gaussian(arg_keys[8], (E, K), K ** -0.5, 3.0, ((0, 8),), jnp.float32),
        "conv_bias": jnp.clip(jax.random.uniform(arg_keys[9], (E,), jnp.float32, -1.0, 1.0) * block_levels(arg_keys[9], (E,), ((0, 8),), -0.4, 0.0), -1.0, 1.0),
        "w_xproj": gaussian(arg_keys[10], (E, R + 2 * N), E ** -0.5, 0.109375, ((0, 8),)),
        "w_dt": gaussian(arg_keys[11], (R, E), R ** -0.5, 0.625, ((1, 8),)),
        "dt_bias": jnp.clip(-6.9 + 4.6000001430511475 * jax.random.uniform(arg_keys[12], (E,), jnp.float32) ** block_levels(arg_keys[12], (E,), ((0, 8),), -0.2, 0.2), -6.9, -2.3),
        "a_log": jnp.clip(2.77 * jax.random.uniform(arg_keys[13], (E, N), jnp.float32) ** block_levels(arg_keys[13], (E, N), ((0, 8),), -0.2, 0.2), 0.0, 2.77),
        "d_skip": jnp.clip(0.5 + 1.0 * jax.random.uniform(arg_keys[14], (E,), jnp.float32) ** block_levels(arg_keys[14], (E,), ((0, 8),), -0.2, 0.2), 0.5, 1.5),
        "w_out": gaussian(arg_keys[15], (E, D), (E // 8) ** -0.5, 0.3125, ((0, 8),)),
        "grad_out": gaussian(arg_keys[16], (TOKENS, D), 1.0, 6.0, ((0, 32),)),
    }


EPSILON = 1e-06
HIGHEST = lax.Precision.HIGHEST

@jax.custom_vjp
def low(v):
    return lax.optimization_barrier(v.astype(jnp.bfloat16)).astype(jnp.float32)

@jax.custom_vjp
def low_back(v):
    return v

def low_keep(v):
    return (low(v), None)

def low_pass(kept, grad):
    return (grad,)

def back_keep(v):
    return (v, None)

def back_low(kept, grad):
    return (low(grad),)
low.defvjp(low_keep, low_pass)
low_back.defvjp(back_keep, back_low)

def exact_dot(left, right):
    return jnp.dot(left, right, precision=HIGHEST, preferred_element_type=jnp.float32)

def combine_pairs(earlier, later):
    return (earlier[0] * later[0], later[0] * earlier[1] + later[1])

def linear_scan(coeffs, drives):
    return lax.associative_scan(combine_pairs, (coeffs, drives), axis=0)[1]

def delay_rows(operand, lag):
    if lag == 0:
        return operand
    padding = jnp.zeros((lag,) + operand.shape[1:], operand.dtype)
    return jnp.concatenate([padding, operand[:-lag]], axis=0)

def scan_block(pieces, b_mat, c_mat, keep_fwd, keep_bwd):
    deltas, act_block, log_block = pieces
    a_neg = -jnp.exp(log_block).T
    decay = jnp.exp(deltas[:, None, :] * a_neg[None])
    drive = (deltas * act_block)[:, None, :] * b_mat[:, :, None]
    state_fwd = linear_scan(decay * keep_fwd[:, None, None], drive)
    state_bwd = jnp.flip(linear_scan(jnp.flip(decay * keep_bwd[:, None, None], 0), jnp.flip(drive, 0)), 0)
    return lax.optimization_barrier(jnp.sum((state_fwd + state_bwd) * c_mat[:, :, None], axis=1))

def forward(wide, w_ada, b_ada, norm_gain, w_in_x, w_in_z, conv_weight, conv_bias, w_xproj, w_dt, dt_bias, a_log, d_skip, w_out, cond_act, onehot, keep_fwd, keep_bwd, in_seq):
    seq_total = cond_act.shape[0]
    modulation = exact_dot(cond_act, w_ada.reshape(3 * D, D).T).reshape(seq_total, 3, D) + b_ada[None]
    tok_mod = exact_dot(onehot, modulation.reshape(seq_total, 3 * D))
    shift_tok = tok_mod[:, :D]
    scale_tok = tok_mod[:, D:2 * D]
    gate_tok = tok_mod[:, 2 * D:]
    centred = wide - lax.optimization_barrier(jnp.mean(wide, axis=1, keepdims=True))
    normed = centred * lax.rsqrt(lax.optimization_barrier(jnp.mean(centred * centred, axis=1, keepdims=True)) + EPSILON)
    xmod = low(normed * norm_gain[None] * (1.0 + scale_tok) + shift_tok)
    x_inner = low_back(exact_dot(xmod, w_in_x.T))
    z_inner = low_back(exact_dot(xmod, w_in_z.T))
    conv_pre = jnp.zeros_like(x_inner) + conv_bias[None, :]
    for tap_index in range(K):
        lag = K - 1 - tap_index
        valid = (in_seq >= lag).astype(jnp.float32)[:, None]
        conv_pre = conv_pre + conv_weight[:, tap_index][None, :] * delay_rows(x_inner, lag) * valid
    act = low(jax.nn.silu(conv_pre))
    proj = low_back(exact_dot(act, w_xproj))
    dt_low = low(proj[:, :R])
    b_mat = proj[:, R:R + N]
    c_mat = proj[:, R + N:]
    deltas = jax.nn.softplus(low_back(exact_dot(dt_low, w_dt)) + dt_bias[None])
    block_width = min(E, 128)
    block_count = E // block_width
    total = deltas.shape[0]
    delta_blocks = deltas.reshape(total, block_count, block_width).transpose(1, 0, 2)
    act_blocks = act.reshape(total, block_count, block_width).transpose(1, 0, 2)
    log_blocks = a_log.reshape(block_count, block_width, N)
    runner = jax.checkpoint(lambda pieces: scan_block(pieces, b_mat, c_mat, keep_fwd, keep_bwd))
    scanned = lax.map(runner, (delta_blocks, act_blocks, log_blocks))
    scanned = scanned.transpose(1, 0, 2).reshape(total, E)
    mixed = scanned + d_skip[None] * act
    gated = low(mixed * jax.nn.silu(z_inner))
    branch = low_back(exact_dot(gated, w_out))
    return wide + gate_tok * branch

def reference(activations, condition, seq_lengths, w_ada, b_ada, norm_gain, w_in_x, w_in_z, conv_weight, conv_bias, w_xproj, w_dt, dt_bias, a_log, d_skip, w_out, grad_out):
    seq_lens = seq_lengths.astype(jnp.int32)
    seq_ends = jnp.cumsum(seq_lens, axis=1).astype(jnp.int32)
    row_base = (jnp.arange(N_ROWS, dtype=jnp.int32) * TOK_DEV)[:, None]
    begins = (seq_ends - seq_lens + row_base).reshape(-1)
    finals = (seq_ends - 1 + row_base).reshape(-1)
    position = jnp.arange(TOKENS, dtype=jnp.int32)
    member = (position[:, None] >= begins[None, :]) & (position[:, None] <= finals[None, :])
    onehot = member.astype(jnp.float32)
    keep_fwd = 1.0 - jnp.any(position[:, None] == begins[None, :], axis=1).astype(jnp.float32)
    keep_bwd = 1.0 - jnp.any(position[:, None] == finals[None, :], axis=1).astype(jnp.float32)
    in_seq = lax.optimization_barrier(jnp.sum(onehot * (position[:, None] - begins[None, :]).astype(jnp.float32), axis=1))
    cond_act = low(jax.nn.silu(condition.astype(jnp.float32)))

    def run(wide, p_ada, p_bada, p_gain, p_inx, p_inz, p_convw, p_convb, p_xproj, p_wdt, p_dtb, p_alog, p_skip, p_out):
        return forward(wide, p_ada, p_bada, p_gain, p_inx, p_inz, p_convw, p_convb, p_xproj, p_wdt, p_dtb, p_alog, p_skip, p_out, cond_act, onehot, keep_fwd, keep_bwd, in_seq)
    result, puller = jax.vjp(run, activations.astype(jnp.float32), w_ada.astype(jnp.float32), b_ada.astype(jnp.float32), norm_gain.astype(jnp.float32), w_in_x.astype(jnp.float32), w_in_z.astype(jnp.float32), conv_weight.astype(jnp.float32), conv_bias.astype(jnp.float32), w_xproj.astype(jnp.float32), w_dt.astype(jnp.float32), dt_bias.astype(jnp.float32), a_log.astype(jnp.float32), d_skip.astype(jnp.float32), w_out.astype(jnp.float32))
    grads = puller(grad_out.astype(jnp.float32))
    return (result.astype(jnp.bfloat16), grads[0].astype(jnp.bfloat16), grads[1], grads[2], grads[3], grads[4], grads[5], grads[6], grads[7], grads[8], grads[9], grads[10], grads[11], grads[12], grads[13])
```

```python
import functools, math
import jax, jax.numpy as jnp
from jax import lax
from jax.experimental import pallas as pl
from jax.experimental.pallas import tpu as pltpu
from jax.sharding import PartitionSpec as P
CHUNK=16
LOG2E=math.log2(math.e)
f32=jnp.float32; bf16=jnp.bfloat16

def scan_kernel(n_seq, row_mode, begins_ref, delta_ref, act_ref, dm_ref, an_ref, bt_ref, ct_ref, cblk_ref, bblk_ref,
                y_ref, dd_ref, da_ref, ga_ref, dbm_ref, dcm_ref, pf_s, db_s, drv_b, both_b, dd_b, de_b, darow_s):
    T, C = delta_ref.shape
    N = an_ref.shape[0]
    n_chunks = T // CHUNK
    an = an_ref[...]
    a2 = an * LOG2E

    def rows(ref, t):
        if row_mode == 0:
            return ref[pl.ds(t, 1), :]
        half = ref[pl.ds(t, 8, stride=0), :]
        return jnp.concatenate([half, half], axis=0)

    def prep(c):
        base = pl.multiple_of(c * CHUNK, CHUNK)
        darow_s[...] = delta_ref[pl.ds(base, CHUNK), :] * act_ref[pl.ds(base, CHUNK), :].astype(f32)
        return base

    def has_start(base, shift):
        hit = False
        for s in range(1, n_seq):
            at = begins_ref[0, s] - shift
            here = (at >= base) & (at < base + CHUNK)
            hit = here if hit is False else (hit | here)
        return hit

    def keep_at(t, shift):
        keep = None
        for s in range(1, n_seq):
            k = jnp.where(begins_ref[0, s] - shift == t, 0.0, 1.0).astype(f32)
            keep = k if keep is None else keep * k
        return keep

    def forward(c, carry):
        base = prep(c)
        bt = bt_ref[c]
        ct = ct_ref[c]

        def run(masked, sf, g):
            for i in range(CHUNK):
                decay = jnp.exp2(rows(delta_ref, base + i) * a2)
                drive = rows(darow_s, i) * bt[:, i : i + 1]
                if masked:
                    keep = keep_at(base + i, 0)
                    sf = sf * keep
                    g = g * keep
                pf = decay * sf
                sf = pf + drive
                db = rows(dm_ref, base + i) * ct[:, i : i + 1] + g
                g = decay * db
                at = pl.multiple_of(base * N + i * N, N)
                pf_s[pl.ds(at, N), :] = pf
                db_s[pl.ds(at, N), :] = db
            return sf, g

        if n_seq == 1:
            return run(False, *carry)
        return lax.cond(has_start(base, 0), functools.partial(run, True), functools.partial(run, False), *carry)

    zero = jnp.zeros((N, C), f32)
    lax.fori_loop(0, n_chunks, forward, (zero, zero))
    tile = pl.program_id(0)
    r = lax.broadcasted_iota(jnp.int32, (CHUNK, CHUNK * N), 0)
    q = lax.broadcasted_iota(jnp.int32, (CHUNK, CHUNK * N), 1) // N
    diag = (r == q).astype(f32)
    ones_blk = diag.astype(bf16)

    def backward(k, carry):
        c = n_chunks - 1 - k
        base = prep(c)
        bt = bt_ref[c]
        ct = ct_ref[c]

        def run(masked, sb, g, ga):
            for i in range(CHUNK - 1, -1, -1):
                drow = rows(delta_ref, base + i)
                decay = jnp.exp2(drow * a2)
                drive = rows(darow_s, i) * bt[:, i : i + 1]
                if masked:
                    keep = keep_at(base + i, 1)
                    sb = sb * keep
                    g = g * keep
                pb = decay * sb
                sb = pb + drive
                df = rows(dm_ref, base + i) * ct[:, i : i + 1] + g
                g = decay * df
                at = pl.multiple_of(base * N + i * N, N)
                pf = pf_s[pl.ds(at, N), :]
                db = db_s[pl.ds(at, N), :]
                d_expo = df * pf + db * pb
                ga = ga + d_expo * drow
                both_b[i * N : (i + 1) * N, :] = (pf + drive + sb).astype(bf16)
                dd_b[i * N : (i + 1) * N, :] = (df + db).astype(bf16)
                de_b[i * N : (i + 1) * N, :] = (d_expo * an).astype(bf16)
            return sb, g, ga

        if n_seq == 1:
            carry = run(False, *carry)
        else:
            carry = lax.cond(has_start(base, 1), functools.partial(run, True), functools.partial(run, False), *carry)
        here = pl.ds(base, CHUNK)
        both = both_b[...]
        ddv = dd_b[...]
        y_ref[here, :] = jnp.dot(cblk_ref[here, :], both, preferred_element_type=f32)
        through = jnp.dot(bblk_ref[here, :], ddv, preferred_element_type=f32)
        expo = jnp.dot(ones_blk, de_b[...], preferred_element_type=f32)
        delta = delta_ref[here, :]
        dd_ref[here, :] = expo + through * act_ref[here, :].astype(f32)
        da_ref[here, :] = through * delta
        tdot = functools.partial(lax.dot_general, dimension_numbers=(((1,), (1,)), ((), ())), preferred_element_type=f32)
        dcm = jnp.sum(tdot(dm_ref[here, :].astype(bf16), both) * diag, axis=0, keepdims=True)
        dbm = jnp.sum(tdot(darow_s[...].astype(bf16), ddv) * diag, axis=0, keepdims=True)

        @pl.when(tile == 0)
        def _():
            dcm_ref[pl.ds(c, 1), :] = dcm
            dbm_ref[pl.ds(c, 1), :] = dbm

        @pl.when(tile != 0)
        def _():
            dcm_ref[pl.ds(c, 1), :] += dcm
            dbm_ref[pl.ds(c, 1), :] += dbm

        return carry

    _, _, ga = lax.fori_loop(0, n_chunks, backward, (zero, zero, zero))
    ga_ref[...] = ga


def scans(deltas, act_low, d_mixed, a_neg, b_mat, c_mat, begins, row_mode=0):
    T, C = deltas.shape
    N = a_neg.shape[0]
    tile = 128 if C % 128 == 0 else C
    n_tiles = C // tile
    n_chunks = T // CHUNK
    bt = b_mat.reshape(n_chunks, CHUNK, N).transpose(0, 2, 1)
    ct = c_mat.reshape(n_chunks, CHUNK, N).transpose(0, 2, 1)
    same = (jnp.arange(T)[:, None] % CHUNK == jnp.arange(CHUNK * N)[None, :] // N)
    blk = lambda m: jnp.where(same, jnp.tile(m, (1, CHUNK)), 0.0).astype(bf16)
    col = lambda: pl.BlockSpec((T, tile), lambda j: (0, j))
    fix = lambda shape: pl.BlockSpec(shape, lambda j: (0,) * len(shape))
    sds = jax.ShapeDtypeStruct
    out = pl.pallas_call(
        functools.partial(scan_kernel, begins.shape[1], row_mode),
        grid=(n_tiles,),
        in_specs=[pl.BlockSpec(memory_space=pltpu.SMEM), col(), col(), col(), pl.BlockSpec((N, tile), lambda j: (0, j)),
                  fix(bt.shape), fix(ct.shape), fix((T, CHUNK * N)), fix((T, CHUNK * N))],
        out_specs=[col(), col(), col(), pl.BlockSpec((N, tile), lambda j: (0, j)), fix((n_chunks, CHUNK * N)), fix((n_chunks, CHUNK * N))],
        out_shape=[sds((T, C), f32), sds((T, C), f32), sds((T, C), f32), sds((N, C), f32),
                   sds((n_chunks, CHUNK * N), f32), sds((n_chunks, CHUNK * N), f32)],
        scratch_shapes=[pltpu.VMEM((T * N, tile), f32), pltpu.VMEM((T * N, tile), f32), pltpu.VMEM((CHUNK, tile), f32),
                        pltpu.VMEM((CHUNK * N, tile), bf16), pltpu.VMEM((CHUNK * N, tile), bf16), pltpu.VMEM((CHUNK * N, tile), bf16),
                        pltpu.VMEM((CHUNK, tile), f32)],
        compiler_params=pltpu.CompilerParams(vmem_limit_bytes=56 * 2**20, dimension_semantics=("arbitrary",)),
        cost_estimate=pl.CostEstimate(flops=T * C * N * 60, bytes_accessed=T * C * 24, transcendentals=2 * T * C * N),
        name="scan_all",
    )(begins, deltas, act_low, d_mixed, a_neg, bt, ct, blk(c_mat), blk(b_mat))
    y, dd, da, ga, dbm, dcm = out
    return y, dd, da, ga, dbm.reshape(T, N), dcm.reshape(T, N)


EPSILON = 1e-06
HIGHEST = lax.Precision.HIGHEST


def low_dot(left, right):
    return jnp.dot(left, right, preferred_element_type=f32)


def dot_across(left, right):
    return lax.dot_general(left, right, (((1,), (1,)), ((), ())), preferred_element_type=f32)


def dot_tokens(left, right):
    return lax.dot_general(left, right, (((0,), (0,)), ((), ())), preferred_element_type=f32)


def delay_rows(operand, lag):
    if lag == 0:
        return operand
    padding = jnp.zeros((lag,) + operand.shape[1:], operand.dtype)
    return jnp.concatenate([padding, operand[:-lag]], axis=0)


def advance_rows(operand, lag):
    if lag == 0:
        return operand
    padding = jnp.zeros((lag,) + operand.shape[1:], operand.dtype)
    return jnp.concatenate([operand[lag:], padding], axis=0)


def silu_slope(operand):
    squash = jax.nn.sigmoid(operand)
    return squash * (1.0 + operand * (1.0 - squash))


def ring_order(n):
    down = 4 if n % 8 == 0 else 1
    across = n // down
    order = [i * across for i in range(down)]
    for back, i in enumerate(reversed(range(down))):
        row = range(1, across) if back % 2 == 0 else reversed(range(1, across))
        order += [i * across + j for j in row]
    return order


class Ring:
    def __init__(self):
        self.n = lax.axis_size("chan")
        self.order = ring_order(self.n)
        self.table = jnp.array(self.order, jnp.int32)
        place = [0] * self.n
        for k, i in enumerate(self.order):
            place[i] = k
        self.place = jnp.array(place, jnp.int32)[lax.axis_index("chan")]
        self.right = [(self.order[k], self.order[(k + 1) % self.n]) for k in range(self.n)]
        self.left = [(b, a) for a, b in self.right]

    def owner(self, away):
        return self.table[(self.place + away + self.n) % self.n]

    def go_right(self, x):
        return lax.ppermute(x, "chan", self.right)

    def go_left(self, x):
        return lax.ppermute(x, "chan", self.left)

    def blocks(self, x):
        half = self.n // 2
        cut = x.shape[0] // 2
        from_left, from_right = x, x
        found = [(self.owner(0), x)]
        for step in range(1, half):
            from_left, from_right = self.go_right(from_left), self.go_left(from_right)
            found += [(self.owner(-step), from_left), (self.owner(step), from_right)]
        far = jnp.concatenate([self.go_right(from_left[:cut]), self.go_left(from_right[cut:])], axis=0)
        return found + [(self.owner(half), far)]

    def gather(self, x):
        rows = x.shape[0]
        whole = jnp.zeros((self.n * rows,) + x.shape[1:], x.dtype)
        for owner, block in self.blocks(x):
            whole = lax.dynamic_update_slice_in_dim(whole, block, owner * rows, 0)
        return whole

    def scatter(self, part):
        half = self.n // 2
        rows = part.shape[0] // self.n
        cut = rows // 2
        mine = lambda away: lax.dynamic_slice_in_dim(part, self.owner(away) * rows, rows, 0)
        wide = lambda v: v.astype(f32)
        far = mine(half).astype(bf16)
        right, left = self.go_right(far[:cut]), self.go_left(far[cut:])
        for away in range(half - 1, 0, -1):
            ahead, behind = wide(mine(away)), wide(mine(-away))
            if away == half - 1:
                ahead = jnp.concatenate([ahead[:cut] + wide(right), ahead[cut:]], axis=0)
                behind = jnp.concatenate([behind[:cut], behind[cut:] + wide(left)], axis=0)
            else:
                ahead, behind = ahead + wide(right), behind + wide(left)
            right, left = self.go_right(ahead.astype(bf16)), self.go_left(behind.astype(bf16))
        return wide(mine(0)) + wide(right) + wide(left)


def is_power(n):
    return n & (n - 1) == 0


def bits_of(n):
    return [1 << b for b in range(n.bit_length() - 1)]


def sum_chan(x, wire):
    n = lax.axis_size("chan")
    index = lax.axis_index("chan")
    if not is_power(n) or x.shape[0] % (16 * n):
        return lax.psum(x, "chan")
    perm = lambda b: [(i, i ^ b) for i in range(n)]
    for b in bits_of(n):
        h = x.shape[0] // 2
        upper = (index // b) % 2
        keep = lax.dynamic_slice_in_dim(x, upper * h, h, 0)
        send = lax.dynamic_slice_in_dim(x, (1 - upper) * h, h, 0)
        x = keep + lax.ppermute(send.astype(wire), "chan", perm(b)).astype(f32)
    x = x.astype(wire)
    for b in reversed(bits_of(n)):
        upper = (index // b) % 2
        other = lax.ppermute(x, "chan", perm(b))
        x = jnp.concatenate([jnp.where(upper == 0, x, other), jnp.where(upper == 0, other, x)], axis=0)
    return x


def small_gather(x, axis):
    n = lax.axis_size(axis)
    if not is_power(n) or n > 8:
        return lax.all_gather(x, axis, axis=0)
    index = lax.axis_index(axis)
    every = jnp.stack([x] + [lax.ppermute(x, axis, [(i, i ^ k) for i in range(n)]) for k in range(1, n)])
    return unmix(every, index, n)


def unmix(every, index, n):
    shape = every.shape
    levels = bits_of(n)
    every = every.reshape((2,) * len(levels) + shape[1:])
    for place, b in enumerate(reversed(levels)):
        every = jnp.where((index // b) % 2 == 1, jnp.flip(every, place), every)
    return every.reshape(shape)


def small_scatter(x):
    n = lax.axis_size("chan")
    if not is_power(n) or n > 8:
        return lax.psum_scatter(x, "chan", scatter_dimension=0, tiled=False)
    mixed = unmix(x, lax.axis_index("chan"), n)
    return sum([lax.ppermute(mixed[k], "chan", [(i, i ^ k) for i in range(n)]) for k in range(1, n)], mixed[0])


def sum_rows(x, wire):
    n = lax.axis_size("rows")
    if n != 4:
        return lax.psum(x, "rows")
    core = [(0, 1), (1, 0), (2, 3), (3, 2)]
    chip = [(0, 2), (2, 0), (1, 3), (3, 1)]
    upper = lax.axis_index("rows") % 2
    h = x.shape[0] // 2
    keep = lax.dynamic_slice_in_dim(x, upper * h, h, 0)
    send = lax.dynamic_slice_in_dim(x, (1 - upper) * h, h, 0)
    pair = (keep + lax.ppermute(send, "rows", core)).astype(wire)
    total = pair.astype(f32) + lax.ppermute(pair, "rows", chip).astype(f32)
    other = lax.ppermute(total, "rows", core)
    return jnp.concatenate([jnp.where(upper == 0, total, other), jnp.where(upper == 0, other, total)], axis=0)


def local(
    activations,
    condition,
    seq_lengths,
    w_ada,
    b_ada,
    norm_gain,
    w_in_x,
    w_in_z,
    conv_weight,
    conv_bias,
    w_xproj,
    w_dt,
    dt_bias,
    a_log,
    d_skip,
    w_out,
    grad_out,
):
    ring = Ring()
    tok_loc, width = activations.shape
    low_rank = w_dt.shape[0]
    states = a_log.shape[1]
    channels = a_log.shape[0]
    conv_taps = conv_weight.shape[1]
    parts = lax.axis_size("chan")
    tok_count = tok_loc * parts
    tok_start = lax.axis_index("chan") * tok_loc
    seq_lens = seq_lengths[0]
    seq_count = seq_lens.shape[0]
    seq_ends = jnp.cumsum(seq_lens)
    begins = seq_ends - seq_lens
    position = jnp.arange(tok_count, dtype=jnp.int32)
    member = (position[:, None] >= begins[None, :]) & (position[:, None] < seq_ends[None, :])
    onehot = member.astype(f32)
    in_seq = jnp.sum(onehot * (position[:, None] - begins[None, :]).astype(f32), axis=1)
    per_token = lambda rows, hot: sum(hot[:, s : s + 1] * rows[s][None] for s in range(seq_count))
    cond_act = jax.nn.silu(condition.astype(f32)).astype(bf16)
    cond_all = small_gather(cond_act, "rows").reshape(-1, width)
    modulation = (
        jnp.einsum("si,kji->skj", cond_act, w_ada, preferred_element_type=f32) + b_ada[None]
    )
    part_width = norm_gain.shape[0]
    packed = jnp.concatenate([modulation.reshape(3 * seq_count, part_width), norm_gain[None]], axis=0)
    packed = small_gather(packed, "chan").transpose(1, 0, 2).reshape(3 * seq_count + 1, width)
    mod_full = packed[: 3 * seq_count].reshape(seq_count, 3, width)
    gain_full = packed[3 * seq_count]
    whole = ring.gather(activations)
    whole_up = ring.gather(grad_out)
    shift_tok = per_token(mod_full[:, 0], onehot)
    scale_tok = per_token(mod_full[:, 1], onehot)
    gate_tok = per_token(mod_full[:, 2], onehot)
    wide = whole.astype(f32)
    centred = wide - jnp.mean(wide, axis=1, keepdims=True)
    inv_std = lax.rsqrt(jnp.mean(centred * centred, axis=1, keepdims=True) + EPSILON)
    normed = centred * inv_std
    xmod = (normed * gain_full[None] * (1.0 + scale_tok) + shift_tok).astype(bf16)
    x_inner = dot_across(xmod, w_in_x)
    conv_pre = jnp.zeros_like(x_inner) + conv_bias[None, :]
    for tap_index in range(conv_taps):
        lag = conv_taps - 1 - tap_index
        valid = (in_seq >= lag).astype(f32)[:, None]
        conv_pre = conv_pre + conv_weight[:, tap_index][None, :] * delay_rows(x_inner, lag) * valid
    act_low = jax.nn.silu(conv_pre).astype(bf16)
    act = act_low.astype(f32)
    proj = sum_chan(low_dot(act_low, w_xproj), PROJ_WIRE)
    dt_low = proj[:, :low_rank].astype(bf16)
    b_mat = proj[:, low_rank : low_rank + states].astype(f32)
    c_mat = proj[:, low_rank + states :].astype(f32)
    dt_raw = low_dot(dt_low, w_dt) + dt_bias[None, :]
    deltas = jax.nn.softplus(dt_raw)
    a_neg = -jnp.exp(a_log).T
    z_inner = dot_across(xmod, w_in_z)
    gate_z = jax.nn.silu(z_inner)
    d_branch_all = (whole_up.astype(f32) * gate_tok).astype(bf16)
    d_gated = dot_across(d_branch_all, w_out)
    d_mixed = d_gated * gate_z
    y, d_deltas, d_act_scan, d_log, d_b_part, d_c_part = scans(
        deltas, act_low, d_mixed, a_neg, b_mat, c_mat, begins[None]
    )
    d_dt_raw = d_deltas * jax.nn.sigmoid(dt_raw)
    d_dt_low = d_dt_raw.astype(bf16)
    proj_terms = jnp.concatenate([dot_across(d_dt_low, w_dt), d_b_part, d_c_part], axis=1)
    d_proj = sum_chan(proj_terms, DPROJ_WIRE).astype(bf16)
    mixed = y + d_skip[None, :] * act
    gated = (mixed * gate_z).astype(bf16)
    branch_part = low_dot(gated, w_out).astype(bf16)
    branch = ring.scatter(branch_part)
    onehot_loc = lax.dynamic_slice_in_dim(onehot, tok_start, tok_loc, 0)
    block_out = (activations.astype(f32) + per_token(mod_full[:, 2], onehot_loc) * branch).astype(bf16)
    grad_w_out = sum_rows(dot_tokens(gated, d_branch_all), bf16)
    d_z_low = (d_gated * mixed * silu_slope(z_inner)).astype(bf16)
    grad_w_in_z = sum_rows(dot_tokens(d_z_low, xmod), bf16)
    d_act = d_mixed * d_skip[None, :] + d_act_scan + dot_across(d_proj, w_xproj)
    d_conv = d_act * silu_slope(conv_pre)
    d_x_inner = jnp.zeros_like(d_conv)
    tap_grads = []
    for tap_index in range(conv_taps):
        lag = conv_taps - 1 - tap_index
        valid = (in_seq >= lag).astype(f32)[:, None]
        masked = d_conv * valid
        tap_grads.append(jnp.sum(masked * delay_rows(x_inner, lag), axis=0))
        d_x_inner = d_x_inner + conv_weight[:, tap_index][None, :] * advance_rows(masked, lag)
    d_x_low = d_x_inner.astype(bf16)
    d_xmod_part = (low_dot(d_x_low, w_in_x) + low_dot(d_z_low, w_in_z)).astype(bf16)
    d_xmod = ring.scatter(d_xmod_part)
    grad_w_in_x = sum_rows(dot_tokens(d_x_low, xmod), bf16)
    small = jnp.concatenate(
        [
            dot_tokens(d_proj, act_low),
            dot_tokens(dt_low, d_dt_low),
            d_log * a_neg,
            jnp.stack(tap_grads),
            jnp.sum(d_conv, axis=0)[None],
            jnp.sum(d_dt_raw, axis=0)[None],
            jnp.sum(d_mixed * act, axis=0)[None],
        ],
        axis=0,
    )
    small = jnp.pad(small, ((0, -small.shape[0] % 16), (0, 0)))
    small = sum_rows(small, f32)
    counts = [w_xproj.shape[1], low_rank, states, conv_taps, 1, 1, 1]
    pieces, at = [], 0
    for count in counts:
        pieces.append(small[at : at + count])
        at += count
    share = d_xmod_part.astype(f32)
    share_normed = share * normed
    share_gate = whole_up.astype(f32) * branch_part.astype(f32)
    seq_sum = lambda v: jnp.stack([jnp.sum(onehot[:, s : s + 1] * v, axis=0) for s in range(seq_count)])
    sums = jnp.stack([seq_sum(share), seq_sum(share_normed), seq_sum(share_gate)], axis=1)
    sums = small_scatter(sums.reshape(seq_count, 3, parts, part_width).transpose(2, 0, 1, 3))
    gain_term = jnp.sum(sums[:, 1] * (1.0 + modulation[:, 1]), axis=0)
    d_mod = jnp.stack([sums[:, 0], sums[:, 1] * norm_gain[None], sums[:, 2]], axis=1)
    reach = jnp.concatenate([d_mod.reshape(3 * seq_count, part_width), gain_term[None]], axis=0)
    reach = small_gather(reach, "rows")
    grad_gain = jnp.sum(reach[:, 3 * seq_count], axis=0)
    d_mod_all = reach[:, : 3 * seq_count].reshape(-1, 3, part_width)
    grad_b_ada = jnp.sum(d_mod_all, axis=0)
    grad_w_ada = jnp.einsum(
        "skj,si->kji",
        d_mod_all,
        cond_all.astype(f32),
        precision=HIGHEST,
        preferred_element_type=f32,
    )
    wide_loc = activations.astype(f32)
    centred_loc = wide_loc - jnp.mean(wide_loc, axis=1, keepdims=True)
    inv_std_loc = lax.rsqrt(jnp.mean(centred_loc * centred_loc, axis=1, keepdims=True) + EPSILON)
    normed_loc = centred_loc * inv_std_loc
    scale_loc = per_token(mod_full[:, 1], onehot_loc)
    d_normed = d_xmod * (1.0 + scale_loc) * gain_full[None, :]
    mean_first = jnp.mean(d_normed, axis=1, keepdims=True)
    mean_second = jnp.mean(d_normed * normed_loc, axis=1, keepdims=True)
    grad_input = (
        inv_std_loc * (d_normed - mean_first - normed_loc * mean_second) + grad_out.astype(f32)
    ).astype(bf16)
    return (
        block_out,
        grad_input,
        grad_w_ada,
        grad_b_ada,
        grad_gain,
        grad_w_in_x,
        grad_w_in_z,
        pieces[3].T,
        pieces[4][0],
        pieces[0].T,
        pieces[1],
        pieces[5][0],
        pieces[2].T,
        pieces[6][0],
        grad_w_out,
    )


PROJ_WIRE = bf16
DPROJ_WIRE = bf16


def solution(mesh):
    return jax.shard_map(
        local,
        mesh=mesh,
        in_specs=(
            P(("rows", "chan"), None),
            P("rows", None),
            P("rows", None),
            P(None, "chan", None),
            P(None, "chan"),
            P("chan"),
            P("chan", None),
            P("chan", None),
            P("chan", None),
            P("chan"),
            P("chan", None),
            P(None, "chan"),
            P("chan"),
            P("chan", None),
            P("chan"),
            P("chan", None),
            P(("rows", "chan"), None),
        ),
        out_specs=(
            P(("rows", "chan"), None),
            P(("rows", "chan"), None),
            P(None, "chan", None),
            P(None, "chan"),
            P("chan"),
            P("chan", None),
            P("chan", None),
            P("chan", None),
            P("chan"),
            P("chan", None),
            P(None, "chan"),
            P("chan"),
            P("chan", None),
            P("chan"),
            P("chan", None),
        ),
        check_vma=False,
    )
```

```python
import functools
import math

import jax
import jax.numpy as jnp
from jax import lax
from jax.experimental import pallas as pl
from jax.experimental.pallas import tpu as pltpu
from jax.sharding import PartitionSpec as P

CHUNK = 16
LANES = 128
LOG2E = math.log2(math.e)
f32 = jnp.float32
bf16 = jnp.bfloat16


def scan_kernel(
    n_seq,
    states,
    begins_ref,
    proj_ref,
    act_ref,
    z_ref,
    d_gated_ref,
    w_dt_ref,
    dt_bias_ref,
    an_ref,
    skip_ref,
    gated_ref,
    d_z_ref,
    d_dt_ref,
    d_act_ref,
    ga_ref,
    sums_ref,
    terms_ref,
    b_all,
    c_all,
    pf_all,
    db_all,
    b_blk_all,
    c_blk_all,
    delta_all,
    step_all,
    dm_all,
    exp_all,
):
    tokens, channels = act_ref.shape
    n_pairs = tokens // (2 * CHUNK)
    wide = CHUNK * states
    low_rank = proj_ref.shape[1] - 2 * states
    an = an_ref[...]
    a2 = an * LOG2E
    dot = functools.partial(jnp.dot, preferred_element_type=f32)
    across = functools.partial(
        lax.dot_general, dimension_numbers=(((1,), (1,)), ((), ())), preferred_element_type=f32
    )

    def diagonal(rows):
        r = lax.broadcasted_iota(jnp.int32, (rows, wide), 0) % CHUNK
        return (r == lax.broadcasted_iota(jnp.int32, (rows, wide), 1) // states).astype(f32)

    diag = diagonal(CHUNK)
    ones_blk = diag.astype(bf16)
    m = lax.broadcasted_iota(jnp.int32, (low_rank + 2 * states, wide), 0)
    q = lax.broadcasted_iota(jnp.int32, (low_rank + 2 * states, wide), 1) % states
    pick_b = (m == low_rank + q).astype(bf16)
    pick_c = (m == low_rank + states + q).astype(bf16)
    tile = pl.program_id(0)

    @pl.when(tile == 0)
    def _():
        many = diagonal(LANES)

        def spread(k, carry):
            base = pl.multiple_of(k * LANES, LANES)
            proj = proj_ref[pl.ds(base, LANES), :]
            low = proj.astype(bf16)
            b_blk_all[pl.ds(base, LANES), :] = (dot(low, pick_b) * many).astype(bf16)
            c_blk_all[pl.ds(base, LANES), :] = (dot(low, pick_c) * many).astype(bf16)
            turned = proj.astype(f32).T
            bt = turned[low_rank : low_rank + states]
            ct = turned[low_rank + states :]
            for i in range(LANES):
                at = pl.ds(pl.multiple_of(base * states + i * states, states), states)
                b_all[at, :] = jnp.broadcast_to(bt[:, i : i + 1], (states, channels))
                c_all[at, :] = jnp.broadcast_to(ct[:, i : i + 1], (states, channels))
            return carry

        lax.fori_loop(0, tokens // LANES, spread, 0)

    def prepare(k, carry):
        here = pl.ds(pl.multiple_of(k * LANES, LANES), LANES)
        dt_raw = dot(proj_ref[here, :].astype(bf16), w_dt_ref[...]) + dt_bias_ref[...]
        delta = jnp.maximum(dt_raw, 0.0) + jnp.log1p(jnp.exp(-jnp.abs(dt_raw)))
        delta_all[here, :] = delta
        step_all[here, :] = delta * act_ref[here, :].astype(f32)
        z = z_ref[here, :]
        dm_all[here, :] = d_gated_ref[here, :] * (z * jax.nn.sigmoid(z))
        return carry

    lax.fori_loop(0, tokens // LANES, prepare, 0)

    def keep_at(t):
        keep = None
        for s in range(1, n_seq):
            k = jnp.where(begins_ref[0, s] == t, 0.0, 1.0).astype(f32)
            keep = k if keep is None else keep * k
        return keep

    def sweep(body, cut, carry):
        plain, masked = functools.partial(body, False), functools.partial(body, True)
        if n_seq == 1:
            return lax.fori_loop(0, n_pairs, plain, carry)
        if n_seq > 2:
            return lax.fori_loop(0, n_pairs, masked, carry)
        carry = lax.fori_loop(0, cut, plain, carry)
        carry = masked(cut, carry)
        return lax.fori_loop(cut + 1, n_pairs, plain, carry)

    def row(ref, t):
        return ref[pl.ds(t, 1), :]

    def forward(masked, pair, carry):
        sf, g = carry
        base = pl.multiple_of(pair * 2 * CHUNK, 2 * CHUNK)
        for i in range(2 * CHUNK):
            at = pl.ds(pl.multiple_of(base * states + i * states, states), states)
            decay = jnp.exp2(row(delta_all, base + i) * a2)
            if masked:
                keep = keep_at(base + i)
                sf = sf * keep
                g = g * keep
            pf = decay * sf
            sf = pf + row(step_all, base + i) * b_all[at, :]
            db = row(dm_all, base + i) * c_all[at, :] + g
            g = decay * db
            pf_all[at, :] = pf
            db_all[at, :] = db
        return sf, g

    zero = jnp.zeros((states, channels), f32)
    first = begins_ref[0, n_seq - 1]
    sweep(forward, first // (2 * CHUNK), (zero, zero))

    def backward(masked, k, carry):
        sb, g, ga = carry
        base = pl.multiple_of((n_pairs - 1 - k) * 2 * CHUNK, 2 * CHUNK)
        for i in range(2 * CHUNK - 1, -1, -1):
            at = pl.ds(pl.multiple_of(base * states + i * states, states), states)
            delta = row(delta_all, base + i)
            decay = jnp.exp2(delta * a2)
            drive = row(step_all, base + i) * b_all[at, :]
            if masked:
                keep = keep_at(base + i + 1)
                sb = sb * keep
                g = g * keep
            pb = decay * sb
            sb = pb + drive
            df = row(dm_all, base + i) * c_all[at, :] + g
            g = decay * df
            pf = pf_all[at, :]
            db = db_all[at, :]
            d_expo = df * pf + db * pb
            ga = ga + d_expo * delta
            pf_all[at, :] = pf + drive + sb
            db_all[at, :] = df + db
            exp_all[at, :] = (d_expo * an).astype(bf16)
        return sb, g, ga

    cut = n_pairs - 1 - (first - 1) // (2 * CHUNK)
    _, _, ga = sweep(backward, cut, (zero, zero, zero))
    ga_ref[...] = ga

    def finish(k, carry):
        by_bias, by_skip = carry
        base = pl.multiple_of(k * LANES, LANES)
        here = pl.ds(base, LANES)
        low = proj_ref[here, :].astype(bf16)
        act = act_ref[here, :].astype(f32)
        d_mixed = dm_all[here, :]
        dm_low = d_mixed.astype(bf16)
        step_low = step_all[here, :].astype(bf16)
        y, through, expo, dcm, dbm = [], [], [], [], []
        for c in range(LANES // CHUNK):
            at = pl.ds(pl.multiple_of(base * states + c * wide, wide), wide)
            mine = pl.ds(pl.multiple_of(base + c * CHUNK, CHUNK), CHUNK)
            span = slice(c * CHUNK, (c + 1) * CHUNK)
            both = pf_all[at, :].astype(bf16)
            drv = db_all[at, :].astype(bf16)
            y.append(dot(c_blk_all[mine, :], both))
            through.append(dot(b_blk_all[mine, :], drv))
            expo.append(dot(ones_blk, exp_all[at, :]))
            dcm.append((across(dm_low[span], both) * diag).astype(bf16))
            dbm.append((across(step_low[span], drv) * diag).astype(bf16))
        whole = lambda parts: jnp.concatenate(parts, axis=0)
        skip = skip_ref[...]
        z = z_ref[here, :]
        sigma = jax.nn.sigmoid(z)
        mixed = whole(y) + skip * act
        gated_ref[here, :] = (mixed * (z * sigma)).astype(bf16)
        d_z_ref[here, :] = (d_gated_ref[here, :] * mixed * (sigma * (1.0 + z * (1.0 - sigma)))).astype(bf16)
        via = whole(through)
        d_act_ref[here, :] = d_mixed * skip + via * delta_all[here, :]
        dt_raw = dot(low, w_dt_ref[...]) + dt_bias_ref[...]
        d_dt_raw = (whole(expo) + via * act) * jax.nn.sigmoid(dt_raw)
        d_dt = d_dt_raw.astype(bf16)
        d_dt_ref[here, :] = d_dt
        terms = across(d_dt, w_dt_ref[...]) + across(whole(dbm), pick_b) + across(whole(dcm), pick_c)

        @pl.when(tile == 0)
        def _():
            terms_ref[here, :] = terms

        @pl.when(tile != 0)
        def _():
            terms_ref[here, :] += terms

        total = lambda v: jnp.sum(v, axis=0, keepdims=True)
        return by_bias + total(d_dt_raw), by_skip + total(d_mixed * act)

    none = jnp.zeros((1, channels), f32)
    by_bias, by_skip = lax.fori_loop(0, tokens // LANES, finish, (none, none))
    sums_ref[0:8, :] = jnp.broadcast_to(by_bias, (8, channels))
    sums_ref[8:16, :] = jnp.broadcast_to(by_skip, (8, channels))


def scans(proj, act_low, z_inner, d_gated, w_dt, dt_bias, a_neg, d_skip, begins):
    tokens, channels = act_low.shape
    states = a_neg.shape[0]
    tile = LANES if channels % LANES == 0 else channels
    wide = CHUNK * states
    w_dt = jnp.pad(w_dt, ((0, 2 * states), (0, 0)))
    col = lambda: pl.BlockSpec((tokens, tile), lambda j: (0, j))
    rows = lambda n: pl.BlockSpec((n, tile), lambda j: (0, j))
    full = lambda: pl.BlockSpec(proj.shape, lambda j: (0, 0))
    sds = jax.ShapeDtypeStruct
    return pl.pallas_call(
        functools.partial(scan_kernel, begins.shape[1], states),
        grid=(channels // tile,),
        in_specs=[
            pl.BlockSpec(memory_space=pltpu.SMEM),
            full(),
            col(),
            col(),
            col(),
            rows(w_dt.shape[0]),
            rows(1),
            rows(states),
            rows(1),
        ],
        out_specs=[col(), col(), col(), col(), rows(states), rows(16), full()],
        out_shape=[
            sds((tokens, channels), bf16),
            sds((tokens, channels), bf16),
            sds((tokens, channels), bf16),
            sds((tokens, channels), f32),
            sds((states, channels), f32),
            sds((16, channels), f32),
            sds(proj.shape, f32),
        ],
        scratch_shapes=[pltpu.VMEM((tokens * states, tile), f32)] * 4
        + [pltpu.VMEM((tokens, wide), bf16)] * 2
        + [pltpu.VMEM((tokens, tile), f32)] * 3
        + [pltpu.VMEM((tokens * states, tile), bf16)],
        compiler_params=pltpu.CompilerParams(vmem_limit_bytes=62 * 2**20, dimension_semantics=("arbitrary",)),
        cost_estimate=pl.CostEstimate(
            flops=tokens * channels * states * 60,
            bytes_accessed=tokens * channels * 24,
            transcendentals=2 * tokens * channels * states,
        ),
        name="scan_all",
    )(begins, proj, act_low, z_inner, d_gated, w_dt, dt_bias[None], a_neg, d_skip[None])


EPSILON = 1e-06
HIGHEST = lax.Precision.HIGHEST


def low_dot(left, right):
    return jnp.dot(left, right, preferred_element_type=f32)


def dot_across(left, right):
    return lax.dot_general(left, right, (((1,), (1,)), ((), ())), preferred_element_type=f32)


def dot_tokens(left, right):
    return lax.dot_general(left, right, (((0,), (0,)), ((), ())), preferred_element_type=f32)


def delay_rows(operand, lag):
    if lag == 0:
        return operand
    padding = jnp.zeros((lag,) + operand.shape[1:], operand.dtype)
    return jnp.concatenate([padding, operand[:-lag]], axis=0)


def advance_rows(operand, lag):
    if lag == 0:
        return operand
    padding = jnp.zeros((lag,) + operand.shape[1:], operand.dtype)
    return jnp.concatenate([operand[lag:], padding], axis=0)


def after(x, *others):
    return lax.optimization_barrier((x,) + others)[0]


def silu_slope(operand):
    squash = jax.nn.sigmoid(operand)
    return squash * (1.0 + operand * (1.0 - squash))


class Ring:
    def __init__(self):
        self.n = lax.axis_size("chan")
        self.down = 4 if self.n % 8 == 0 else 1
        self.across = self.n // self.down
        order = [self.at(p) for p in range(self.n)]
        self.right = [(order[k], order[(k + 1) % self.n]) for k in range(self.n)]
        self.left = [(b, a) for a, b in self.right]
        index = lax.axis_index("chan")
        i, j = index // self.across, index % self.across
        back = self.down - 1 - i
        step = jnp.where(back % 2 == 0, j - 1, self.across - 1 - j)
        self.place = jnp.where(j == 0, i, self.down + back * (self.across - 1) + step)

    def at(self, p):
        if self.down == 1:
            return p
        back, step = (p - self.down) // (self.across - 1), (p - self.down) % (self.across - 1)
        if isinstance(p, int):
            column = 1 + step if back % 2 == 0 else self.across - 1 - step
            return p * self.across if p < self.down else (self.down - 1 - back) * self.across + column
        column = jnp.where(back % 2 == 0, 1 + step, self.across - 1 - step)
        return jnp.where(p < self.down, p * self.across, (self.down - 1 - back) * self.across + column)

    def owner(self, away):
        p = self.place + away
        if away > 0:
            p = jnp.where(p >= self.n, p - self.n, p)
        elif away < 0:
            p = jnp.where(p < 0, p + self.n, p)
        return self.at(p)

    def go_right(self, x):
        return lax.ppermute(x, "chan", self.right)

    def go_left(self, x):
        return lax.ppermute(x, "chan", self.left)

    def blocks(self, x):
        half = self.n // 2
        cut = x.shape[0] // 2
        from_left, from_right = x, x
        found = [(self.owner(0), x)]
        for step in range(1, half):
            from_left, from_right = self.go_right(from_left), self.go_left(from_right)
            found += [(self.owner(-step), from_left), (self.owner(step), from_right)]
        far = jnp.concatenate([self.go_right(from_left[:cut]), self.go_left(from_right[cut:])], axis=0)
        return found + [(self.owner(half), far)]

    def whole(self, blocks, *others):
        rows = blocks[0][1].shape[0]
        whole = jnp.zeros((self.n * rows,) + blocks[0][1].shape[1:], blocks[0][1].dtype)
        if others:
            whole = after(whole, *others)
        for owner, block in blocks:
            whole = lax.dynamic_update_slice_in_dim(whole, block, owner * rows, 0)
        return whole

    def scatter(self, part, stages=None):
        half = self.n // 2
        rows = part.shape[0] // self.n
        cut = rows // 2
        mine = lambda away: lax.dynamic_slice_in_dim(part, self.owner(away) * rows, rows, 0)
        wide = lambda v: v.astype(f32)
        far = mine(half)
        right, left = self.go_right(far[:cut]), self.go_left(far[cut:])
        sent, arrived = [(far,)], [(right, left)]
        for away in range(half - 1, 0, -1):
            ahead, behind = wide(mine(away)), wide(mine(-away))
            if away == half - 1:
                ahead = jnp.concatenate([ahead[:cut] + wide(right), ahead[cut:]], axis=0)
                behind = jnp.concatenate([behind[:cut], behind[cut:] + wide(left)], axis=0)
            else:
                ahead, behind = ahead + wide(right), behind + wide(left)
            ahead, behind = ahead.astype(bf16), behind.astype(bf16)
            held = (stages or {}).get(half - away)
            if held:
                ahead, behind = lax.optimization_barrier((ahead, behind) + tuple(held))[:2]
            sent.append((ahead, behind))
            right, left = self.go_right(ahead), self.go_left(behind)
            arrived.append((right, left))
        return wide(mine(0)) + wide(right) + wide(left), arrived, sent


def is_power(n):
    return n & (n - 1) == 0


def bits_of(n):
    return [1 << b for b in range(n.bit_length() - 1)]


def sum_chan(x, wire, stages=None):
    n = lax.axis_size("chan")
    index = lax.axis_index("chan")
    if not is_power(n) or x.shape[0] % (16 * n):
        x = lax.psum(x, "chan")
        return x, [x] * 8
    perm = lambda b: [(i, i ^ b) for i in range(n)]
    arrived = []

    def exchange(send, b):
        held = (stages or {}).get(len(arrived))
        if held:
            send = after(send, *held)
        arrived.append(lax.ppermute(send, "chan", perm(b)))
        return arrived[-1]

    for b in bits_of(n):
        h = x.shape[0] // 2
        upper = (index // b) % 2
        keep = lax.dynamic_slice_in_dim(x, upper * h, h, 0)
        send = lax.dynamic_slice_in_dim(x, (1 - upper) * h, h, 0)
        x = keep + exchange(send.astype(wire), b).astype(f32)
    x = x.astype(wire)
    for b in reversed(bits_of(n)):
        upper = (index // b) % 2
        other = exchange(x, b)
        x = jnp.concatenate([jnp.where(upper == 0, x, other), jnp.where(upper == 0, other, x)], axis=0)
    return x, arrived


def small_gather(x, axis, stages=()):
    n = lax.axis_size(axis)
    if not is_power(n) or n > 8:
        return lax.all_gather(x, axis, axis=0)
    index = lax.axis_index(axis)
    x = x[None]
    for level, b in enumerate(bits_of(n)):
        if level < len(stages):
            x = after(x, *stages[level])
        other = lax.ppermute(x, axis, [(i, i ^ b) for i in range(n)])
        lower = (index // b) % 2 == 0
        x = jnp.concatenate([jnp.where(lower, x, other), jnp.where(lower, other, x)], axis=0)
    return x


def small_sum(x, stages):
    n = lax.axis_size("chan")
    if not is_power(n) or n > 8:
        return lax.psum(x, "chan")
    for level, b in enumerate(bits_of(n)):
        other = lax.ppermute(x, "chan", [(i, i ^ b) for i in range(n)])
        x, other = lax.optimization_barrier((x, other) + tuple(stages[level]))[:2]
        x = x + other
    return x


def sum_rows(x, wire, stages=((), ())):
    n = lax.axis_size("rows")
    if n != 4:
        return lax.psum(x, "rows")
    other = lax.ppermute(x, "rows", [(0, 1), (1, 0), (2, 3), (3, 2)])
    x, other = lax.optimization_barrier((x, other) + tuple(stages[0]))[:2]
    pair = (x + other).astype(wire)
    other = lax.ppermute(pair, "rows", [(0, 2), (2, 0), (1, 3), (3, 1)])
    pair, other = lax.optimization_barrier((pair, other) + tuple(stages[1]))[:2]
    return pair.astype(f32) + other.astype(f32)


def place_norm_kernel(n_seq, count, owners_ref, begins_ref, mod_ref, *refs):
    blocks, (xmod_ref, normed_ref, held) = refs[:count], refs[count:]
    rows, width = xmod_ref.shape
    step = 2 * CHUNK if rows % (2 * CHUNK) == 0 else rows
    k = pl.program_id(0)
    base = owners_ref[k] * rows

    def hold(block_ref):
        held[...] = block_ref[...]

    for i in range(count):
        pl.when(k == i)(functools.partial(hold, blocks[i]))
    shift, scale = mod_ref[0:1, :], mod_ref[1:2, :]
    gain = mod_ref[3 * n_seq : 3 * n_seq + 1, :]
    for start in range(0, rows, step):
        here = slice(start, start + step)
        wide = held[here, :].astype(f32)
        centred = wide - jnp.sum(wide, axis=1, keepdims=True) * (1.0 / width)
        square = jnp.sum(centred * centred, axis=1, keepdims=True) * (1.0 / width)
        normed = centred * lax.rsqrt(square + EPSILON)
        token = base + start + lax.broadcasted_iota(jnp.int32, (step, 1), 0)
        add, by = shift, gain * (1.0 + scale)
        for s in range(1, n_seq):
            later = token >= begins_ref[0, s]
            add = jnp.where(later, mod_ref[3 * s : 3 * s + 1, :], add)
            by = jnp.where(later, gain * (1.0 + mod_ref[3 * s + 1 : 3 * s + 2, :]), by)
        xmod_ref[here, :] = (normed * by + add).astype(bf16)
        normed_ref[here, :] = normed.astype(bf16)


def place_gate_kernel(n_seq, count, owners_ref, begins_ref, mod_ref, *refs):
    blocks, (gated_ref, plain_ref) = refs[:count], refs[count:]
    rows = gated_ref.shape[0]
    step = CHUNK if rows % CHUNK == 0 else rows
    k = pl.program_id(0)
    base = owners_ref[k] * rows

    def fill(block_ref):
        def part(p, carry):
            here = pl.ds(pl.multiple_of(p * step, step), step)
            low = block_ref[here, :]
            token = base + p * step + lax.broadcasted_iota(jnp.int32, (step, 1), 0)
            gate = mod_ref[2:3, :]
            for s in range(1, n_seq):
                gate = jnp.where(token >= begins_ref[0, s], mod_ref[3 * s + 2 : 3 * s + 3, :], gate)
            gated_ref[here, :] = (low.astype(f32) * gate).astype(bf16)
            plain_ref[here, :] = low
            return carry

        lax.fori_loop(0, rows // step, part, 0)

    for i in range(count):
        pl.when(k == i)(functools.partial(fill, blocks[i]))


def place(kernel, blocks, begins, mod, name, scratch=False):
    owners = jnp.stack([owner for owner, _ in blocks]).astype(jnp.int32)
    parts = [block for _, block in blocks]
    rows, width = parts[0].shape
    count = len(parts)
    whole = jax.ShapeDtypeStruct((count * rows, width), bf16)
    out = lambda: pl.BlockSpec((rows, width), lambda k, owners_ref, begins_ref: (owners_ref[k], 0))
    fixed = lambda shape: pl.BlockSpec(shape, lambda k, owners_ref, begins_ref: (0, 0))
    return pl.pallas_call(
        functools.partial(kernel, begins.shape[1], count),
        grid_spec=pltpu.PrefetchScalarGridSpec(
            num_scalar_prefetch=2,
            grid=(count,),
            in_specs=[fixed(mod.shape)] + [fixed((rows, width))] * count,
            out_specs=[out(), out()],
            scratch_shapes=[pltpu.VMEM((rows, width), bf16)] if scratch else [],
        ),
        out_shape=[whole, whole],
        compiler_params=pltpu.CompilerParams(vmem_limit_bytes=28 * 2**20, dimension_semantics=("arbitrary",)),
        cost_estimate=pl.CostEstimate(
            flops=count * rows * width * 20, bytes_accessed=count * rows * width * 6, transcendentals=0
        ),
        name=name,
    )(owners, begins, mod, *parts)


def sums_kernel(n_seq, begins_ref, share_ref, normed_ref, up_ref, branch_ref, out_ref):
    rows, width = share_ref.shape
    k = pl.program_id(0)

    @pl.when(k == 0)
    def _():
        out_ref[...] = jnp.zeros(out_ref.shape, f32)

    lanes = 2 * LANES if width % (2 * LANES) == 0 else width
    token = k * rows + lax.broadcasted_iota(jnp.int32, (rows, 1), 0)
    for at in range(0, width, lanes):
        cols = slice(at, at + lanes)
        share = share_ref[:, cols].astype(f32)
        terms = [share, share * normed_ref[:, cols].astype(f32)]
        terms.append(up_ref[:, cols].astype(f32) * branch_ref[:, cols].astype(f32))
        for j, term in enumerate(terms):
            rest = jnp.sum(term, axis=0, keepdims=True)
            for s in range(n_seq - 1, 0, -1):
                later = jnp.sum(jnp.where(token >= begins_ref[0, s], term, 0.0), axis=0, keepdims=True)
                at_row = j * n_seq + s
                mine = later if s == n_seq - 1 else later - after_it
                out_ref[at_row : at_row + 1, cols] += mine
                after_it = later
            out_ref[j * n_seq : j * n_seq + 1, cols] += rest - (after_it if n_seq > 1 else 0.0)


def token_sums(share, normed, up, branch, begins):
    tokens, width = share.shape
    n_seq = begins.shape[1]
    rows = LANES
    spec = lambda: pl.BlockSpec((rows, width), lambda k: (k, 0))
    height = 3 * n_seq + (-3 * n_seq % 8)
    return pl.pallas_call(
        functools.partial(sums_kernel, n_seq),
        grid=(tokens // rows,),
        in_specs=[pl.BlockSpec(memory_space=pltpu.SMEM), spec(), spec(), spec(), spec()],
        out_specs=pl.BlockSpec((height, width), lambda k: (0, 0)),
        out_shape=jax.ShapeDtypeStruct((height, width), f32),
        compiler_params=pltpu.CompilerParams(vmem_limit_bytes=32 * 2**20, dimension_semantics=("arbitrary",)),
        cost_estimate=pl.CostEstimate(flops=tokens * width * 12, bytes_accessed=tokens * width * 8, transcendentals=0),
        name="token_sums",
    )(begins, share, normed, up, branch)


def local(
    activations,
    condition,
    seq_lengths,
    w_ada,
    b_ada,
    norm_gain,
    w_in_x,
    w_in_z,
    conv_weight,
    conv_bias,
    w_xproj,
    w_dt,
    dt_bias,
    a_log,
    d_skip,
    w_out,
    grad_out,
):
    ring = Ring()
    tok_loc, width = activations.shape
    low_rank = w_dt.shape[0]
    states = a_log.shape[1]
    channels = a_log.shape[0]
    conv_taps = conv_weight.shape[1]
    tok_count = tok_loc * ring.n
    tok_start = lax.axis_index("chan") * tok_loc
    act_blocks = ring.blocks(activations)
    act_in = [b for _, b in act_blocks[1:]]
    cond_act = jax.nn.silu(condition.astype(f32)).astype(bf16)
    modulation = (
        jnp.einsum("si,kji->skj", cond_act, w_ada, preferred_element_type=f32) + b_ada[None]
    )
    part_width = norm_gain.shape[0]
    seq_count = seq_lengths.shape[1]
    packed = jnp.concatenate([modulation.reshape(3 * seq_count, part_width), norm_gain[None]], axis=0)
    packed = small_gather(packed, "chan", [(), act_in[0:2], act_in[2:4]])
    seq_lengths, conv_weight, conv_bias, w_dt, dt_bias, a_log, d_skip = lax.optimization_barrier(
        (seq_lengths, conv_weight, conv_bias, w_dt, dt_bias, a_log, d_skip, act_in[2], act_in[3])
    )[:7]
    seq_lens = seq_lengths[0]
    seq_ends = jnp.cumsum(seq_lens)
    begins = seq_ends - seq_lens
    position = jnp.arange(tok_count, dtype=jnp.int32)
    member = (position[:, None] >= begins[None, :]) & (position[:, None] < seq_ends[None, :])
    onehot = member.astype(f32)
    in_seq = jnp.sum(onehot * (position[:, None] - begins[None, :]).astype(f32), axis=1)
    per_token = lambda rows, hot: sum(hot[:, s : s + 1] * rows[s][None] for s in range(seq_count))
    packed = packed.transpose(1, 0, 2).reshape(3 * seq_count + 1, width)
    packed = jnp.pad(packed, ((0, -packed.shape[0] % 8), (0, 0)))
    mod_full = packed[: 3 * seq_count].reshape(seq_count, 3, width)
    gain_full = packed[3 * seq_count]
    a_neg = -jnp.exp(a_log).T
    up_blocks = ring.blocks(after(grad_out, act_in[-1]))
    up_in = [b for _, b in up_blocks[1:]]
    xmod, normed = place(place_norm_kernel, act_blocks, begins[None], packed, "place_norm", True)
    x_inner = dot_across(after(xmod, *up_in[0:2]), w_in_x)
    conv_pre = jnp.zeros_like(x_inner) + conv_bias[None, :]
    for tap_index in range(conv_taps):
        lag = conv_taps - 1 - tap_index
        valid = (in_seq >= lag).astype(f32)[:, None]
        conv_pre = conv_pre + conv_weight[:, tap_index][None, :] * delay_rows(x_inner, lag) * valid
    act_low = jax.nn.silu(conv_pre).astype(bf16)
    proj, proj_in = sum_chan(low_dot(act_low, w_xproj), PROJ_WIRE, {1: up_in[2:4], 3: up_in[4:6]})
    dt_low = proj[:, :low_rank].astype(bf16)
    z_inner = dot_across(after(xmod, act_low), w_in_z)
    d_branch_all, whole_up = place(place_gate_kernel, up_blocks, begins[None], packed, "place_gate")
    d_gated = dot_across(d_branch_all, w_out)
    gated, d_z_low, d_dt_low, d_act, d_log, bias_skip, proj_terms = scans(
        proj, act_low, z_inner, d_gated, w_dt, dt_bias, a_neg, d_skip, begins[None]
    )
    branch_part = lax.optimization_barrier(low_dot(gated, w_out).astype(bf16))
    branch, branch_in, branch_out = ring.scatter(branch_part)
    d_proj, d_proj_in = sum_chan(proj_terms, DPROJ_WIRE, {2: branch_in[0], 5: branch_in[1]})
    d_proj = d_proj.astype(bf16)
    onehot_loc = lax.dynamic_slice_in_dim(onehot, tok_start, tok_loc, 0)
    block_out = (activations.astype(f32) + per_token(mod_full[:, 2], onehot_loc) * branch).astype(bf16)
    gated, d_z_grad = lax.optimization_barrier((gated, d_z_low) + branch_out[0])[:2]
    grad_w_out = sum_rows(dot_tokens(gated, d_branch_all), bf16, (d_proj_in[1:2], branch_in[-1]))
    grad_w_in_z = sum_rows(dot_tokens(d_z_grad, xmod), bf16, (d_proj_in[2:3], branch_in[-1]))
    d_act = d_act + dot_across(d_proj, w_xproj)
    d_conv = d_act * silu_slope(conv_pre)
    d_x_inner = jnp.zeros_like(d_conv)
    tap_grads = []
    for tap_index in range(conv_taps):
        lag = conv_taps - 1 - tap_index
        valid = (in_seq >= lag).astype(f32)[:, None]
        masked = d_conv * valid
        tap_grads.append(jnp.sum(masked * delay_rows(x_inner, lag), axis=0))
        d_x_inner = d_x_inner + conv_weight[:, tap_index][None, :] * advance_rows(masked, lag)
    d_x_low = d_x_inner.astype(bf16)
    d_xmod_part = (low_dot(d_x_low, w_in_x) + low_dot(d_z_low, w_in_z)).astype(bf16)
    d_xmod_part = after(d_xmod_part, *branch_in[-1])
    d_xmod, d_xmod_in, d_xmod_out = ring.scatter(d_xmod_part, {2: (grad_w_out, grad_w_in_z), 3: (block_out,)})
    ins = (d_xmod_in + [d_xmod_in[-1]] * 4)[:4]
    outs = (d_xmod_out + [d_xmod_out[-1]] * 4)[:4]
    d_x_grad = after(d_x_low, *outs[0])
    d_proj, d_xmod_share = lax.optimization_barrier((d_proj, d_xmod_part) + outs[1])[:2]
    grad_w_in_x = sum_rows(dot_tokens(d_x_grad, xmod), bf16, (ins[0], ins[2]))
    small = jnp.concatenate(
        [
            dot_tokens(d_proj, act_low),
            dot_tokens(dt_low, d_dt_low),
            d_log * a_neg,
            jnp.stack(tap_grads),
            jnp.sum(d_conv, axis=0)[None],
            bias_skip[0:1],
            bias_skip[8:9],
        ],
        axis=0,
    )
    small = jnp.pad(small, ((0, -small.shape[0] % 16), (0, 0)))
    small = sum_rows(small, f32, (ins[1], ins[2]))
    counts = [w_xproj.shape[1], low_rank, states, conv_taps, 1, 1, 1]
    pieces, at = [], 0
    for count in counts:
        pieces.append(small[at : at + count])
        at += count
    sums = token_sums(d_xmod_share, normed, whole_up, branch_part, begins[None])
    sums = small_sum(sums, (ins[1], ins[2], ins[3]))
    sums = lax.dynamic_slice_in_dim(sums, lax.axis_index("chan") * part_width, part_width, 1)
    by_shift, by_scale, by_gate = [sums[k * seq_count : (k + 1) * seq_count] for k in range(3)]
    gain_term = jnp.sum(by_scale * (1.0 + modulation[:, 1]), axis=0)
    d_mod = jnp.stack([by_shift, by_scale * norm_gain[None], by_gate], axis=1)
    reach = jnp.concatenate([d_mod.reshape(3 * seq_count, part_width), gain_term[None]], axis=0)
    reach = small_gather(reach, "rows")
    cond_all = small_gather(after(cond_act, act_in[-1]), "rows").reshape(-1, width)
    grad_gain = jnp.sum(reach[:, 3 * seq_count], axis=0)
    d_mod_all = reach[:, : 3 * seq_count].reshape(-1, 3, part_width)
    grad_b_ada = jnp.sum(d_mod_all, axis=0)
    grad_w_ada = jnp.einsum(
        "skj,si->kji",
        d_mod_all,
        cond_all.astype(f32),
        precision=HIGHEST,
        preferred_element_type=f32,
    )
    wide_loc = activations.astype(f32)
    centred_loc = wide_loc - jnp.mean(wide_loc, axis=1, keepdims=True)
    inv_std_loc = lax.rsqrt(jnp.mean(centred_loc * centred_loc, axis=1, keepdims=True) + EPSILON)
    normed_loc = centred_loc * inv_std_loc
    scale_loc = per_token(mod_full[:, 1], onehot_loc)
    d_normed = d_xmod * (1.0 + scale_loc) * gain_full[None, :]
    mean_first = jnp.mean(d_normed, axis=1, keepdims=True)
    mean_second = jnp.mean(d_normed * normed_loc, axis=1, keepdims=True)
    grad_input = (
        inv_std_loc * (d_normed - mean_first - normed_loc * mean_second) + grad_out.astype(f32)
    ).astype(bf16)
    return (
        block_out,
        grad_input,
        grad_w_ada,
        grad_b_ada,
        grad_gain,
        grad_w_in_x,
        grad_w_in_z,
        pieces[3].T,
        pieces[4][0],
        pieces[0].T,
        pieces[1],
        pieces[5][0],
        pieces[2].T,
        pieces[6][0],
        grad_w_out,
    )


PROJ_WIRE = bf16
DPROJ_WIRE = bf16


def solution(mesh):
    return jax.shard_map(
        local,
        mesh=mesh,
        in_specs=(
            P(("rows", "chan"), None),
            P("rows", None),
            P("rows", None),
            P(None, "chan", None),
            P(None, "chan"),
            P("chan"),
            P("chan", None),
            P("chan", None),
            P("chan", None),
            P("chan"),
            P("chan", None),
            P(None, "chan"),
            P("chan"),
            P("chan", None),
            P("chan"),
            P("chan", None),
            P(("rows", "chan"), None),
        ),
        out_specs=(
            P(("rows", "chan"), None),
            P(("rows", "chan"), None),
            P(None, "chan", None),
            P(None, "chan"),
            P("chan"),
            P("chan", None),
            P("chan", None),
            P("chan", None),
            P("chan"),
            P("chan", None),
            P(None, "chan"),
            P("chan"),
            P("chan", None),
            P("chan"),
            P("chan", None),
        ),
        check_vma=False,
    )
```

```python
import functools
import math

import jax
import jax.numpy as jnp
from jax import lax
from jax.experimental import pallas as pl
from jax.experimental.pallas import tpu as pltpu
from jax.sharding import PartitionSpec as P

CHUNK = 16
LANES = 128
LOG2E = math.log2(math.e)
f32 = jnp.float32
bf16 = jnp.bfloat16


def scan_kernel(
    n_seq,
    states,
    begins_ref,
    proj_ref,
    act_ref,
    z_ref,
    d_gated_ref,
    w_dt_ref,
    dt_bias_ref,
    an_ref,
    skip_ref,
    gated_ref,
    d_z_ref,
    d_dt_ref,
    d_act_ref,
    ga_ref,
    sums_ref,
    terms_ref,
    b_all,
    c_all,
    pf_all,
    db_all,
    b_blk_all,
    c_blk_all,
    delta_all,
    step_all,
    dm_all,
    exp_all,
):
    tokens, channels = act_ref.shape
    n_pairs = tokens // (2 * CHUNK)
    wide = CHUNK * states
    low_rank = proj_ref.shape[1] - 2 * states
    an = an_ref[...]
    a2 = an * LOG2E
    dot = functools.partial(jnp.dot, preferred_element_type=f32)
    across = functools.partial(
        lax.dot_general, dimension_numbers=(((1,), (1,)), ((), ())), preferred_element_type=f32
    )

    def diagonal(rows):
        r = lax.broadcasted_iota(jnp.int32, (rows, wide), 0) % CHUNK
        return (r == lax.broadcasted_iota(jnp.int32, (rows, wide), 1) // states).astype(f32)

    diag = diagonal(CHUNK)
    ones_blk = diag.astype(bf16)
    m = lax.broadcasted_iota(jnp.int32, (low_rank + 2 * states, wide), 0)
    q = lax.broadcasted_iota(jnp.int32, (low_rank + 2 * states, wide), 1) % states
    pick_b = (m == low_rank + q).astype(bf16)
    pick_c = (m == low_rank + states + q).astype(bf16)
    tile = pl.program_id(0)

    @pl.when(tile == 0)
    def _():
        many = diagonal(LANES)

        def spread(k, carry):
            base = pl.multiple_of(k * LANES, LANES)
            proj = proj_ref[pl.ds(base, LANES), :]
            low = proj.astype(bf16)
            b_blk_all[pl.ds(base, LANES), :] = (dot(low, pick_b) * many).astype(bf16)
            c_blk_all[pl.ds(base, LANES), :] = (dot(low, pick_c) * many).astype(bf16)
            turned = proj.astype(f32).T
            bt = turned[low_rank : low_rank + states]
            ct = turned[low_rank + states :]
            for i in range(LANES):
                at = pl.ds(pl.multiple_of(base * states + i * states, states), states)
                b_all[at, :] = jnp.broadcast_to(bt[:, i : i + 1], (states, channels))
                c_all[at, :] = jnp.broadcast_to(ct[:, i : i + 1], (states, channels))
            return carry

        lax.fori_loop(0, tokens // LANES, spread, 0)

    def prepare(k, carry):
        here = pl.ds(pl.multiple_of(k * LANES, LANES), LANES)
        dt_raw = dot(proj_ref[here, :].astype(bf16), w_dt_ref[...]) + dt_bias_ref[...]
        delta = jnp.maximum(dt_raw, 0.0) + jnp.log1p(jnp.exp(-jnp.abs(dt_raw)))
        delta_all[here, :] = delta
        step_all[here, :] = delta * act_ref[here, :].astype(f32)
        z = z_ref[here, :]
        dm_all[here, :] = d_gated_ref[here, :] * (z * jax.nn.sigmoid(z))
        return carry

    lax.fori_loop(0, tokens // LANES, prepare, 0)

    def keep_at(t):
        keep = None
        for s in range(1, n_seq):
            k = jnp.where(begins_ref[0, s] == t, 0.0, 1.0).astype(f32)
            keep = k if keep is None else keep * k
        return keep

    def sweep(body, cut, carry):
        plain, masked = functools.partial(body, False), functools.partial(body, True)
        if n_seq == 1:
            return lax.fori_loop(0, n_pairs, plain, carry)
        if n_seq > 2:
            return lax.fori_loop(0, n_pairs, masked, carry)
        carry = lax.fori_loop(0, cut, plain, carry)
        carry = masked(cut, carry)
        return lax.fori_loop(cut + 1, n_pairs, plain, carry)

    def row(ref, t):
        return ref[pl.ds(t, 1), :]

    def forward(masked, pair, carry):
        sf, g = carry
        base = pl.multiple_of(pair * 2 * CHUNK, 2 * CHUNK)
        for i in range(2 * CHUNK):
            at = pl.ds(pl.multiple_of(base * states + i * states, states), states)
            decay = jnp.exp2(row(delta_all, base + i) * a2)
            if masked:
                keep = keep_at(base + i)
                sf = sf * keep
                g = g * keep
            pf = decay * sf
            sf = pf + row(step_all, base + i) * b_all[at, :]
            db = row(dm_all, base + i) * c_all[at, :] + g
            g = decay * db
            pf_all[at, :] = pf
            db_all[at, :] = db
        return sf, g

    zero = jnp.zeros((states, channels), f32)
    first = begins_ref[0, n_seq - 1]
    sweep(forward, first // (2 * CHUNK), (zero, zero))

    def backward(masked, k, carry):
        sb, g, ga = carry
        base = pl.multiple_of((n_pairs - 1 - k) * 2 * CHUNK, 2 * CHUNK)
        for i in range(2 * CHUNK - 1, -1, -1):
            at = pl.ds(pl.multiple_of(base * states + i * states, states), states)
            delta = row(delta_all, base + i)
            decay = jnp.exp2(delta * a2)
            drive = row(step_all, base + i) * b_all[at, :]
            if masked:
                keep = keep_at(base + i + 1)
                sb = sb * keep
                g = g * keep
            pb = decay * sb
            sb = pb + drive
            df = row(dm_all, base + i) * c_all[at, :] + g
            g = decay * df
            pf = pf_all[at, :]
            db = db_all[at, :]
            d_expo = df * pf + db * pb
            ga = ga + d_expo * delta
            pf_all[at, :] = pf + drive + sb
            db_all[at, :] = df + db
            exp_all[at, :] = (d_expo * an).astype(bf16)
        return sb, g, ga

    cut = n_pairs - 1 - (first - 1) // (2 * CHUNK)
    _, _, ga = sweep(backward, cut, (zero, zero, zero))
    ga_ref[...] = ga

    def finish(k, carry):
        by_bias, by_skip = carry
        base = pl.multiple_of(k * LANES, LANES)
        here = pl.ds(base, LANES)
        low = proj_ref[here, :].astype(bf16)
        act = act_ref[here, :].astype(f32)
        d_mixed = dm_all[here, :]
        dm_low = d_mixed.astype(bf16)
        step_low = step_all[here, :].astype(bf16)
        y, through, expo, dcm, dbm = [], [], [], [], []
        for c in range(LANES // CHUNK):
            at = pl.ds(pl.multiple_of(base * states + c * wide, wide), wide)
            mine = pl.ds(pl.multiple_of(base + c * CHUNK, CHUNK), CHUNK)
            span = slice(c * CHUNK, (c + 1) * CHUNK)
            both = pf_all[at, :].astype(bf16)
            drv = db_all[at, :].astype(bf16)
            y.append(dot(c_blk_all[mine, :], both))
            through.append(dot(b_blk_all[mine, :], drv))
            expo.append(dot(ones_blk, exp_all[at, :]))
            dcm.append((across(dm_low[span], both) * diag).astype(bf16))
            dbm.append((across(step_low[span], drv) * diag).astype(bf16))
        whole = lambda parts: jnp.concatenate(parts, axis=0)
        skip = skip_ref[...]
        z = z_ref[here, :]
        sigma = jax.nn.sigmoid(z)
        mixed = whole(y) + skip * act
        gated_ref[here, :] = (mixed * (z * sigma)).astype(bf16)
        d_z_ref[here, :] = (d_gated_ref[here, :] * mixed * (sigma * (1.0 + z * (1.0 - sigma)))).astype(bf16)
        via = whole(through)
        d_act_ref[here, :] = d_mixed * skip + via * delta_all[here, :]
        dt_raw = dot(low, w_dt_ref[...]) + dt_bias_ref[...]
        d_dt_raw = (whole(expo) + via * act) * jax.nn.sigmoid(dt_raw)
        d_dt = d_dt_raw.astype(bf16)
        d_dt_ref[here, :] = d_dt
        terms = across(d_dt, w_dt_ref[...]) + across(whole(dbm), pick_b) + across(whole(dcm), pick_c)

        @pl.when(tile == 0)
        def _():
            terms_ref[here, :] = terms

        @pl.when(tile != 0)
        def _():
            terms_ref[here, :] += terms

        total = lambda v: jnp.sum(v, axis=0, keepdims=True)
        return by_bias + total(d_dt_raw), by_skip + total(d_mixed * act)

    none = jnp.zeros((1, channels), f32)
    by_bias, by_skip = lax.fori_loop(0, tokens // LANES, finish, (none, none))
    sums_ref[0:8, :] = jnp.broadcast_to(by_bias, (8, channels))
    sums_ref[8:16, :] = jnp.broadcast_to(by_skip, (8, channels))


def scans(proj, act_low, z_inner, d_gated, w_dt, dt_bias, a_neg, d_skip, begins):
    tokens, channels = act_low.shape
    states = a_neg.shape[0]
    tile = LANES if channels % LANES == 0 else channels
    wide = CHUNK * states
    w_dt = jnp.pad(w_dt, ((0, 2 * states), (0, 0)))
    col = lambda: pl.BlockSpec((tokens, tile), lambda j: (0, j))
    rows = lambda n: pl.BlockSpec((n, tile), lambda j: (0, j))
    full = lambda: pl.BlockSpec(proj.shape, lambda j: (0, 0))
    if z_inner.shape[1] % tile or tile % LANES:
        z_inner = z_inner[:, -channels:]
    ahead = (z_inner.shape[1] - channels) // tile
    z_col = pl.BlockSpec((tokens, tile), lambda j: (0, ahead + j))
    sds = jax.ShapeDtypeStruct
    return pl.pallas_call(
        functools.partial(scan_kernel, begins.shape[1], states),
        grid=(channels // tile,),
        in_specs=[
            pl.BlockSpec(memory_space=pltpu.SMEM),
            full(),
            col(),
            z_col,
            col(),
            rows(w_dt.shape[0]),
            rows(1),
            rows(states),
            rows(1),
        ],
        out_specs=[col(), col(), col(), col(), rows(states), rows(16), full()],
        out_shape=[
            sds((tokens, channels), bf16),
            sds((tokens, channels), bf16),
            sds((tokens, channels), bf16),
            sds((tokens, channels), f32),
            sds((states, channels), f32),
            sds((16, channels), f32),
            sds(proj.shape, f32),
        ],
        scratch_shapes=[pltpu.VMEM((tokens * states, tile), f32)] * 4
        + [pltpu.VMEM((tokens, wide), bf16)] * 2
        + [pltpu.VMEM((tokens, tile), f32)] * 3
        + [pltpu.VMEM((tokens * states, tile), bf16)],
        compiler_params=pltpu.CompilerParams(vmem_limit_bytes=62 * 2**20, dimension_semantics=("arbitrary",)),
        cost_estimate=pl.CostEstimate(
            flops=tokens * channels * states * 60,
            bytes_accessed=tokens * channels * 24,
            transcendentals=2 * tokens * channels * states,
        ),
        name="scan_all",
    )(begins, proj, act_low, z_inner, d_gated, w_dt, dt_bias[None], a_neg, d_skip[None])


EPSILON = 1e-06
HIGHEST = lax.Precision.HIGHEST


def low_dot(left, right):
    return jnp.dot(left, right, preferred_element_type=f32)


def dot_across(left, right):
    return lax.dot_general(left, right, (((1,), (1,)), ((), ())), preferred_element_type=f32)


def dot_tokens(left, right):
    return lax.dot_general(left, right, (((0,), (0,)), ((), ())), preferred_element_type=f32)


def delay_rows(operand, lag):
    if lag == 0:
        return operand
    padding = jnp.zeros((lag,) + operand.shape[1:], operand.dtype)
    return jnp.concatenate([padding, operand[:-lag]], axis=0)


def advance_rows(operand, lag):
    if lag == 0:
        return operand
    padding = jnp.zeros((lag,) + operand.shape[1:], operand.dtype)
    return jnp.concatenate([operand[lag:], padding], axis=0)


def after(x, *others):
    others = tuple(jax.tree.leaves(others))
    return lax.optimization_barrier((x, others))[0] if others else x


class Steps:
    def __init__(self, steps):
        self.steps = steps
        self.result = self.sent = self.arrived = None
        next(steps)

    def go(self, *others):
        if self.result is None:
            try:
                self.sent, self.arrived = self.steps.send(others)
            except StopIteration as stop:
                self.result = stop.value
        return self.arrived

    def end(self, *others):
        while self.result is None:
            self.go(*others)
        return self.result


def silu_slope(operand):
    squash = jax.nn.sigmoid(operand)
    return squash * (1.0 + operand * (1.0 - squash))


class Ring:
    def __init__(self):
        self.n = lax.axis_size("chan")
        self.down = 4 if self.n % 8 == 0 else 1
        self.across = self.n // self.down
        order = [self.at(p) for p in range(self.n)]
        self.right = [(order[k], order[(k + 1) % self.n]) for k in range(self.n)]
        self.left = [(b, a) for a, b in self.right]
        index = lax.axis_index("chan")
        i, j = index // self.across, index % self.across
        back = self.down - 1 - i
        step = jnp.where(back % 2 == 0, j - 1, self.across - 1 - j)
        self.place = jnp.where(j == 0, i, self.down + back * (self.across - 1) + step)

    def at(self, p):
        if self.down == 1:
            return p
        back, step = (p - self.down) // (self.across - 1), (p - self.down) % (self.across - 1)
        if isinstance(p, int):
            column = 1 + step if back % 2 == 0 else self.across - 1 - step
            return p * self.across if p < self.down else (self.down - 1 - back) * self.across + column
        column = jnp.where(back % 2 == 0, 1 + step, self.across - 1 - step)
        return jnp.where(p < self.down, p * self.across, (self.down - 1 - back) * self.across + column)

    def owner(self, away):
        p = self.place + away
        if away > 0:
            p = jnp.where(p >= self.n, p - self.n, p)
        elif away < 0:
            p = jnp.where(p < 0, p + self.n, p)
        return self.at(p)

    def go_right(self, x):
        return lax.ppermute(x, "chan", self.right)

    def go_left(self, x):
        return lax.ppermute(x, "chan", self.left)

    def blocks(self, x):
        half = self.n // 2
        cut = x.shape[0] // 2
        pair = x, x
        found = [(self.owner(0), x)]
        waits = yield
        for step in range(1, half):
            sent = after(pair, waits)
            pair = self.go_right(sent[0]), self.go_left(sent[1])
            found += [(self.owner(-step), pair[0]), (self.owner(step), pair[1])]
            waits = yield sent, pair
        sent = after((pair[0][:cut], pair[1][cut:]), waits)
        pair = self.go_right(sent[0]), self.go_left(sent[1])
        yield sent, pair
        return found + [(self.owner(half), jnp.concatenate(pair, axis=0))]

    def scatter(self, part):
        half = self.n // 2
        rows = part.shape[0] // self.n
        cut = rows // 2
        mine = lambda away: lax.dynamic_slice_in_dim(part, self.owner(away) * rows, rows, 0)
        wide = lambda v: v.astype(f32)
        far = mine(half)
        right, left = yield far[:cut], far[cut:]
        for away in range(half - 1, 0, -1):
            ahead, behind = wide(mine(away)), wide(mine(-away))
            if away == half - 1:
                ahead = jnp.concatenate([ahead[:cut] + wide(right), ahead[cut:]], axis=0)
                behind = jnp.concatenate([behind[:cut], behind[cut:] + wide(left)], axis=0)
            else:
                ahead, behind = ahead + wide(right), behind + wide(left)
            right, left = yield ahead.astype(bf16), behind.astype(bf16)
        return wide(mine(0)) + wide(right) + wide(left)

    def hop(self, sums, *others):
        sums = [one for one in sums if one.result is None]
        if not sums:
            return
        join = lambda side: jnp.concatenate([one.pair[side] for one in sums], axis=0)
        right, left = lax.optimization_barrier((join(0), join(1), tuple(jax.tree.leaves(others))))[:2]
        right, left = lax.optimization_barrier((self.go_right(right), self.go_left(left)))
        at = 0
        for one in sums:
            rows = one.pair[0].shape[0]
            one.take((right[at : at + rows], left[at : at + rows]))
            at += rows


class Scatter:
    def __init__(self, ring, part):
        self.steps = ring.scatter(part)
        self.result, self.arrived = None, None
        self.pair = next(self.steps)

    def take(self, arrived):
        self.arrived = arrived
        try:
            self.pair = self.steps.send(arrived)
        except StopIteration as stop:
            self.result = stop.value


def is_power(n):
    return n & (n - 1) == 0


def bits_of(n):
    return [1 << b for b in range(n.bit_length() - 1)]


def sum_chan(x, wire):
    n = lax.axis_size("chan")
    index = lax.axis_index("chan")
    waits = yield
    if not is_power(n) or x.shape[0] % (16 * n):
        return lax.psum(after(x, waits), "chan")
    perm = lambda b: [(i, i ^ b) for i in range(n)]
    for b in bits_of(n):
        h = x.shape[0] // 2
        upper = (index // b) % 2
        keep = lax.dynamic_slice_in_dim(x, upper * h, h, 0)
        send = lax.dynamic_slice_in_dim(x, (1 - upper) * h, h, 0).astype(wire)
        send = after(send, waits)
        other = lax.ppermute(send, "chan", perm(b))
        waits = yield send, other
        x = keep + other.astype(f32)
    x = x.astype(wire)
    for b in reversed(bits_of(n)):
        upper = (index // b) % 2
        x = after(x, waits)
        other = lax.ppermute(x, "chan", perm(b))
        waits = yield x, other
        x = jnp.concatenate([jnp.where(upper == 0, x, other), jnp.where(upper == 0, other, x)], axis=0)
    return after(x, waits)


def small_gather(x, axis):
    n = lax.axis_size(axis)
    waits = yield
    if not is_power(n) or n > 8:
        return lax.all_gather(after(x, waits), axis, axis=0)
    index = lax.axis_index(axis)
    x = x[None]
    for b in bits_of(n):
        x = after(x, waits)
        other = lax.ppermute(x, axis, [(i, i ^ b) for i in range(n)])
        waits = yield x, other
        other = after(other, waits)
        lower = (index // b) % 2 == 0
        x = jnp.concatenate([jnp.where(lower, x, other), jnp.where(lower, other, x)], axis=0)
    return x


def small_sum(x, axis):
    n = lax.axis_size(axis)
    waits = yield
    if not is_power(n) or n > 8:
        return lax.psum(after(x, waits), axis)
    for b in bits_of(n):
        x = after(x, waits)
        other = lax.ppermute(x, axis, [(i, i ^ b) for i in range(n)])
        waits = yield x, other
        x = x + after(other, waits)
    return x


def join_kernel(upper_ref, mine_ref, other_ref, out_ref):
    k = pl.program_id(0)

    @pl.when(k == upper_ref[0])
    def _():
        out_ref[...] = mine_ref[...]

    @pl.when(k != upper_ref[0])
    def _():
        out_ref[...] = other_ref[...]


def join_halves(mine, other):
    rows, half = mine.shape
    fixed = lambda: pl.BlockSpec((rows, half), lambda k, upper_ref: (0, 0))
    return pl.pallas_call(
        join_kernel,
        grid_spec=pltpu.PrefetchScalarGridSpec(
            num_scalar_prefetch=1,
            grid=(2,),
            in_specs=[fixed(), fixed()],
            out_specs=pl.BlockSpec((rows, half), lambda k, upper_ref: (0, k)),
        ),
        out_shape=jax.ShapeDtypeStruct((rows, 2 * half), f32),
        compiler_params=pltpu.CompilerParams(vmem_limit_bytes=24 * 2**20, dimension_semantics=("arbitrary",)),
        cost_estimate=pl.CostEstimate(flops=0, bytes_accessed=rows * half * 16, transcendentals=0),
        name="join_halves",
    )((lax.axis_index("rows") % 2).astype(jnp.int32)[None], mine, other)


def sum_grad(left, right, wire):
    n = lax.axis_size("rows")
    waits = yield
    left = after(left, waits)
    if n != 4:
        return lax.psum(dot_tokens(left, right), "rows")
    core = [(0, 1), (1, 0), (2, 3), (3, 2)]
    chip = [(0, 2), (2, 0), (1, 3), (3, 1)]
    low, high = right
    send = dot_tokens(left, high)
    other = lax.ppermute(send, "rows", core)
    waits = yield send, other
    pair = (dot_tokens(after(left, send), low) + after(other, waits)).astype(wire)
    other = lax.ppermute(pair, "rows", chip)
    waits = yield pair, other
    total = pair.astype(f32) + after(other, waits).astype(f32)
    other = lax.ppermute(total, "rows", core)
    waits = yield total, other
    return join_halves(total, after(other, waits))


def core_halves(x):
    if lax.axis_size("rows") != 4:
        return x
    half = x.shape[1] // 2
    upper = lax.axis_index("rows") % 2
    part = lambda which: lax.dynamic_slice_in_dim(x, which * half, half, 1)
    return part(upper), part(1 - upper)


def place_norm_kernel(n_seq, count, owners_ref, begins_ref, mod_ref, *refs):
    blocks, (xmod_ref, normed_ref, held) = refs[:count], refs[-3:]
    rows, width = xmod_ref.shape
    step = 2 * CHUNK if rows % (2 * CHUNK) == 0 else rows
    k = pl.program_id(0)
    base = owners_ref[k] * rows

    def hold(block_ref):
        held[...] = block_ref[...]

    for i in range(count):
        pl.when(k == i)(functools.partial(hold, blocks[i]))
    shift, scale = mod_ref[0:1, :], mod_ref[1:2, :]
    gain = mod_ref[3 * n_seq : 3 * n_seq + 1, :]
    for start in range(0, rows, step):
        here = slice(start, start + step)
        wide = held[here, :].astype(f32)
        centred = wide - jnp.sum(wide, axis=1, keepdims=True) * (1.0 / width)
        square = jnp.sum(centred * centred, axis=1, keepdims=True) * (1.0 / width)
        normed = centred * lax.rsqrt(square + EPSILON)
        token = base + start + lax.broadcasted_iota(jnp.int32, (step, 1), 0)
        add, by = shift, gain * (1.0 + scale)
        for s in range(1, n_seq):
            later = token >= begins_ref[0, s]
            add = jnp.where(later, mod_ref[3 * s : 3 * s + 1, :], add)
            by = jnp.where(later, gain * (1.0 + mod_ref[3 * s + 1 : 3 * s + 2, :]), by)
        xmod_ref[here, :] = (normed * by + add).astype(bf16)
        normed_ref[here, :] = normed.astype(bf16)


def place_gate_kernel(n_seq, count, owners_ref, begins_ref, mod_ref, *refs):
    blocks, (gated_ref, plain_ref) = refs[:count], refs[-2:]
    rows = gated_ref.shape[0]
    step = CHUNK if rows % CHUNK == 0 else rows
    k = pl.program_id(0)
    base = owners_ref[k] * rows

    def fill(block_ref):
        def part(p, carry):
            here = pl.ds(pl.multiple_of(p * step, step), step)
            low = block_ref[here, :]
            token = base + p * step + lax.broadcasted_iota(jnp.int32, (step, 1), 0)
            gate = mod_ref[2:3, :]
            for s in range(1, n_seq):
                gate = jnp.where(token >= begins_ref[0, s], mod_ref[3 * s + 2 : 3 * s + 3, :], gate)
            gated_ref[here, :] = (low.astype(f32) * gate).astype(bf16)
            plain_ref[here, :] = low
            return carry

        lax.fori_loop(0, rows // step, part, 0)

    for i in range(count):
        pl.when(k == i)(functools.partial(fill, blocks[i]))


def place(kernel, blocks, begins, mod, name, total, scratch=False, into=()):
    owners = jnp.stack([owner for owner, _ in blocks]).astype(jnp.int32)
    parts = [block for _, block in blocks]
    rows, width = parts[0].shape
    count = len(parts)
    whole = jax.ShapeDtypeStruct((total, width), bf16)
    held = [pl.BlockSpec(memory_space=pl.ANY)] * len(into)
    out = lambda: pl.BlockSpec((rows, width), lambda k, owners_ref, begins_ref: (owners_ref[k], 0))
    fixed = lambda shape: pl.BlockSpec(shape, lambda k, owners_ref, begins_ref: (0, 0))
    return pl.pallas_call(
        functools.partial(kernel, begins.shape[1], count),
        grid_spec=pltpu.PrefetchScalarGridSpec(
            num_scalar_prefetch=2,
            grid=(count,),
            in_specs=[fixed(mod.shape)] + [fixed((rows, width))] * count + held,
            out_specs=[out(), out()],
            scratch_shapes=[pltpu.VMEM((rows, width), bf16)] if scratch else [],
        ),
        out_shape=[whole, whole],
        input_output_aliases={3 + count + k: k for k in range(len(into))},
        compiler_params=pltpu.CompilerParams(vmem_limit_bytes=28 * 2**20, dimension_semantics=("arbitrary",)),
        cost_estimate=pl.CostEstimate(
            flops=count * rows * width * 20, bytes_accessed=count * rows * width * 6, transcendentals=0
        ),
        name=name,
    )(owners, begins, mod, *parts, *into)


def sums_kernel(n_seq, begins_ref, share_ref, normed_ref, up_ref, branch_ref, out_ref):
    rows, width = share_ref.shape
    k = pl.program_id(0)

    @pl.when(k == 0)
    def _():
        out_ref[...] = jnp.zeros(out_ref.shape, f32)

    lanes = 2 * LANES if width % (2 * LANES) == 0 else width
    token = k * rows + lax.broadcasted_iota(jnp.int32, (rows, 1), 0)
    for at in range(0, width, lanes):
        cols = slice(at, at + lanes)
        share = share_ref[:, cols].astype(f32)
        terms = [share, share * normed_ref[:, cols].astype(f32)]
        terms.append(up_ref[:, cols].astype(f32) * branch_ref[:, cols].astype(f32))
        for j, term in enumerate(terms):
            rest = jnp.sum(term, axis=0, keepdims=True)
            for s in range(n_seq - 1, 0, -1):
                later = jnp.sum(jnp.where(token >= begins_ref[0, s], term, 0.0), axis=0, keepdims=True)
                at_row = j * n_seq + s
                mine = later if s == n_seq - 1 else later - after_it
                out_ref[at_row : at_row + 1, cols] += mine
                after_it = later
            out_ref[j * n_seq : j * n_seq + 1, cols] += rest - (after_it if n_seq > 1 else 0.0)


def token_sums(share, normed, up, branch, begins):
    tokens, width = share.shape
    n_seq = begins.shape[1]
    rows = LANES
    spec = lambda: pl.BlockSpec((rows, width), lambda k: (k, 0))
    height = 3 * n_seq + (-3 * n_seq % 8)
    return pl.pallas_call(
        functools.partial(sums_kernel, n_seq),
        grid=(tokens // rows,),
        in_specs=[pl.BlockSpec(memory_space=pltpu.SMEM), spec(), spec(), spec(), spec()],
        out_specs=pl.BlockSpec((height, width), lambda k: (0, 0)),
        out_shape=jax.ShapeDtypeStruct((height, width), f32),
        compiler_params=pltpu.CompilerParams(vmem_limit_bytes=32 * 2**20, dimension_semantics=("arbitrary",)),
        cost_estimate=pl.CostEstimate(flops=tokens * width * 12, bytes_accessed=tokens * width * 8, transcendentals=0),
        name="token_sums",
    )(begins, share, normed, up, branch)


def local(
    activations,
    condition,
    seq_lengths,
    w_ada,
    b_ada,
    norm_gain,
    w_in_x,
    w_in_z,
    conv_weight,
    conv_bias,
    w_xproj,
    w_dt,
    dt_bias,
    a_log,
    d_skip,
    w_out,
    grad_out,
):
    ring = Ring()
    tok_loc, width = activations.shape
    low_rank = w_dt.shape[0]
    states = a_log.shape[1]
    channels = a_log.shape[0]
    conv_taps = conv_weight.shape[1]
    tok_count = tok_loc * ring.n
    tok_start = lax.axis_index("chan") * tok_loc
    act_ring = Steps(ring.blocks(activations))
    act_in = [act_ring.go()]
    cond_act = jax.nn.silu(condition.astype(f32)).astype(bf16)
    modulation = (
        jnp.einsum("si,kji->skj", cond_act, w_ada, preferred_element_type=f32) + b_ada[None]
    )
    part_width = norm_gain.shape[0]
    seq_count = seq_lengths.shape[1]
    packed = jnp.concatenate([modulation.reshape(3 * seq_count, part_width), norm_gain[None]], axis=0)
    packing = Steps(small_gather(packed, "chan"))
    packing.go()
    act_in.append(act_ring.go())
    packing.go(act_in[0])
    seq_lengths, conv_weight, conv_bias, w_dt, dt_bias, a_log, d_skip = after(
        (seq_lengths, conv_weight, conv_bias, w_dt, dt_bias, a_log, d_skip), act_in[0]
    )
    w_in = after(jnp.concatenate([w_in_x, w_in_z], axis=0), act_in[0])
    seq_lens = seq_lengths[0]
    seq_ends = jnp.cumsum(seq_lens)
    begins = seq_ends - seq_lens
    position = jnp.arange(tok_count, dtype=jnp.int32)
    member = (position[:, None] >= begins[None, :]) & (position[:, None] < seq_ends[None, :])
    onehot = member.astype(f32)
    in_seq = jnp.sum(onehot * (position[:, None] - begins[None, :]).astype(f32), axis=1)
    per_token = lambda rows, hot: sum(hot[:, s : s + 1] * rows[s][None] for s in range(seq_count))
    a_neg = -jnp.exp(a_log).T
    act_in.append(act_ring.go(w_in, in_seq))
    packing.go(act_in[1])
    far_wait = packing.arrived
    packed = packing.end().transpose(1, 0, 2).reshape(3 * seq_count + 1, width)
    packed = jnp.pad(packed, ((0, -packed.shape[0] % 8), (0, 0)))
    mod_full = packed[: 3 * seq_count].reshape(seq_count, 3, width)
    gain_full = packed[3 * seq_count]
    act_ring.go(far_wait)
    act_blocks = act_ring.end()
    soon = 5 if len(act_blocks) == 8 else 0
    norm = functools.partial(place, place_norm_kernel, begins=begins[None], mod=packed, total=tok_count, scratch=True)
    so_far = tuple(norm(act_blocks[:soon], name="place_norm_soon")) if soon else ()
    up_ring = Steps(ring.blocks(after(grad_out, act_in[-1])))
    up_in = [up_ring.go()]
    xmod, normed = norm(act_blocks[soon:], name="place_norm", into=so_far)
    inner = dot_across(xmod, w_in)
    x_inner = inner[:, :channels]
    xmod_halves = core_halves(after(xmod, inner))
    conv_pre = jnp.zeros_like(x_inner) + conv_bias[None, :]
    for tap_index in range(conv_taps):
        lag = conv_taps - 1 - tap_index
        valid = (in_seq >= lag).astype(f32)[:, None]
        conv_pre = conv_pre + conv_weight[:, tap_index][None, :] * delay_rows(x_inner, lag) * valid
    act_low = jax.nn.silu(conv_pre).astype(bf16)
    up_in.append(up_ring.go())
    adding = Steps(sum_chan(low_dot(act_low, w_xproj), PROJ_WIRE))
    adding.go(up_in[0])
    adding.go()
    adding.go(up_in[1])
    up_in.append(up_ring.go())
    adding.go()
    adding.go(up_in[2])
    up_ring.go()
    proj = adding.end()
    dt_low = proj[:, :low_rank].astype(bf16)
    d_branch_all, whole_up = place(
        place_gate_kernel, up_ring.end(), begins[None], packed, "place_gate", tok_count
    )
    d_gated = dot_across(d_branch_all, w_out)
    gated, d_z_low, d_dt_low, d_act, d_log, bias_skip, proj_terms = scans(
        proj, act_low, inner, d_gated, w_dt, dt_bias, a_neg, d_skip, begins[None]
    )
    adding = Steps(sum_chan(proj_terms, DPROJ_WIRE))
    branch_part = lax.optimization_barrier(low_dot(gated, w_out).astype(bf16))
    branch_sum = Scatter(ring, branch_part)
    adding.go()
    ring.hop([branch_sum])
    out_rows = Steps(sum_grad(gated, core_halves(d_branch_all), bf16))
    in_z_rows = Steps(sum_grad(d_z_low, xmod_halves, bf16))
    out_rows.go(branch_part)
    arrived = adding.arrived
    adding.go(out_rows.sent)
    in_z_rows.go(arrived)
    arrived = adding.arrived
    adding.go(in_z_rows.sent, branch_sum.arrived)
    ring.hop([branch_sum])
    out_rows.go(arrived)
    arrived = adding.arrived
    adding.go(out_rows.sent)
    in_z_rows.go(arrived)
    adding.go(in_z_rows.sent)
    adding.go()
    d_proj = adding.end().astype(bf16)
    d_act = d_act + dot_across(d_proj, w_xproj)
    d_conv = d_act * silu_slope(conv_pre)
    d_x_inner = jnp.zeros_like(d_conv)
    tap_grads = []
    for tap_index in range(conv_taps):
        lag = conv_taps - 1 - tap_index
        valid = (in_seq >= lag).astype(f32)[:, None]
        masked = d_conv * valid
        tap_grads.append(jnp.sum(masked * delay_rows(x_inner, lag), axis=0))
        d_x_inner = d_x_inner + conv_weight[:, tap_index][None, :] * advance_rows(masked, lag)
    d_x_low = d_x_inner.astype(bf16)
    in_x_rows = Steps(sum_grad(d_x_low, xmod_halves, bf16))
    in_x_rows.go()
    d_x_late, d_z_low = after((d_x_low, d_z_low), in_x_rows.sent)
    d_xmod_part = (low_dot(d_x_late, w_in_x) + low_dot(d_z_low, w_in_z)).astype(bf16)
    d_xmod_part = lax.optimization_barrier(d_xmod_part)
    d_xmod_sum = Scatter(ring, d_xmod_part)
    both = [branch_sum, d_xmod_sum]
    ring.hop(both)
    first = d_xmod_sum.arrived
    ring.hop(both)
    share = after(d_xmod_part, first)
    summing = Steps(small_sum(token_sums(share, normed, whole_up, branch_part, begins[None]), "chan"))
    summing.go()
    in_x_rows.go(first)
    out_rows.go(first)
    d_proj = after(d_proj, first)
    small = jnp.concatenate(
        [
            dot_tokens(d_proj, act_low),
            dot_tokens(dt_low, d_dt_low),
            d_log * a_neg,
            jnp.stack(tap_grads),
            jnp.sum(d_conv, axis=0)[None],
            bias_skip[0:1],
            bias_skip[8:9],
        ],
        axis=0,
    )
    small = jnp.pad(small, ((0, -small.shape[0] % 16), (0, 0)))
    small_rows = Steps(small_sum(small, "rows"))
    small_rows.go()
    second = d_xmod_sum.arrived
    ring.hop(both, summing.sent, in_x_rows.sent, out_rows.sent, small_rows.sent)
    summing.go(second)
    in_z_rows.go(second)
    small_rows.go(second)
    grad_w_out = out_rows.end(second)
    third = d_xmod_sum.arrived
    ring.hop(both, summing.sent, in_z_rows.sent, small_rows.sent, grad_w_out)
    summing.go(third)
    in_x_rows.go(third)
    grad_w_in_z = in_z_rows.end(third)
    while d_xmod_sum.result is None:
        ring.hop(both)
    branch, d_xmod = branch_sum.result, d_xmod_sum.result
    grad_w_in_x = in_x_rows.end(d_xmod_sum.arrived)
    small = small_rows.end(d_xmod_sum.arrived)
    onehot_loc = lax.dynamic_slice_in_dim(onehot, tok_start, tok_loc, 0)
    counts = [w_xproj.shape[1], low_rank, states, conv_taps, 1, 1, 1]
    pieces, at = [], 0
    for count in counts:
        pieces.append(small[at : at + count])
        at += count
    sums = summing.end(d_xmod_sum.arrived)
    sums = lax.dynamic_slice_in_dim(sums, lax.axis_index("chan") * part_width, part_width, 1)
    by_shift, by_scale, by_gate = [sums[k * seq_count : (k + 1) * seq_count] for k in range(3)]
    gain_term = jnp.sum(by_scale * (1.0 + modulation[:, 1]), axis=0)
    d_mod = jnp.stack([by_shift, by_scale * norm_gain[None], by_gate], axis=1)
    cond_rows = cond_act.astype(f32).reshape(-1, part_width)
    reach = jnp.concatenate([d_mod.reshape(3 * seq_count, part_width), gain_term[None], cond_rows], axis=0)
    reach = Steps(small_gather(reach, "rows")).end()
    cond_all = reach[:, 3 * seq_count + 1 :].reshape(-1, width)
    block_out = (activations.astype(f32) + per_token(mod_full[:, 2], onehot_loc) * branch).astype(bf16)
    grad_gain = jnp.sum(reach[:, 3 * seq_count], axis=0)
    d_mod_all = reach[:, : 3 * seq_count].reshape(-1, 3, part_width)
    grad_b_ada = jnp.sum(d_mod_all, axis=0)
    grad_w_ada = jnp.einsum(
        "skj,si->kji",
        d_mod_all,
        cond_all,
        precision=HIGHEST,
        preferred_element_type=f32,
    )
    wide_loc = activations.astype(f32)
    centred_loc = wide_loc - jnp.mean(wide_loc, axis=1, keepdims=True)
    inv_std_loc = lax.rsqrt(jnp.mean(centred_loc * centred_loc, axis=1, keepdims=True) + EPSILON)
    normed_loc = centred_loc * inv_std_loc
    scale_loc = per_token(mod_full[:, 1], onehot_loc)
    d_normed = d_xmod * (1.0 + scale_loc) * gain_full[None, :]
    mean_first = jnp.mean(d_normed, axis=1, keepdims=True)
    mean_second = jnp.mean(d_normed * normed_loc, axis=1, keepdims=True)
    grad_input = (
        inv_std_loc * (d_normed - mean_first - normed_loc * mean_second) + grad_out.astype(f32)
    ).astype(bf16)
    return (
        block_out,
        grad_input,
        grad_w_ada,
        grad_b_ada,
        grad_gain,
        grad_w_in_x,
        grad_w_in_z,
        pieces[3].T,
        pieces[4][0],
        pieces[0].T,
        pieces[1],
        pieces[5][0],
        pieces[2].T,
        pieces[6][0],
        grad_w_out,
    )


PROJ_WIRE = bf16
DPROJ_WIRE = bf16


def solution(mesh):
    return jax.shard_map(
        local,
        mesh=mesh,
        in_specs=(
            P(("rows", "chan"), None),
            P("rows", None),
            P("rows", None),
            P(None, "chan", None),
            P(None, "chan"),
            P("chan"),
            P("chan", None),
            P("chan", None),
            P("chan", None),
            P("chan"),
            P("chan", None),
            P(None, "chan"),
            P("chan"),
            P("chan", None),
            P("chan"),
            P("chan", None),
            P(("rows", "chan"), None),
        ),
        out_specs=(
            P(("rows", "chan"), None),
            P(("rows", "chan"), None),
            P(None, "chan", None),
            P(None, "chan"),
            P("chan"),
            P("chan", None),
            P("chan", None),
            P("chan", None),
            P("chan"),
            P("chan", None),
            P(None, "chan"),
            P("chan"),
            P("chan", None),
            P("chan"),
            P("chan", None),
        ),
        check_vma=False,
    )
```

```python
import functools
import math

import jax
import jax.numpy as jnp
from jax import lax
from jax.experimental import pallas as pl
from jax.experimental.pallas import tpu as pltpu
from jax.sharding import PartitionSpec as P

CHUNK = 16
LANES = 128
LOG2E = math.log2(math.e)
f32 = jnp.float32
bf16 = jnp.bfloat16


def scan_kernel(
    n_seq,
    states,
    begins_ref,
    proj_ref,
    act_ref,
    z_ref,
    d_gated_ref,
    w_dt_ref,
    dt_bias_ref,
    an_ref,
    skip_ref,
    gated_ref,
    d_z_ref,
    d_dt_ref,
    d_act_ref,
    ga_ref,
    sums_ref,
    terms_ref,
    b_all,
    c_all,
    pf_all,
    db_all,
    b_blk_all,
    c_blk_all,
    delta_all,
    step_all,
    dm_all,
    exp_all,
):
    tokens, channels = act_ref.shape
    n_pairs = tokens // (2 * CHUNK)
    wide = CHUNK * states
    low_rank = proj_ref.shape[1] - 2 * states
    an = an_ref[...]
    a2 = an * LOG2E
    dot = functools.partial(jnp.dot, preferred_element_type=f32)
    across = functools.partial(
        lax.dot_general, dimension_numbers=(((1,), (1,)), ((), ())), preferred_element_type=f32
    )

    def diagonal(rows):
        r = lax.broadcasted_iota(jnp.int32, (rows, wide), 0) % CHUNK
        return (r == lax.broadcasted_iota(jnp.int32, (rows, wide), 1) // states).astype(f32)

    diag = diagonal(CHUNK)
    ones_blk = diag.astype(bf16)
    m = lax.broadcasted_iota(jnp.int32, (low_rank + 2 * states, wide), 0)
    q = lax.broadcasted_iota(jnp.int32, (low_rank + 2 * states, wide), 1) % states
    pick_b = (m == low_rank + q).astype(bf16)
    pick_c = (m == low_rank + states + q).astype(bf16)
    tile = pl.program_id(0)

    @pl.when(tile == 0)
    def _():
        many = diagonal(LANES)

        def spread(k, carry):
            base = pl.multiple_of(k * LANES, LANES)
            proj = proj_ref[pl.ds(base, LANES), :]
            low = proj.astype(bf16)
            b_blk_all[pl.ds(base, LANES), :] = (dot(low, pick_b) * many).astype(bf16)
            c_blk_all[pl.ds(base, LANES), :] = (dot(low, pick_c) * many).astype(bf16)
            turned = proj.astype(f32).T
            bt = turned[low_rank : low_rank + states]
            ct = turned[low_rank + states :]
            for i in range(LANES):
                at = pl.ds(pl.multiple_of(base * states + i * states, states), states)
                b_all[at, :] = jnp.broadcast_to(bt[:, i : i + 1], (states, channels))
                c_all[at, :] = jnp.broadcast_to(ct[:, i : i + 1], (states, channels))
            return carry

        lax.fori_loop(0, tokens // LANES, spread, 0)

    def prepare(k, carry):
        here = pl.ds(pl.multiple_of(k * LANES, LANES), LANES)
        dt_raw = dot(proj_ref[here, :].astype(bf16), w_dt_ref[...]) + dt_bias_ref[...]
        delta = jnp.maximum(dt_raw, 0.0) + jnp.log1p(jnp.exp(-jnp.abs(dt_raw)))
        delta_all[here, :] = delta
        step_all[here, :] = delta * act_ref[here, :].astype(f32)
        z = z_ref[here, :]
        dm_all[here, :] = d_gated_ref[here, :] * (z * jax.nn.sigmoid(z))
        return carry

    lax.fori_loop(0, tokens // LANES, prepare, 0, unroll=5 if tokens % (5 * LANES) == 0 else 1)

    def keep_at(t):
        keep = None
        for s in range(1, n_seq):
            k = jnp.where(begins_ref[0, s] == t, 0.0, 1.0).astype(f32)
            keep = k if keep is None else keep * k
        return keep

    def sweep(body, cut, carry):
        plain, masked = functools.partial(body, False), functools.partial(body, True)
        if n_seq == 1:
            return lax.fori_loop(0, n_pairs, plain, carry)
        if n_seq > 2:
            return lax.fori_loop(0, n_pairs, masked, carry)
        carry = lax.fori_loop(0, cut, plain, carry)
        carry = masked(cut, carry)
        return lax.fori_loop(cut + 1, n_pairs, plain, carry)

    def row(ref, t):
        return ref[pl.ds(t, 1), :]

    def forward(masked, pair, carry):
        sf, g = carry
        base = pl.multiple_of(pair * 2 * CHUNK, 2 * CHUNK)
        for i in range(2 * CHUNK):
            at = pl.ds(pl.multiple_of(base * states + i * states, states), states)
            decay = jnp.exp2(row(delta_all, base + i) * a2)
            if masked:
                keep = keep_at(base + i)
                sf = sf * keep
                g = g * keep
            pf = decay * sf
            sf = pf + row(step_all, base + i) * b_all[at, :]
            db = row(dm_all, base + i) * c_all[at, :] + g
            g = decay * db
            pf_all[at, :] = pf
            db_all[at, :] = db
        return sf, g

    zero = jnp.zeros((states, channels), f32)
    first = begins_ref[0, n_seq - 1]
    sweep(forward, first // (2 * CHUNK), (zero, zero))

    def backward(masked, k, carry):
        sb, g, ga = carry
        base = pl.multiple_of((n_pairs - 1 - k) * 2 * CHUNK, 2 * CHUNK)
        for i in range(2 * CHUNK - 1, -1, -1):
            at = pl.ds(pl.multiple_of(base * states + i * states, states), states)
            delta = row(delta_all, base + i)
            decay = jnp.exp2(delta * a2)
            drive = row(step_all, base + i) * b_all[at, :]
            if masked:
                keep = keep_at(base + i + 1)
                sb = sb * keep
                g = g * keep
            pb = decay * sb
            sb = pb + drive
            df = row(dm_all, base + i) * c_all[at, :] + g
            g = decay * df
            pf = pf_all[at, :]
            db = db_all[at, :]
            d_expo = df * pf + db * pb
            ga = ga + d_expo * delta
            pf_all[at, :] = pf + drive + sb
            db_all[at, :] = df + db
            exp_all[at, :] = (d_expo * an).astype(bf16)
        return sb, g, ga

    cut = n_pairs - 1 - (first - 1) // (2 * CHUNK)
    _, _, ga = sweep(backward, cut, (zero, zero, zero))
    ga_ref[...] = ga

    def finish(k, carry):
        by_bias, by_skip = carry
        base = pl.multiple_of(k * LANES, LANES)
        here = pl.ds(base, LANES)
        low = proj_ref[here, :].astype(bf16)
        act = act_ref[here, :].astype(f32)
        d_mixed = dm_all[here, :]
        dm_low = d_mixed.astype(bf16)
        step_low = step_all[here, :].astype(bf16)
        y, through, expo, dcm, dbm = [], [], [], [], []
        for c in range(LANES // CHUNK):
            at = pl.ds(pl.multiple_of(base * states + c * wide, wide), wide)
            mine = pl.ds(pl.multiple_of(base + c * CHUNK, CHUNK), CHUNK)
            span = slice(c * CHUNK, (c + 1) * CHUNK)
            both = pf_all[at, :].astype(bf16)
            drv = db_all[at, :].astype(bf16)
            y.append(dot(c_blk_all[mine, :], both))
            through.append(dot(b_blk_all[mine, :], drv))
            expo.append(dot(ones_blk, exp_all[at, :]))
            dcm.append((across(dm_low[span], both) * diag).astype(bf16))
            dbm.append((across(step_low[span], drv) * diag).astype(bf16))
        whole = lambda parts: jnp.concatenate(parts, axis=0)
        skip = skip_ref[...]
        z = z_ref[here, :]
        sigma = jax.nn.sigmoid(z)
        mixed = whole(y) + skip * act
        gated_ref[here, :] = (mixed * (z * sigma)).astype(bf16)
        d_z_ref[here, :] = (d_gated_ref[here, :] * mixed * (sigma * (1.0 + z * (1.0 - sigma)))).astype(bf16)
        via = whole(through)
        d_act_ref[here, :] = d_mixed * skip + via * delta_all[here, :]
        dt_raw = dot(low, w_dt_ref[...]) + dt_bias_ref[...]
        d_dt_raw = (whole(expo) + via * act) * jax.nn.sigmoid(dt_raw)
        d_dt = d_dt_raw.astype(bf16)
        d_dt_ref[here, :] = d_dt
        terms = across(d_dt, w_dt_ref[...]) + across(whole(dbm), pick_b) + across(whole(dcm), pick_c)

        @pl.when(tile == 0)
        def _():
            terms_ref[here, :] = terms

        @pl.when(tile != 0)
        def _():
            terms_ref[here, :] += terms

        total = lambda v: jnp.sum(v, axis=0, keepdims=True)
        return by_bias + total(d_dt_raw), by_skip + total(d_mixed * act)

    none = jnp.zeros((1, channels), f32)
    by_bias, by_skip = lax.fori_loop(0, tokens // LANES, finish, (none, none))
    sums_ref[0:8, :] = jnp.broadcast_to(by_bias, (8, channels))
    sums_ref[8:16, :] = jnp.broadcast_to(by_skip, (8, channels))


def scans(proj, act_low, z_inner, d_gated, w_dt, dt_bias, a_neg, d_skip, begins):
    tokens, channels = act_low.shape
    states = a_neg.shape[0]
    tile = LANES if channels % LANES == 0 else channels
    wide = CHUNK * states
    w_dt = jnp.pad(w_dt, ((0, 2 * states), (0, 0)))
    col = lambda: pl.BlockSpec((tokens, tile), lambda j: (0, j))
    rows = lambda n: pl.BlockSpec((n, tile), lambda j: (0, j))
    full = lambda: pl.BlockSpec(proj.shape, lambda j: (0, 0))
    if z_inner.shape[1] % tile or tile % LANES:
        z_inner = z_inner[:, -channels:]
    ahead = (z_inner.shape[1] - channels) // tile
    z_col = pl.BlockSpec((tokens, tile), lambda j: (0, ahead + j))
    sds = jax.ShapeDtypeStruct
    return pl.pallas_call(
        functools.partial(scan_kernel, begins.shape[1], states),
        grid=(channels // tile,),
        in_specs=[
            pl.BlockSpec(memory_space=pltpu.SMEM),
            full(),
            col(),
            z_col,
            col(),
            rows(w_dt.shape[0]),
            rows(1),
            rows(states),
            rows(1),
        ],
        out_specs=[col(), col(), col(), col(), rows(states), rows(16), full()],
        out_shape=[
            sds((tokens, channels), bf16),
            sds((tokens, channels), bf16),
            sds((tokens, channels), bf16),
            sds((tokens, channels), f32),
            sds((states, channels), f32),
            sds((16, channels), f32),
            sds(proj.shape, f32),
        ],
        scratch_shapes=[pltpu.VMEM((tokens * states, tile), f32)] * 4
        + [pltpu.VMEM((tokens, wide), bf16)] * 2
        + [pltpu.VMEM((tokens, tile), f32)] * 3
        + [pltpu.VMEM((tokens * states, tile), bf16)],
        compiler_params=pltpu.CompilerParams(vmem_limit_bytes=62 * 2**20, dimension_semantics=("arbitrary",)),
        cost_estimate=pl.CostEstimate(
            flops=tokens * channels * states * 60,
            bytes_accessed=tokens * channels * 24,
            transcendentals=2 * tokens * channels * states,
        ),
        name="scan_all",
    )(begins, proj, act_low, z_inner, d_gated, w_dt, dt_bias[None], a_neg, d_skip[None])


EPSILON = 1e-06
HIGHEST = lax.Precision.HIGHEST


def low_dot(left, right):
    return jnp.dot(left, right, preferred_element_type=f32)


def dot_across(left, right):
    return lax.dot_general(left, right, (((1,), (1,)), ((), ())), preferred_element_type=f32)


def dot_tokens(left, right):
    return lax.dot_general(left, right, (((0,), (0,)), ((), ())), preferred_element_type=f32)


def delay_rows(operand, lag):
    if lag == 0:
        return operand
    padding = jnp.zeros((lag,) + operand.shape[1:], operand.dtype)
    return jnp.concatenate([padding, operand[:-lag]], axis=0)


def advance_rows(operand, lag):
    if lag == 0:
        return operand
    padding = jnp.zeros((lag,) + operand.shape[1:], operand.dtype)
    return jnp.concatenate([operand[lag:], padding], axis=0)


def after(x, *others):
    others = tuple(jax.tree.leaves(others))
    return lax.optimization_barrier((x, others))[0] if others else x


class Steps:
    def __init__(self, steps):
        self.steps = steps
        self.result = self.sent = self.arrived = None
        next(steps)

    def go(self, *others):
        if self.result is None:
            try:
                self.sent, self.arrived = self.steps.send(others)
            except StopIteration as stop:
                self.result = stop.value
        return self.arrived

    def end(self, *others):
        while self.result is None:
            self.go(*others)
        return self.result


def silu_slope(operand):
    squash = jax.nn.sigmoid(operand)
    return squash * (1.0 + operand * (1.0 - squash))


class Ring:
    def __init__(self):
        self.n = lax.axis_size("chan")
        self.down = 4 if self.n % 8 == 0 else 1
        self.across = self.n // self.down
        order = [self.at(p) for p in range(self.n)]
        self.right = [(order[k], order[(k + 1) % self.n]) for k in range(self.n)]
        self.left = [(b, a) for a, b in self.right]
        index = lax.axis_index("chan")
        i, j = index // self.across, index % self.across
        back = self.down - 1 - i
        step = jnp.where(back % 2 == 0, j - 1, self.across - 1 - j)
        self.place = jnp.where(j == 0, i, self.down + back * (self.across - 1) + step)

    def at(self, p):
        if self.down == 1:
            return p
        back, step = (p - self.down) // (self.across - 1), (p - self.down) % (self.across - 1)
        if isinstance(p, int):
            column = 1 + step if back % 2 == 0 else self.across - 1 - step
            return p * self.across if p < self.down else (self.down - 1 - back) * self.across + column
        column = jnp.where(back % 2 == 0, 1 + step, self.across - 1 - step)
        return jnp.where(p < self.down, p * self.across, (self.down - 1 - back) * self.across + column)

    def owner(self, away):
        p = self.place + away
        if away > 0:
            p = jnp.where(p >= self.n, p - self.n, p)
        elif away < 0:
            p = jnp.where(p < 0, p + self.n, p)
        return self.at(p)

    def go_right(self, x):
        return lax.ppermute(x, "chan", self.right)

    def go_left(self, x):
        return lax.ppermute(x, "chan", self.left)

    def blocks(self, x):
        half = self.n // 2
        cut = x.shape[0] // 2
        pair = x, x
        found = [(self.owner(0), x)]
        waits = yield
        for step in range(1, half):
            sent = after(pair, waits)
            pair = self.go_right(sent[0]), self.go_left(sent[1])
            found += [(self.owner(-step), pair[0]), (self.owner(step), pair[1])]
            waits = yield sent, pair
        sent = after((pair[0][:cut], pair[1][cut:]), waits)
        pair = self.go_right(sent[0]), self.go_left(sent[1])
        yield sent, pair
        return found + [(self.owner(half), jnp.concatenate(pair, axis=0))]

    def scatter(self, part):
        half = self.n // 2
        rows = part.shape[0] // self.n
        cut = rows // 2
        mine = lambda away: lax.dynamic_slice_in_dim(part, self.owner(away) * rows, rows, 0)
        wide = lambda v: v.astype(f32)
        far = mine(half)
        right, left = yield far[:cut], far[cut:]
        for away in range(half - 1, 0, -1):
            ahead, behind = wide(mine(away)), wide(mine(-away))
            if away == half - 1:
                ahead = jnp.concatenate([ahead[:cut] + wide(right), ahead[cut:]], axis=0)
                behind = jnp.concatenate([behind[:cut], behind[cut:] + wide(left)], axis=0)
            else:
                ahead, behind = ahead + wide(right), behind + wide(left)
            right, left = yield ahead.astype(bf16), behind.astype(bf16)
        return wide(mine(0)) + wide(right) + wide(left)

    def hop(self, sums, *others):
        self.land(self.launch(sums, *others))

    def launch(self, sums, *others):
        sums = [one for one in sums if one.result is None]
        if not sums:
            return sums, None
        join = lambda side: jnp.concatenate([one.pair[side] for one in sums], axis=0)
        right, left = lax.optimization_barrier((join(0), join(1), tuple(jax.tree.leaves(others))))[:2]
        return sums, (self.go_right(right), self.go_left(left))

    def land(self, flight, *others):
        sums, pair = flight
        if not sums:
            return
        right, left = lax.optimization_barrier((pair, tuple(jax.tree.leaves(others))))[0]
        at = 0
        for one in sums:
            rows = one.pair[0].shape[0]
            one.take((right[at : at + rows], left[at : at + rows]))
            at += rows


class Scatter:
    def __init__(self, ring, part):
        self.steps = ring.scatter(part)
        self.result, self.arrived = None, None
        self.pair = next(self.steps)

    def take(self, arrived):
        self.arrived = arrived
        try:
            self.pair = self.steps.send(arrived)
        except StopIteration as stop:
            self.result = stop.value


def is_power(n):
    return n & (n - 1) == 0


def bits_of(n):
    return [1 << b for b in range(n.bit_length() - 1)]


def sum_chan(x, wire):
    n = lax.axis_size("chan")
    index = lax.axis_index("chan")
    waits = yield
    if not is_power(n) or x.shape[0] % (16 * n):
        return lax.psum(after(x, waits), "chan")
    perm = lambda b: [(i, i ^ b) for i in range(n)]
    for b in bits_of(n):
        h = x.shape[0] // 2
        upper = (index // b) % 2
        keep = lax.dynamic_slice_in_dim(x, upper * h, h, 0)
        send = lax.dynamic_slice_in_dim(x, (1 - upper) * h, h, 0).astype(wire)
        send = after(send, waits)
        other = lax.ppermute(send, "chan", perm(b))
        waits = yield send, other
        x = keep + other.astype(f32)
    x = x.astype(wire)
    for b in reversed(bits_of(n)):
        upper = (index // b) % 2
        x = after(x, waits)
        other = lax.ppermute(x, "chan", perm(b))
        waits = yield x, other
        x = jnp.concatenate([jnp.where(upper == 0, x, other), jnp.where(upper == 0, other, x)], axis=0)
    return after(x, waits)


def small_gather(x, axis):
    n = lax.axis_size(axis)
    waits = yield
    if not is_power(n) or n > 8:
        return lax.all_gather(after(x, waits), axis, axis=0)
    index = lax.axis_index(axis)
    x = x[None]
    for b in bits_of(n):
        x = after(x, waits)
        other = lax.ppermute(x, axis, [(i, i ^ b) for i in range(n)])
        waits = yield x, other
        other = after(other, waits)
        lower = (index // b) % 2 == 0
        x = jnp.concatenate([jnp.where(lower, x, other), jnp.where(lower, other, x)], axis=0)
    return x


def small_sum(x, axis):
    n = lax.axis_size(axis)
    waits = yield
    if not is_power(n) or n > 8:
        return lax.psum(after(x, waits), axis)
    for b in bits_of(n):
        x = after(x, waits)
        other = lax.ppermute(x, axis, [(i, i ^ b) for i in range(n)])
        waits = yield x, other
        x = x + after(other, waits)
    return x


def join_kernel(upper_ref, mine_ref, other_ref, out_ref):
    k = pl.program_id(0)

    @pl.when(k == upper_ref[0])
    def _():
        out_ref[...] = mine_ref[...]

    @pl.when(k != upper_ref[0])
    def _():
        out_ref[...] = other_ref[...]


def join_halves(mine, other):
    rows, half = mine.shape
    fixed = lambda: pl.BlockSpec((rows, half), lambda k, upper_ref: (0, 0))
    return pl.pallas_call(
        join_kernel,
        grid_spec=pltpu.PrefetchScalarGridSpec(
            num_scalar_prefetch=1,
            grid=(2,),
            in_specs=[fixed(), fixed()],
            out_specs=pl.BlockSpec((rows, half), lambda k, upper_ref: (0, k)),
        ),
        out_shape=jax.ShapeDtypeStruct((rows, 2 * half), f32),
        compiler_params=pltpu.CompilerParams(vmem_limit_bytes=24 * 2**20, dimension_semantics=("arbitrary",)),
        cost_estimate=pl.CostEstimate(flops=0, bytes_accessed=rows * half * 16, transcendentals=0),
        name="join_halves",
    )((lax.axis_index("rows") % 2).astype(jnp.int32)[None], mine, other)


def sum_grad(left, right, wire):
    n = lax.axis_size("rows")
    waits = yield
    left = after(left, waits)
    if n != 4:
        return lax.psum(dot_tokens(left, right), "rows")
    core = [(0, 1), (1, 0), (2, 3), (3, 2)]
    chip = [(0, 2), (2, 0), (1, 3), (3, 1)]
    low, high = right
    send = dot_tokens(left, high)
    other = lax.ppermute(send, "rows", core)
    waits = yield send, other
    pair = (dot_tokens(after(left, send), low) + after(other, waits)).astype(wire)
    other = lax.ppermute(pair, "rows", chip)
    waits = yield pair, other
    total = pair.astype(f32) + after(other, waits).astype(f32)
    other = lax.ppermute(total, "rows", core)
    waits = yield total, other
    return join_halves(total, after(other, waits))


def core_halves(x):
    if lax.axis_size("rows") != 4:
        return x
    half = x.shape[1] // 2
    upper = lax.axis_index("rows") % 2
    part = lambda which: lax.dynamic_slice_in_dim(x, which * half, half, 1)
    return part(upper), part(1 - upper)


def place_norm_kernel(n_seq, count, owners_ref, begins_ref, mod_ref, *refs):
    blocks, (xmod_ref, normed_ref, held) = refs[:count], refs[-3:]
    rows, width = xmod_ref.shape
    step = 2 * CHUNK if rows % (2 * CHUNK) == 0 else rows
    k = pl.program_id(0)
    base = owners_ref[k] * rows

    def hold(block_ref):
        held[...] = block_ref[...]

    for i in range(count):
        pl.when(k == i)(functools.partial(hold, blocks[i]))
    shift, scale = mod_ref[0:1, :], mod_ref[1:2, :]
    gain = mod_ref[3 * n_seq : 3 * n_seq + 1, :]
    for start in range(0, rows, step):
        here = slice(start, start + step)
        wide = held[here, :].astype(f32)
        centred = wide - jnp.sum(wide, axis=1, keepdims=True) * (1.0 / width)
        square = jnp.sum(centred * centred, axis=1, keepdims=True) * (1.0 / width)
        normed = centred * lax.rsqrt(square + EPSILON)
        token = base + start + lax.broadcasted_iota(jnp.int32, (step, 1), 0)
        add, by = shift, gain * (1.0 + scale)
        for s in range(1, n_seq):
            later = token >= begins_ref[0, s]
            add = jnp.where(later, mod_ref[3 * s : 3 * s + 1, :], add)
            by = jnp.where(later, gain * (1.0 + mod_ref[3 * s + 1 : 3 * s + 2, :]), by)
        xmod_ref[here, :] = (normed * by + add).astype(bf16)
        normed_ref[here, :] = normed.astype(bf16)


def place_gate_kernel(n_seq, count, owners_ref, begins_ref, mod_ref, *refs):
    blocks, (gated_ref, plain_ref) = refs[:count], refs[-2:]
    rows = gated_ref.shape[0]
    step = CHUNK if rows % CHUNK == 0 else rows
    k = pl.program_id(0)
    base = owners_ref[k] * rows

    def fill(block_ref):
        def part(p, carry):
            here = pl.ds(pl.multiple_of(p * step, step), step)
            low = block_ref[here, :]
            token = base + p * step + lax.broadcasted_iota(jnp.int32, (step, 1), 0)
            gate = mod_ref[2:3, :]
            for s in range(1, n_seq):
                gate = jnp.where(token >= begins_ref[0, s], mod_ref[3 * s + 2 : 3 * s + 3, :], gate)
            gated_ref[here, :] = (low.astype(f32) * gate).astype(bf16)
            plain_ref[here, :] = low
            return carry

        lax.fori_loop(0, rows // step, part, 0)

    for i in range(count):
        pl.when(k == i)(functools.partial(fill, blocks[i]))


def place(kernel, blocks, begins, mod, name, total, scratch=False, into=()):
    owners = jnp.stack([owner for owner, _ in blocks]).astype(jnp.int32)
    parts = [block for _, block in blocks]
    rows, width = parts[0].shape
    count = len(parts)
    whole = jax.ShapeDtypeStruct((total, width), bf16)
    held = [pl.BlockSpec(memory_space=pl.ANY)] * len(into)
    out = lambda: pl.BlockSpec((rows, width), lambda k, owners_ref, begins_ref: (owners_ref[k], 0))
    fixed = lambda shape: pl.BlockSpec(shape, lambda k, owners_ref, begins_ref: (0, 0))
    return pl.pallas_call(
        functools.partial(kernel, begins.shape[1], count),
        grid_spec=pltpu.PrefetchScalarGridSpec(
            num_scalar_prefetch=2,
            grid=(count,),
            in_specs=[fixed(mod.shape)] + [fixed((rows, width))] * count + held,
            out_specs=[out(), out()],
            scratch_shapes=[pltpu.VMEM((rows, width), bf16)] if scratch else [],
        ),
        out_shape=[whole, whole],
        input_output_aliases={3 + count + k: k for k in range(len(into))},
        compiler_params=pltpu.CompilerParams(vmem_limit_bytes=28 * 2**20, dimension_semantics=("arbitrary",)),
        cost_estimate=pl.CostEstimate(
            flops=count * rows * width * 20, bytes_accessed=count * rows * width * 6, transcendentals=0
        ),
        name=name,
    )(owners, begins, mod, *parts, *into)


def own_columns(x, part, *others):
    count = x.shape[1] // part

    def kernel(index_ref, x_ref, *refs):
        for p in range(count):

            @pl.when(index_ref[0] == p)
            def _():
                refs[-1][...] = x_ref[:, p * part : (p + 1) * part]

    return pl.pallas_call(
        kernel,
        in_specs=[pl.BlockSpec(memory_space=pltpu.SMEM), pl.BlockSpec(memory_space=pltpu.VMEM)]
        + [pl.BlockSpec(memory_space=pl.ANY)] * len(others),
        out_specs=pl.BlockSpec(memory_space=pltpu.VMEM),
        out_shape=jax.ShapeDtypeStruct((x.shape[0], part), x.dtype),
        name="own_columns",
    )(lax.axis_index("chan").astype(jnp.int32)[None], x, *others)


def sums_kernel(n_seq, begins_ref, share_ref, normed_ref, up_ref, branch_ref, out_ref):
    rows, width = share_ref.shape
    k = pl.program_id(0)

    @pl.when(k == 0)
    def _():
        out_ref[...] = jnp.zeros(out_ref.shape, f32)

    lanes = 2 * LANES if width % (2 * LANES) == 0 else width
    token = k * rows + lax.broadcasted_iota(jnp.int32, (rows, 1), 0)
    for at in range(0, width, lanes):
        cols = slice(at, at + lanes)
        share = share_ref[:, cols].astype(f32)
        terms = [share, share * normed_ref[:, cols].astype(f32)]
        terms.append(up_ref[:, cols].astype(f32) * branch_ref[:, cols].astype(f32))
        for j, term in enumerate(terms):
            rest = jnp.sum(term, axis=0, keepdims=True)
            for s in range(n_seq - 1, 0, -1):
                later = jnp.sum(jnp.where(token >= begins_ref[0, s], term, 0.0), axis=0, keepdims=True)
                at_row = j * n_seq + s
                mine = later if s == n_seq - 1 else later - after_it
                out_ref[at_row : at_row + 1, cols] += mine
                after_it = later
            out_ref[j * n_seq : j * n_seq + 1, cols] += rest - (after_it if n_seq > 1 else 0.0)


def token_sums(share, normed, up, branch, begins):
    tokens, width = share.shape
    n_seq = begins.shape[1]
    rows = LANES
    spec = lambda: pl.BlockSpec((rows, width), lambda k: (k, 0))
    height = 3 * n_seq + (-3 * n_seq % 8)
    return pl.pallas_call(
        functools.partial(sums_kernel, n_seq),
        grid=(tokens // rows,),
        in_specs=[pl.BlockSpec(memory_space=pltpu.SMEM), spec(), spec(), spec(), spec()],
        out_specs=pl.BlockSpec((height, width), lambda k: (0, 0)),
        out_shape=jax.ShapeDtypeStruct((height, width), f32),
        compiler_params=pltpu.CompilerParams(vmem_limit_bytes=32 * 2**20, dimension_semantics=("arbitrary",)),
        cost_estimate=pl.CostEstimate(flops=tokens * width * 12, bytes_accessed=tokens * width * 8, transcendentals=0),
        name="token_sums",
    )(begins, share, normed, up, branch)


def local(
    activations,
    condition,
    seq_lengths,
    w_ada,
    b_ada,
    norm_gain,
    w_in_x,
    w_in_z,
    conv_weight,
    conv_bias,
    w_xproj,
    w_dt,
    dt_bias,
    a_log,
    d_skip,
    w_out,
    grad_out,
):
    ring = Ring()
    tok_loc, width = activations.shape
    low_rank = w_dt.shape[0]
    states = a_log.shape[1]
    channels = a_log.shape[0]
    conv_taps = conv_weight.shape[1]
    tok_count = tok_loc * ring.n
    tok_start = lax.axis_index("chan") * tok_loc
    act_ring = Steps(ring.blocks(activations))
    act_in = [act_ring.go()]
    cond_act = jax.nn.silu(condition.astype(f32)).astype(bf16)
    modulation = (
        jnp.einsum("si,kji->skj", cond_act, w_ada, preferred_element_type=f32) + b_ada[None]
    )
    part_width = norm_gain.shape[0]
    seq_count = seq_lengths.shape[1]
    packed = jnp.concatenate([modulation.reshape(3 * seq_count, part_width), norm_gain[None]], axis=0)
    packing = Steps(small_gather(packed, "chan"))
    packing.go()
    act_in.append(act_ring.go())
    packing.go(act_in[0])
    seq_lengths, conv_weight, conv_bias, w_dt, dt_bias, a_log, d_skip = after(
        (seq_lengths, conv_weight, conv_bias, w_dt, dt_bias, a_log, d_skip), act_in[0]
    )
    w_in = after(jnp.concatenate([w_in_x, w_in_z], axis=0), act_in[0])
    seq_lens = seq_lengths[0]
    seq_ends = jnp.cumsum(seq_lens)
    begins = seq_ends - seq_lens
    position = jnp.arange(tok_count, dtype=jnp.int32)
    member = (position[:, None] >= begins[None, :]) & (position[:, None] < seq_ends[None, :])
    onehot = member.astype(f32)
    in_seq = jnp.sum(onehot * (position[:, None] - begins[None, :]).astype(f32), axis=1)
    per_token = lambda rows, hot: sum(hot[:, s : s + 1] * rows[s][None] for s in range(seq_count))
    a_neg = -jnp.exp(a_log).T
    act_in.append(act_ring.go(w_in, in_seq))
    packing.go(act_in[1])
    far_wait = packing.arrived
    packed = packing.end().transpose(1, 0, 2).reshape(3 * seq_count + 1, width)
    packed = jnp.pad(packed, ((0, -packed.shape[0] % 8), (0, 0)))
    mod_full = packed[: 3 * seq_count].reshape(seq_count, 3, width)
    gain_full = packed[3 * seq_count]
    act_ring.go(far_wait)
    act_blocks = act_ring.end()
    soon = 5 if len(act_blocks) == 8 else 0
    norm = functools.partial(place, place_norm_kernel, begins=begins[None], mod=packed, total=tok_count, scratch=True)
    so_far = tuple(norm(act_blocks[:soon], name="place_norm_soon")) if soon else ()
    up_ring = Steps(ring.blocks(after(grad_out, act_in[-1])))
    up_in = [up_ring.go()]
    xmod, normed = norm(act_blocks[soon:], name="place_norm", into=so_far)
    inner = dot_across(xmod, w_in)
    x_inner = inner[:, :channels]
    xmod_halves = core_halves(after(xmod, inner))
    conv_pre = jnp.zeros_like(x_inner) + conv_bias[None, :]
    for tap_index in range(conv_taps):
        lag = conv_taps - 1 - tap_index
        valid = (in_seq >= lag).astype(f32)[:, None]
        conv_pre = conv_pre + conv_weight[:, tap_index][None, :] * delay_rows(x_inner, lag) * valid
    act_low = jax.nn.silu(conv_pre).astype(bf16)
    up_in.append(up_ring.go())
    adding = Steps(sum_chan(low_dot(act_low, w_xproj), PROJ_WIRE))
    adding.go(up_in[0])
    adding.go()
    adding.go(up_in[1])
    up_in.append(up_ring.go())
    adding.go()
    adding.go(up_in[2])
    up_ring.go()
    proj = adding.end()
    dt_low = proj[:, :low_rank].astype(bf16)
    d_branch_all, whole_up = place(
        place_gate_kernel, up_ring.end(), begins[None], packed, "place_gate", tok_count
    )
    d_gated = dot_across(d_branch_all, w_out)
    gated, d_z_low, d_dt_low, d_act, d_log, bias_skip, proj_terms = scans(
        proj, act_low, inner, d_gated, w_dt, dt_bias, a_neg, d_skip, begins[None]
    )
    adding = Steps(sum_chan(proj_terms, DPROJ_WIRE))
    branch_part = lax.optimization_barrier(low_dot(gated, w_out).astype(bf16))
    branch_sum = Scatter(ring, branch_part)
    adding.go()
    ring.hop([branch_sum])
    out_rows = Steps(sum_grad(gated, core_halves(d_branch_all), bf16))
    in_z_rows = Steps(sum_grad(d_z_low, xmod_halves, bf16))
    out_rows.go(branch_part)
    arrived = adding.arrived
    adding.go(out_rows.sent)
    in_z_rows.go(arrived)
    arrived = adding.arrived
    adding.go(in_z_rows.sent, branch_sum.arrived)
    flight = ring.launch([branch_sum])
    out_rows.go(arrived)
    arrived = adding.arrived
    adding.go(out_rows.sent)
    in_z_rows.go(arrived)
    adding.go(in_z_rows.sent)
    adding.go()
    d_proj = adding.end().astype(bf16)
    ring.land(flight, adding.arrived)
    d_act = d_act + dot_across(d_proj, w_xproj)
    d_conv = d_act * silu_slope(conv_pre)
    d_x_inner = jnp.zeros_like(d_conv)
    tap_grads = []
    for tap_index in range(conv_taps):
        lag = conv_taps - 1 - tap_index
        valid = (in_seq >= lag).astype(f32)[:, None]
        masked = d_conv * valid
        tap_grads.append(jnp.sum(masked * delay_rows(x_inner, lag), axis=0))
        d_x_inner = d_x_inner + conv_weight[:, tap_index][None, :] * advance_rows(masked, lag)
    d_x_low = d_x_inner.astype(bf16)
    in_x_rows = Steps(sum_grad(d_x_low, xmod_halves, bf16))
    d_xmod_part = (low_dot(d_x_low, w_in_x) + low_dot(d_z_low, w_in_z)).astype(bf16)
    d_xmod_part = lax.optimization_barrier(d_xmod_part)
    in_x_rows.go(d_xmod_part)
    d_xmod_sum = Scatter(ring, d_xmod_part)
    both = [branch_sum, d_xmod_sum]
    ring.hop(both)
    first = d_xmod_sum.arrived
    ring.hop(both)
    share = after(d_xmod_part, first)
    summing = Steps(small_sum(token_sums(share, normed, whole_up, branch_part, begins[None]), "chan"))
    summing.go()
    in_x_rows.go(first)
    out_rows.go(first)
    rows_now = jnp.concatenate([modulation[:, 1], cond_act.astype(f32).reshape(-1, part_width)], axis=0)
    knowing = Steps(small_gather(rows_now, "rows"))
    knowing.go(first)
    d_proj = after(d_proj, first)
    small = jnp.concatenate(
        [
            dot_tokens(d_proj, act_low),
            dot_tokens(dt_low, d_dt_low),
            d_log * a_neg,
            jnp.stack(tap_grads),
            jnp.sum(d_conv, axis=0)[None],
            bias_skip[0:1],
            bias_skip[8:9],
        ],
        axis=0,
    )
    small = jnp.pad(small, ((0, -small.shape[0] % 16), (0, 0)))
    small_rows = Steps(small_sum(small, "rows"))
    small_rows.go()
    second = d_xmod_sum.arrived
    ring.hop(both, summing.sent, in_x_rows.sent, out_rows.sent, small_rows.sent)
    summing.go(second)
    in_z_rows.go(second)
    small_rows.go(second)
    knowing.go(second)
    grad_w_out = out_rows.end(second)
    third = d_xmod_sum.arrived
    ring.hop(both, summing.sent, in_z_rows.sent, small_rows.sent, grad_w_out)
    summing.go(third)
    known = knowing.end(third)
    scale_all = known[:, :seq_count].reshape(-1, part_width)
    cond_all = jnp.tile(known[:, seq_count:].reshape(-1, width).astype(bf16), (3, 1))
    in_x_rows.go(third)
    grad_w_in_z = in_z_rows.end(third)
    grad_w_in_x = in_x_rows.end()
    while d_xmod_sum.result is None:
        ring.hop(both)
    last = d_xmod_sum.arrived
    branch, d_xmod = branch_sum.result, d_xmod_sum.result
    sums = own_columns(summing.end(last), part_width, grad_w_in_z, grad_w_in_x)
    reaching = Steps(small_gather(sums, "rows"))
    reaching.go()
    reaching.go()
    reach = reaching.end()
    small = small_rows.end(last)
    onehot_loc = lax.dynamic_slice_in_dim(onehot, tok_start, tok_loc, 0)
    counts = [w_xproj.shape[1], low_rank, states, conv_taps, 1, 1, 1]
    pieces, at = [], 0
    for count in counts:
        pieces.append(small[at : at + count])
        at += count
    by_shift, by_scale, by_gate = [
        reach[:, k * seq_count : (k + 1) * seq_count].reshape(-1, part_width) for k in range(3)
    ]
    grad_gain = jnp.sum(by_scale * (1.0 + scale_all), axis=0)
    d_mod_all = jnp.concatenate([by_shift, by_scale * norm_gain[None], by_gate], axis=1)
    grad_b_ada = jnp.sum(d_mod_all, axis=0).reshape(3, part_width)
    high = d_mod_all.astype(bf16)
    rest = d_mod_all - high.astype(f32)
    middle = rest.astype(bf16)
    split = jnp.concatenate([high, middle, (rest - middle.astype(f32)).astype(bf16)], axis=0)
    grad_w_ada = dot_tokens(split, cond_all).reshape(3, part_width, width)
    block_out = (activations.astype(f32) + per_token(mod_full[:, 2], onehot_loc) * branch).astype(bf16)
    wide_loc = activations.astype(f32)
    centred_loc = wide_loc - jnp.mean(wide_loc, axis=1, keepdims=True)
    inv_std_loc = lax.rsqrt(jnp.mean(centred_loc * centred_loc, axis=1, keepdims=True) + EPSILON)
    normed_loc = centred_loc * inv_std_loc
    scale_loc = per_token(mod_full[:, 1], onehot_loc)
    d_normed = d_xmod * (1.0 + scale_loc) * gain_full[None, :]
    mean_first = jnp.mean(d_normed, axis=1, keepdims=True)
    mean_second = jnp.mean(d_normed * normed_loc, axis=1, keepdims=True)
    grad_input = (
        inv_std_loc * (d_normed - mean_first - normed_loc * mean_second) + grad_out.astype(f32)
    ).astype(bf16)
    return (
        block_out,
        grad_input,
        grad_w_ada,
        grad_b_ada,
        grad_gain,
        grad_w_in_x,
        grad_w_in_z,
        pieces[3].T,
        pieces[4][0],
        pieces[0].T,
        pieces[1],
        pieces[5][0],
        pieces[2].T,
        pieces[6][0],
        grad_w_out,
    )


PROJ_WIRE = bf16
DPROJ_WIRE = bf16


def solution(mesh):
    return jax.shard_map(
        local,
        mesh=mesh,
        in_specs=(
            P(("rows", "chan"), None),
            P("rows", None),
            P("rows", None),
            P(None, "chan", None),
            P(None, "chan"),
            P("chan"),
            P("chan", None),
            P("chan", None),
            P("chan", None),
            P("chan"),
            P("chan", None),
            P(None, "chan"),
            P("chan"),
            P("chan", None),
            P("chan"),
            P("chan", None),
            P(("rows", "chan"), None),
        ),
        out_specs=(
            P(("rows", "chan"), None),
            P(("rows", "chan"), None),
            P(None, "chan", None),
            P(None, "chan"),
            P("chan"),
            P("chan", None),
            P("chan", None),
            P("chan", None),
            P("chan"),
            P("chan", None),
            P(None, "chan"),
            P("chan"),
            P("chan", None),
            P("chan"),
            P("chan", None),
        ),
        check_vma=False,
    )
```

```python
import functools
import math

import jax
import jax.numpy as jnp
from jax import lax
from jax.experimental import pallas as pl
from jax.experimental.pallas import tpu as pltpu
from jax.sharding import PartitionSpec as P

CHUNK = 16
LANES = 128
LOG2E = math.log2(math.e)
f32 = jnp.float32
bf16 = jnp.bfloat16


def scan_kernel(
    n_seq,
    states,
    begins_ref,
    proj_ref,
    act_ref,
    z_ref,
    d_gated_ref,
    w_dt_ref,
    dt_bias_ref,
    an_ref,
    skip_ref,
    gated_ref,
    d_z_ref,
    d_dt_ref,
    d_act_ref,
    ga_ref,
    sums_ref,
    terms_ref,
    b_all,
    c_all,
    pf_all,
    db_all,
    b_blk_all,
    c_blk_all,
    delta_all,
    step_all,
    dm_all,
    exp_all,
):
    tokens, channels = act_ref.shape
    n_pairs = tokens // (2 * CHUNK)
    wide = CHUNK * states
    low_rank = proj_ref.shape[1] - 2 * states
    an = an_ref[...]
    a2 = an * LOG2E
    dot = functools.partial(jnp.dot, preferred_element_type=f32)
    across = functools.partial(
        lax.dot_general, dimension_numbers=(((1,), (1,)), ((), ())), preferred_element_type=f32
    )

    def diagonal(rows):
        r = lax.broadcasted_iota(jnp.int32, (rows, wide), 0) % CHUNK
        return (r == lax.broadcasted_iota(jnp.int32, (rows, wide), 1) // states).astype(f32)

    diag = diagonal(CHUNK)
    half = states // 2
    spot = lax.broadcasted_iota(jnp.int32, (CHUNK, CHUNK * half), 1) // half
    ones_blk = (lax.broadcasted_iota(jnp.int32, (CHUNK, CHUNK * half), 0) == spot).astype(bf16)
    m = lax.broadcasted_iota(jnp.int32, (low_rank + 2 * states, wide), 0)
    q = lax.broadcasted_iota(jnp.int32, (low_rank + 2 * states, wide), 1) % states
    pick_b = (m == low_rank + q).astype(bf16)
    pick_c = (m == low_rank + states + q).astype(bf16)
    tile = pl.program_id(0)

    @pl.when(tile == 0)
    def _():
        many = diagonal(LANES)

        def spread(k, carry):
            base = pl.multiple_of(k * LANES, LANES)
            proj = proj_ref[pl.ds(base, LANES), :]
            low = proj.astype(bf16)
            b_blk_all[pl.ds(base, LANES), :] = (dot(low, pick_b) * many).astype(bf16)
            c_blk_all[pl.ds(base, LANES), :] = (dot(low, pick_c) * many).astype(bf16)
            turned = proj.astype(f32).T
            bt = turned[low_rank : low_rank + states]
            ct = turned[low_rank + states :]
            for i in range(LANES):
                at = pl.ds(pl.multiple_of(base * states + i * states, states), states)
                b_all[at, :] = jnp.broadcast_to(bt[:, i : i + 1], (states, channels))
                c_all[at, :] = jnp.broadcast_to(ct[:, i : i + 1], (states, channels))
            return carry

        lax.fori_loop(0, tokens // LANES, spread, 0)

    def prepare(k, carry):
        here = pl.ds(pl.multiple_of(k * LANES, LANES), LANES)
        dt_raw = dot(proj_ref[here, :].astype(bf16), w_dt_ref[...]) + dt_bias_ref[...]
        delta = jnp.maximum(dt_raw, 0.0) + jnp.log1p(jnp.exp(-jnp.abs(dt_raw)))
        delta_all[here, :] = delta
        step_all[here, :] = delta * act_ref[here, :].astype(f32)
        z = z_ref[here, :]
        dm_all[here, :] = d_gated_ref[here, :] * (z * jax.nn.sigmoid(z))
        return carry

    lax.fori_loop(0, tokens // LANES, prepare, 0, unroll=5 if tokens % (5 * LANES) == 0 else 1)

    def keep_at(t):
        keep = None
        for s in range(1, n_seq):
            k = jnp.where(begins_ref[0, s] == t, 0.0, 1.0).astype(f32)
            keep = k if keep is None else keep * k
        return keep

    def sweep(body, cut, carry):
        plain, masked = functools.partial(body, False), functools.partial(body, True)
        if n_seq == 1:
            return lax.fori_loop(0, n_pairs, plain, carry)
        if n_seq > 2:
            return lax.fori_loop(0, n_pairs, masked, carry)
        carry = lax.fori_loop(0, cut, plain, carry)
        carry = masked(cut, carry)
        return lax.fori_loop(cut + 1, n_pairs, plain, carry)

    def row(ref, t):
        return ref[pl.ds(t, 1), :]

    def forward(masked, pair, carry):
        sf, g = carry
        base = pl.multiple_of(pair * 2 * CHUNK, 2 * CHUNK)
        for i in range(2 * CHUNK):
            at = pl.ds(pl.multiple_of(base * states + i * states, states), states)
            decay = jnp.exp2(row(delta_all, base + i) * a2)
            if masked:
                keep = keep_at(base + i)
                sf = sf * keep
                g = g * keep
            pf = decay * sf
            sf = pf + row(step_all, base + i) * b_all[at, :]
            db = row(dm_all, base + i) * c_all[at, :] + g
            g = decay * db
            pf_all[at, :] = pf
            db_all[at, :] = db
        return sf, g

    zero = jnp.zeros((states, channels), f32)
    first = begins_ref[0, n_seq - 1]
    sweep(forward, first // (2 * CHUNK), (zero, zero))

    def backward(masked, k, carry):
        sb, g, ga = carry
        base = pl.multiple_of((n_pairs - 1 - k) * 2 * CHUNK, 2 * CHUNK)
        for i in range(2 * CHUNK - 1, -1, -1):
            at = pl.ds(pl.multiple_of(base * states + i * states, states), states)
            delta = row(delta_all, base + i)
            decay = jnp.exp2(delta * a2)
            drive = row(step_all, base + i) * b_all[at, :]
            if masked:
                keep = keep_at(base + i + 1)
                sb = sb * keep
                g = g * keep
            pb = decay * sb
            sb = pb + drive
            df = row(dm_all, base + i) * c_all[at, :] + g
            g = decay * df
            pf = pf_all[at, :]
            db = db_all[at, :]
            d_expo = df * pf + db * pb
            ga = ga + d_expo * delta
            pf_all[at, :] = pf + drive + sb
            db_all[at, :] = df + db
            by_n = d_expo * an
            exp_all[pl.ds(pl.multiple_of(base * half + i * half, half), half), :] = by_n[:half] + by_n[half:]
        return sb, g, ga

    cut = n_pairs - 1 - (first - 1) // (2 * CHUNK)
    _, _, ga = sweep(backward, cut, (zero, zero, zero))
    ga_ref[...] = ga

    def finish(k, carry):
        by_bias, by_skip = carry
        base = pl.multiple_of(k * LANES, LANES)
        here = pl.ds(base, LANES)
        low = proj_ref[here, :].astype(bf16)
        act = act_ref[here, :].astype(f32)
        d_mixed = dm_all[here, :]
        dm_low = d_mixed.astype(bf16)
        step_low = step_all[here, :].astype(bf16)
        y, through, expo, dcm, dbm = [], [], [], [], []
        for c in range(LANES // CHUNK):
            at = pl.ds(pl.multiple_of(base * states + c * wide, wide), wide)
            mine = pl.ds(pl.multiple_of(base + c * CHUNK, CHUNK), CHUNK)
            span = slice(c * CHUNK, (c + 1) * CHUNK)
            both = pf_all[at, :].astype(bf16)
            drv = db_all[at, :].astype(bf16)
            y.append(dot(c_blk_all[mine, :], both))
            through.append(dot(b_blk_all[mine, :], drv))
            at = pl.ds(pl.multiple_of(base * half + c * CHUNK * half, CHUNK * half), CHUNK * half)
            expo.append(dot(ones_blk, exp_all[at, :].astype(bf16)))
            dcm.append((across(dm_low[span], both) * diag).astype(bf16))
            dbm.append((across(step_low[span], drv) * diag).astype(bf16))
        whole = lambda parts: jnp.concatenate(parts, axis=0)
        skip = skip_ref[...]
        z = z_ref[here, :]
        sigma = jax.nn.sigmoid(z)
        mixed = whole(y) + skip * act
        gated_ref[here, :] = (mixed * (z * sigma)).astype(bf16)
        d_z_ref[here, :] = (d_gated_ref[here, :] * mixed * (sigma * (1.0 + z * (1.0 - sigma)))).astype(bf16)
        via = whole(through)
        d_act_ref[here, :] = d_mixed * skip + via * delta_all[here, :]
        dt_raw = dot(low, w_dt_ref[...]) + dt_bias_ref[...]
        d_dt_raw = (whole(expo) + via * act) * jax.nn.sigmoid(dt_raw)
        d_dt = d_dt_raw.astype(bf16)
        d_dt_ref[here, :] = d_dt
        terms = across(d_dt, w_dt_ref[...]) + across(whole(dbm), pick_b) + across(whole(dcm), pick_c)

        @pl.when(tile == 0)
        def _():
            terms_ref[here, :] = terms

        @pl.when(tile != 0)
        def _():
            terms_ref[here, :] += terms

        total = lambda v: jnp.sum(v, axis=0, keepdims=True)
        return by_bias + total(d_dt_raw), by_skip + total(d_mixed * act)

    none = jnp.zeros((1, channels), f32)
    by_bias, by_skip = lax.fori_loop(0, tokens // LANES, finish, (none, none))
    sums_ref[0:8, :] = jnp.broadcast_to(by_bias, (8, channels))
    sums_ref[8:16, :] = jnp.broadcast_to(by_skip, (8, channels))


def scans(proj, act_low, z_inner, d_gated, w_dt, dt_bias, a_neg, d_skip, begins):
    tokens, channels = act_low.shape
    states = a_neg.shape[0]
    tile = LANES if channels % LANES == 0 else channels
    wide = CHUNK * states
    w_dt = jnp.pad(w_dt, ((0, 2 * states), (0, 0)))
    col = lambda: pl.BlockSpec((tokens, tile), lambda j: (0, j))
    rows = lambda n: pl.BlockSpec((n, tile), lambda j: (0, j))
    full = lambda: pl.BlockSpec(proj.shape, lambda j: (0, 0))
    if z_inner.shape[1] % tile or tile % LANES:
        z_inner = z_inner[:, -channels:]
    ahead = (z_inner.shape[1] - channels) // tile
    z_col = pl.BlockSpec((tokens, tile), lambda j: (0, ahead + j))
    sds = jax.ShapeDtypeStruct
    return pl.pallas_call(
        functools.partial(scan_kernel, begins.shape[1], states),
        grid=(channels // tile,),
        in_specs=[
            pl.BlockSpec(memory_space=pltpu.SMEM),
            full(),
            col(),
            z_col,
            col(),
            rows(w_dt.shape[0]),
            rows(1),
            rows(states),
            rows(1),
        ],
        out_specs=[col(), col(), col(), col(), rows(states), rows(16), full()],
        out_shape=[
            sds((tokens, channels), bf16),
            sds((tokens, channels), bf16),
            sds((tokens, channels), bf16),
            sds((tokens, channels), f32),
            sds((states, channels), f32),
            sds((16, channels), f32),
            sds(proj.shape, f32),
        ],
        scratch_shapes=[pltpu.VMEM((tokens * states, tile), f32)] * 4
        + [pltpu.VMEM((tokens, wide), bf16)] * 2
        + [pltpu.VMEM((tokens, tile), f32)] * 3
        + [pltpu.VMEM((tokens * states // 2, tile), f32)],
        compiler_params=pltpu.CompilerParams(vmem_limit_bytes=62 * 2**20, dimension_semantics=("arbitrary",)),
        cost_estimate=pl.CostEstimate(
            flops=tokens * channels * states * 60,
            bytes_accessed=tokens * channels * 24,
            transcendentals=2 * tokens * channels * states,
        ),
        name="scan_all",
    )(begins, proj, act_low, z_inner, d_gated, w_dt, dt_bias[None], a_neg, d_skip[None])


EPSILON = 1e-06
HIGHEST = lax.Precision.HIGHEST


def low_dot(left, right):
    return jnp.dot(left, right, preferred_element_type=f32)


def dot_across(left, right):
    return lax.dot_general(left, right, (((1,), (1,)), ((), ())), preferred_element_type=f32)


def dot_tokens(left, right):
    return lax.dot_general(left, right, (((0,), (0,)), ((), ())), preferred_element_type=f32)


def delay_rows(operand, lag):
    if lag == 0:
        return operand
    padding = jnp.zeros((lag,) + operand.shape[1:], operand.dtype)
    return jnp.concatenate([padding, operand[:-lag]], axis=0)


def advance_rows(operand, lag):
    if lag == 0:
        return operand
    padding = jnp.zeros((lag,) + operand.shape[1:], operand.dtype)
    return jnp.concatenate([operand[lag:], padding], axis=0)


def after(x, *others):
    others = tuple(jax.tree.leaves(others))
    return lax.optimization_barrier((x, others))[0] if others else x


class Steps:
    def __init__(self, steps):
        self.steps = steps
        self.result = self.sent = self.arrived = None
        next(steps)

    def go(self, *others):
        if self.result is None:
            try:
                self.sent, self.arrived = self.steps.send(others)
            except StopIteration as stop:
                self.result = stop.value
        return self.arrived

    def end(self, *others):
        while self.result is None:
            self.go(*others)
        return self.result


def silu_slope(operand):
    squash = jax.nn.sigmoid(operand)
    return squash * (1.0 + operand * (1.0 - squash))


class Ring:
    def __init__(self):
        self.n = lax.axis_size("chan")
        self.down = 4 if self.n % 8 == 0 else 1
        self.across = self.n // self.down
        order = [self.at(p) for p in range(self.n)]
        self.right = [(order[k], order[(k + 1) % self.n]) for k in range(self.n)]
        self.left = [(b, a) for a, b in self.right]
        index = lax.axis_index("chan")
        i, j = index // self.across, index % self.across
        back = self.down - 1 - i
        step = jnp.where(back % 2 == 0, j - 1, self.across - 1 - j)
        self.place = jnp.where(j == 0, i, self.down + back * (self.across - 1) + step)

    def at(self, p):
        if self.down == 1:
            return p
        back, step = (p - self.down) // (self.across - 1), (p - self.down) % (self.across - 1)
        if isinstance(p, int):
            column = 1 + step if back % 2 == 0 else self.across - 1 - step
            return p * self.across if p < self.down else (self.down - 1 - back) * self.across + column
        column = jnp.where(back % 2 == 0, 1 + step, self.across - 1 - step)
        return jnp.where(p < self.down, p * self.across, (self.down - 1 - back) * self.across + column)

    def owner(self, away):
        p = self.place + away
        if away > 0:
            p = jnp.where(p >= self.n, p - self.n, p)
        elif away < 0:
            p = jnp.where(p < 0, p + self.n, p)
        return self.at(p)

    def go_right(self, x):
        return lax.ppermute(x, "chan", self.right)

    def go_left(self, x):
        return lax.ppermute(x, "chan", self.left)

    def blocks(self, x):
        half = self.n // 2
        cut = x.shape[0] // 2
        pair = x, x
        found = [(self.owner(0), x)]
        waits = yield
        for step in range(1, half):
            sent = after(pair, waits)
            pair = self.go_right(sent[0]), self.go_left(sent[1])
            found += [(self.owner(-step), pair[0]), (self.owner(step), pair[1])]
            waits = yield sent, pair
        sent = after((pair[0][:cut], pair[1][cut:]), waits)
        pair = self.go_right(sent[0]), self.go_left(sent[1])
        yield sent, pair
        return found + [(self.owner(half), jnp.concatenate(pair, axis=0))]

    def scatter(self, part):
        half = self.n // 2
        rows = part.shape[0] // self.n
        cut = rows // 2
        mine = lambda away: lax.dynamic_slice_in_dim(part, self.owner(away) * rows, rows, 0)
        wide = lambda v: v.astype(f32)
        far = mine(half)
        right, left = yield far[:cut], far[cut:]
        for away in range(half - 1, 0, -1):
            ahead, behind = wide(mine(away)), wide(mine(-away))
            if away == half - 1:
                ahead = jnp.concatenate([ahead[:cut] + wide(right), ahead[cut:]], axis=0)
                behind = jnp.concatenate([behind[:cut], behind[cut:] + wide(left)], axis=0)
            else:
                ahead, behind = ahead + wide(right), behind + wide(left)
            right, left = yield ahead.astype(bf16), behind.astype(bf16)
        return wide(mine(0)) + wide(right) + wide(left)

    def hop(self, sums, *others):
        self.land(self.launch(sums, *others))

    def launch(self, sums, *others):
        sums = [one for one in sums if one.result is None]
        if not sums:
            return sums, None
        join = lambda side: jnp.concatenate([one.pair[side] for one in sums], axis=0)
        right, left = lax.optimization_barrier((join(0), join(1), tuple(jax.tree.leaves(others))))[:2]
        return sums, (self.go_right(right), self.go_left(left))

    def land(self, flight, *others):
        sums, pair = flight
        if not sums:
            return
        right, left = lax.optimization_barrier((pair, tuple(jax.tree.leaves(others))))[0]
        at = 0
        for one in sums:
            rows = one.pair[0].shape[0]
            one.take((right[at : at + rows], left[at : at + rows]))
            at += rows


class Scatter:
    def __init__(self, ring, part):
        self.steps = ring.scatter(part)
        self.result, self.arrived = None, None
        self.pair = next(self.steps)

    def take(self, arrived):
        self.arrived = arrived
        try:
            self.pair = self.steps.send(arrived)
        except StopIteration as stop:
            self.result = stop.value


def is_power(n):
    return n & (n - 1) == 0


def bits_of(n):
    return [1 << b for b in range(n.bit_length() - 1)]


def sum_chan(x, wire):
    n = lax.axis_size("chan")
    index = lax.axis_index("chan")
    waits = yield
    if not is_power(n) or x.shape[0] % (16 * n):
        return lax.psum(after(x, waits), "chan")
    perm = lambda b: [(i, i ^ b) for i in range(n)]
    for b in bits_of(n):
        h = x.shape[0] // 2
        upper = (index // b) % 2
        keep = lax.dynamic_slice_in_dim(x, upper * h, h, 0)
        send = lax.dynamic_slice_in_dim(x, (1 - upper) * h, h, 0).astype(wire)
        send = after(send, waits)
        other = lax.ppermute(send, "chan", perm(b))
        waits = yield send, other
        x = keep + other.astype(f32)
    x = x.astype(wire)
    for b in reversed(bits_of(n)):
        upper = (index // b) % 2
        x = after(x, waits)
        other = lax.ppermute(x, "chan", perm(b))
        waits = yield x, other
        x = jnp.concatenate([jnp.where(upper == 0, x, other), jnp.where(upper == 0, other, x)], axis=0)
    return after(x, waits)


def small_gather(x, axis):
    n = lax.axis_size(axis)
    waits = yield
    if not is_power(n) or n > 8:
        return lax.all_gather(after(x, waits), axis, axis=0)
    index = lax.axis_index(axis)
    x = x[None]
    for b in bits_of(n):
        x = after(x, waits)
        other = lax.ppermute(x, axis, [(i, i ^ b) for i in range(n)])
        waits = yield x, other
        other = after(other, waits)
        lower = (index // b) % 2 == 0
        x = jnp.concatenate([jnp.where(lower, x, other), jnp.where(lower, other, x)], axis=0)
    return x


def small_sum(x, axis):
    n = lax.axis_size(axis)
    waits = yield
    if not is_power(n) or n > 8:
        return lax.psum(after(x, waits), axis)
    for b in bits_of(n):
        x = after(x, waits)
        other = lax.ppermute(x, axis, [(i, i ^ b) for i in range(n)])
        waits = yield x, other
        x = x + after(other, waits)
    return x


def join_kernel(upper_ref, mine_ref, other_ref, out_ref):
    k = pl.program_id(0)

    @pl.when(k == upper_ref[0])
    def _():
        out_ref[...] = mine_ref[...]

    @pl.when(k != upper_ref[0])
    def _():
        out_ref[...] = other_ref[...]


def join_halves(mine, other):
    rows, half = mine.shape
    fixed = lambda: pl.BlockSpec((rows, half), lambda k, upper_ref: (0, 0))
    return pl.pallas_call(
        join_kernel,
        grid_spec=pltpu.PrefetchScalarGridSpec(
            num_scalar_prefetch=1,
            grid=(2,),
            in_specs=[fixed(), fixed()],
            out_specs=pl.BlockSpec((rows, half), lambda k, upper_ref: (0, k)),
        ),
        out_shape=jax.ShapeDtypeStruct((rows, 2 * half), f32),
        compiler_params=pltpu.CompilerParams(vmem_limit_bytes=24 * 2**20, dimension_semantics=("arbitrary",)),
        cost_estimate=pl.CostEstimate(flops=0, bytes_accessed=rows * half * 16, transcendentals=0),
        name="join_halves",
    )((lax.axis_index("rows") % 2).astype(jnp.int32)[None], mine, other)


def sum_grad(left, right, wire):
    n = lax.axis_size("rows")
    waits = yield
    left = after(left, waits)
    if n != 4:
        return lax.psum(dot_tokens(left, right), "rows")
    core = [(0, 1), (1, 0), (2, 3), (3, 2)]
    chip = [(0, 2), (2, 0), (1, 3), (3, 1)]
    low, high = right
    send = dot_tokens(left, high)
    other = lax.ppermute(send, "rows", core)
    waits = yield send, other
    pair = (dot_tokens(after(left, send), low) + after(other, waits)).astype(wire)
    other = lax.ppermute(pair, "rows", chip)
    waits = yield pair, other
    total = pair.astype(f32) + after(other, waits).astype(f32)
    other = lax.ppermute(total, "rows", core)
    waits = yield total, other
    return join_halves(total, after(other, waits))


def core_halves(x):
    if lax.axis_size("rows") != 4:
        return x
    half = x.shape[1] // 2
    upper = lax.axis_index("rows") % 2
    part = lambda which: lax.dynamic_slice_in_dim(x, which * half, half, 1)
    return part(upper), part(1 - upper)


def place_norm_kernel(n_seq, count, owners_ref, begins_ref, mod_ref, *refs):
    blocks, (xmod_ref, normed_ref, held) = refs[:count], refs[-3:]
    rows, width = xmod_ref.shape
    step = 2 * CHUNK if rows % (2 * CHUNK) == 0 else rows
    k = pl.program_id(0)
    base = owners_ref[k] * rows

    def hold(block_ref):
        held[...] = block_ref[...]

    for i in range(count):
        pl.when(k == i)(functools.partial(hold, blocks[i]))
    shift, scale = mod_ref[0:1, :], mod_ref[1:2, :]
    gain = mod_ref[3 * n_seq : 3 * n_seq + 1, :]
    for start in range(0, rows, step):
        here = slice(start, start + step)
        wide = held[here, :].astype(f32)
        centred = wide - jnp.sum(wide, axis=1, keepdims=True) * (1.0 / width)
        square = jnp.sum(centred * centred, axis=1, keepdims=True) * (1.0 / width)
        normed = centred * lax.rsqrt(square + EPSILON)
        token = base + start + lax.broadcasted_iota(jnp.int32, (step, 1), 0)
        add, by = shift, gain * (1.0 + scale)
        for s in range(1, n_seq):
            later = token >= begins_ref[0, s]
            add = jnp.where(later, mod_ref[3 * s : 3 * s + 1, :], add)
            by = jnp.where(later, gain * (1.0 + mod_ref[3 * s + 1 : 3 * s + 2, :]), by)
        xmod_ref[here, :] = (normed * by + add).astype(bf16)
        normed_ref[here, :] = normed.astype(bf16)


def place_gate_kernel(n_seq, count, owners_ref, begins_ref, mod_ref, *refs):
    blocks, (gated_ref, plain_ref) = refs[:count], refs[-2:]
    rows = gated_ref.shape[0]
    step = CHUNK if rows % CHUNK == 0 else rows
    k = pl.program_id(0)
    base = owners_ref[k] * rows

    def fill(block_ref):
        def part(p, carry):
            here = pl.ds(pl.multiple_of(p * step, step), step)
            low = block_ref[here, :]
            token = base + p * step + lax.broadcasted_iota(jnp.int32, (step, 1), 0)
            gate = mod_ref[2:3, :]
            for s in range(1, n_seq):
                gate = jnp.where(token >= begins_ref[0, s], mod_ref[3 * s + 2 : 3 * s + 3, :], gate)
            gated_ref[here, :] = (low.astype(f32) * gate).astype(bf16)
            plain_ref[here, :] = low
            return carry

        lax.fori_loop(0, rows // step, part, 0)

    for i in range(count):
        pl.when(k == i)(functools.partial(fill, blocks[i]))


def place(kernel, blocks, begins, mod, name, total, scratch=False, into=()):
    owners = jnp.stack([owner for owner, _ in blocks]).astype(jnp.int32)
    parts = [block for _, block in blocks]
    rows, width = parts[0].shape
    count = len(parts)
    whole = jax.ShapeDtypeStruct((total, width), bf16)
    held = [pl.BlockSpec(memory_space=pl.ANY)] * len(into)
    out = lambda: pl.BlockSpec((rows, width), lambda k, owners_ref, begins_ref: (owners_ref[k], 0))
    fixed = lambda shape: pl.BlockSpec(shape, lambda k, owners_ref, begins_ref: (0, 0))
    return pl.pallas_call(
        functools.partial(kernel, begins.shape[1], count),
        grid_spec=pltpu.PrefetchScalarGridSpec(
            num_scalar_prefetch=2,
            grid=(count,),
            in_specs=[fixed(mod.shape)] + [fixed((rows, width))] * count + held,
            out_specs=[out(), out()],
            scratch_shapes=[pltpu.VMEM((rows, width), bf16)] if scratch else [],
        ),
        out_shape=[whole, whole],
        input_output_aliases={3 + count + k: k for k in range(len(into))},
        compiler_params=pltpu.CompilerParams(vmem_limit_bytes=28 * 2**20, dimension_semantics=("arbitrary",)),
        cost_estimate=pl.CostEstimate(
            flops=count * rows * width * 20, bytes_accessed=count * rows * width * 6, transcendentals=0
        ),
        name=name,
    )(owners, begins, mod, *parts, *into)


def own_columns(x, part, *others):
    count = x.shape[1] // part

    def kernel(index_ref, x_ref, *refs):
        for p in range(count):

            @pl.when(index_ref[0] == p)
            def _():
                refs[-1][...] = x_ref[:, p * part : (p + 1) * part]

    return pl.pallas_call(
        kernel,
        in_specs=[pl.BlockSpec(memory_space=pltpu.SMEM), pl.BlockSpec(memory_space=pltpu.VMEM)]
        + [pl.BlockSpec(memory_space=pl.ANY)] * len(others),
        out_specs=pl.BlockSpec(memory_space=pltpu.VMEM),
        out_shape=jax.ShapeDtypeStruct((x.shape[0], part), x.dtype),
        name="own_columns",
    )(lax.axis_index("chan").astype(jnp.int32)[None], x, *others)


def sums_kernel(n_seq, begins_ref, share_ref, normed_ref, up_ref, branch_ref, out_ref):
    rows, width = share_ref.shape
    k = pl.program_id(0)

    @pl.when(k == 0)
    def _():
        out_ref[...] = jnp.zeros(out_ref.shape, f32)

    lanes = 2 * LANES if width % (2 * LANES) == 0 else width
    token = k * rows + lax.broadcasted_iota(jnp.int32, (rows, 1), 0)
    for at in range(0, width, lanes):
        cols = slice(at, at + lanes)
        share = share_ref[:, cols].astype(f32)
        terms = [share, share * normed_ref[:, cols].astype(f32)]
        terms.append(up_ref[:, cols].astype(f32) * branch_ref[:, cols].astype(f32))
        for j, term in enumerate(terms):
            rest = jnp.sum(term, axis=0, keepdims=True)
            for s in range(n_seq - 1, 0, -1):
                later = jnp.sum(jnp.where(token >= begins_ref[0, s], term, 0.0), axis=0, keepdims=True)
                at_row = j * n_seq + s
                mine = later if s == n_seq - 1 else later - after_it
                out_ref[at_row : at_row + 1, cols] += mine
                after_it = later
            out_ref[j * n_seq : j * n_seq + 1, cols] += rest - (after_it if n_seq > 1 else 0.0)


def token_sums(share, normed, up, branch, begins):
    tokens, width = share.shape
    n_seq = begins.shape[1]
    rows = LANES
    spec = lambda: pl.BlockSpec((rows, width), lambda k: (k, 0))
    height = 3 * n_seq + (-3 * n_seq % 8)
    return pl.pallas_call(
        functools.partial(sums_kernel, n_seq),
        grid=(tokens // rows,),
        in_specs=[pl.BlockSpec(memory_space=pltpu.SMEM), spec(), spec(), spec(), spec()],
        out_specs=pl.BlockSpec((height, width), lambda k: (0, 0)),
        out_shape=jax.ShapeDtypeStruct((height, width), f32),
        compiler_params=pltpu.CompilerParams(vmem_limit_bytes=32 * 2**20, dimension_semantics=("arbitrary",)),
        cost_estimate=pl.CostEstimate(flops=tokens * width * 12, bytes_accessed=tokens * width * 8, transcendentals=0),
        name="token_sums",
    )(begins, share, normed, up, branch)


def local(
    activations,
    condition,
    seq_lengths,
    w_ada,
    b_ada,
    norm_gain,
    w_in_x,
    w_in_z,
    conv_weight,
    conv_bias,
    w_xproj,
    w_dt,
    dt_bias,
    a_log,
    d_skip,
    w_out,
    grad_out,
):
    ring = Ring()
    tok_loc, width = activations.shape
    low_rank = w_dt.shape[0]
    states = a_log.shape[1]
    channels = a_log.shape[0]
    conv_taps = conv_weight.shape[1]
    tok_count = tok_loc * ring.n
    tok_start = lax.axis_index("chan") * tok_loc
    act_ring = Steps(ring.blocks(activations))
    act_in = [act_ring.go()]
    cond_act = jax.nn.silu(condition.astype(f32)).astype(bf16)
    modulation = (
        jnp.einsum("si,kji->skj", cond_act, w_ada, preferred_element_type=f32) + b_ada[None]
    )
    part_width = norm_gain.shape[0]
    seq_count = seq_lengths.shape[1]
    packed = jnp.concatenate([modulation.reshape(3 * seq_count, part_width), norm_gain[None]], axis=0)
    packing = Steps(small_gather(packed, "chan"))
    packing.go()
    act_in.append(act_ring.go())
    packing.go(act_in[0])
    seq_lengths, conv_weight, conv_bias, w_dt, dt_bias, a_log, d_skip = after(
        (seq_lengths, conv_weight, conv_bias, w_dt, dt_bias, a_log, d_skip), act_in[0]
    )
    w_in = after(jnp.concatenate([w_in_x, w_in_z], axis=0), act_in[0])
    seq_lens = seq_lengths[0]
    seq_ends = jnp.cumsum(seq_lens)
    begins = seq_ends - seq_lens
    position = jnp.arange(tok_count, dtype=jnp.int32)
    member = (position[:, None] >= begins[None, :]) & (position[:, None] < seq_ends[None, :])
    onehot = member.astype(f32)
    in_seq = jnp.sum(onehot * (position[:, None] - begins[None, :]).astype(f32), axis=1)
    per_token = lambda rows, hot: sum(hot[:, s : s + 1] * rows[s][None] for s in range(seq_count))
    a_neg = -jnp.exp(a_log).T
    act_in.append(act_ring.go(w_in, in_seq))
    packing.go(act_in[1])
    far_wait = packing.arrived
    packed = packing.end().transpose(1, 0, 2).reshape(3 * seq_count + 1, width)
    packed = jnp.pad(packed, ((0, -packed.shape[0] % 8), (0, 0)))
    mod_full = packed[: 3 * seq_count].reshape(seq_count, 3, width)
    gain_full = packed[3 * seq_count]
    act_ring.go(far_wait)
    act_blocks = act_ring.end()
    soon = 5 if len(act_blocks) == 8 else 0
    norm = functools.partial(place, place_norm_kernel, begins=begins[None], mod=packed, total=tok_count, scratch=True)
    so_far = tuple(norm(act_blocks[:soon], name="place_norm_soon")) if soon else ()
    up_ring = Steps(ring.blocks(after(grad_out, act_in[-1])))
    up_in = [up_ring.go()]
    xmod, normed = norm(act_blocks[soon:], name="place_norm", into=so_far)
    inner = dot_across(xmod, w_in)
    x_inner = inner[:, :channels]
    xmod_halves = core_halves(after(xmod, inner))
    conv_pre = jnp.zeros_like(x_inner) + conv_bias[None, :]
    for tap_index in range(conv_taps):
        lag = conv_taps - 1 - tap_index
        valid = (in_seq >= lag).astype(f32)[:, None]
        conv_pre = conv_pre + conv_weight[:, tap_index][None, :] * delay_rows(x_inner, lag) * valid
    act_low = jax.nn.silu(conv_pre).astype(bf16)
    up_in.append(up_ring.go())
    adding = Steps(sum_chan(low_dot(act_low, w_xproj), PROJ_WIRE))
    adding.go(up_in[0])
    adding.go()
    adding.go(up_in[1])
    up_in.append(up_ring.go())
    adding.go()
    adding.go(up_in[2])
    up_ring.go()
    proj = adding.end()
    dt_low = proj[:, :low_rank].astype(bf16)
    d_branch_all, whole_up = place(
        place_gate_kernel, up_ring.end(), begins[None], packed, "place_gate", tok_count
    )
    d_gated = dot_across(d_branch_all, w_out)
    gated, d_z_low, d_dt_low, d_act, d_log, bias_skip, proj_terms = scans(
        proj, act_low, inner, d_gated, w_dt, dt_bias, a_neg, d_skip, begins[None]
    )
    adding = Steps(sum_chan(proj_terms, DPROJ_WIRE))
    branch_part = lax.optimization_barrier(low_dot(gated, w_out).astype(bf16))
    branch_sum = Scatter(ring, branch_part)
    adding.go()
    ring.hop([branch_sum])
    out_rows = Steps(sum_grad(gated, core_halves(d_branch_all), bf16))
    in_z_rows = Steps(sum_grad(d_z_low, xmod_halves, bf16))
    out_rows.go(branch_part)
    arrived = adding.arrived
    adding.go(out_rows.sent)
    in_z_rows.go(arrived)
    arrived = adding.arrived
    adding.go(in_z_rows.sent, branch_sum.arrived)
    flight = ring.launch([branch_sum])
    out_rows.go(arrived)
    arrived = adding.arrived
    adding.go(out_rows.sent)
    in_z_rows.go(arrived)
    adding.go(in_z_rows.sent)
    adding.go()
    d_proj = adding.end().astype(bf16)
    ring.land(flight, adding.arrived)
    d_act = d_act + dot_across(d_proj, w_xproj)
    d_conv = d_act * silu_slope(conv_pre)
    d_x_inner = jnp.zeros_like(d_conv)
    tap_grads = []
    for tap_index in range(conv_taps):
        lag = conv_taps - 1 - tap_index
        valid = (in_seq >= lag).astype(f32)[:, None]
        masked = d_conv * valid
        ahead = advance_rows(masked, lag)
        tap_grads.append(jnp.sum(ahead * x_inner, axis=0))
        d_x_inner = d_x_inner + conv_weight[:, tap_index][None, :] * ahead
    d_x_low = d_x_inner.astype(bf16)
    in_x_rows = Steps(sum_grad(d_x_low, xmod_halves, bf16))
    d_xmod_part = (low_dot(d_x_low, w_in_x) + low_dot(d_z_low, w_in_z)).astype(bf16)
    d_xmod_part = lax.optimization_barrier(d_xmod_part)
    in_x_rows.go(d_xmod_part)
    d_xmod_sum = Scatter(ring, d_xmod_part)
    both = [branch_sum, d_xmod_sum]
    ring.hop(both)
    first = d_xmod_sum.arrived
    ring.hop(both)
    share = after(d_xmod_part, first)
    summing = Steps(small_sum(token_sums(share, normed, whole_up, branch_part, begins[None]), "chan"))
    summing.go()
    in_x_rows.go(first)
    out_rows.go(first)
    rows_now = jnp.concatenate([modulation[:, 1], cond_act.astype(f32).reshape(-1, part_width)], axis=0)
    knowing = Steps(small_gather(rows_now, "rows"))
    knowing.go(first)
    d_proj = after(d_proj, first)
    small = jnp.concatenate(
        [
            dot_tokens(d_proj, act_low),
            dot_tokens(dt_low, d_dt_low),
            d_log * a_neg,
            jnp.stack(tap_grads),
            jnp.sum(d_conv, axis=0)[None],
            bias_skip[0:1],
            bias_skip[8:9],
        ],
        axis=0,
    )
    small = jnp.pad(small, ((0, -small.shape[0] % 16), (0, 0)))
    small_rows = Steps(small_sum(small, "rows"))
    small_rows.go()
    second = d_xmod_sum.arrived
    ring.hop(both, summing.sent, in_x_rows.sent, out_rows.sent, small_rows.sent)
    summing.go(second)
    in_z_rows.go(second)
    small_rows.go(second)
    knowing.go(second)
    grad_w_out = out_rows.end(second)
    third = d_xmod_sum.arrived
    ring.hop(both, summing.sent, in_z_rows.sent, small_rows.sent, grad_w_out)
    summing.go(third)
    known = knowing.end(third)
    scale_all = known[:, :seq_count].reshape(-1, part_width)
    cond_all = jnp.tile(known[:, seq_count:].reshape(-1, width).astype(bf16), (3, 1))
    in_x_rows.go(third)
    grad_w_in_z = in_z_rows.end(third)
    grad_w_in_x = in_x_rows.end()
    while d_xmod_sum.result is None:
        ring.hop(both)
    last = d_xmod_sum.arrived
    branch, d_xmod = branch_sum.result, d_xmod_sum.result
    sums = own_columns(summing.end(last), part_width, grad_w_in_z, grad_w_in_x)
    reaching = Steps(small_gather(sums, "rows"))
    reaching.go()
    reaching.go()
    reach = reaching.end()
    small = small_rows.end(last)
    onehot_loc = lax.dynamic_slice_in_dim(onehot, tok_start, tok_loc, 0)
    counts = [w_xproj.shape[1], low_rank, states, conv_taps, 1, 1, 1]
    pieces, at = [], 0
    for count in counts:
        pieces.append(small[at : at + count])
        at += count
    by_shift, by_scale, by_gate = [
        reach[:, k * seq_count : (k + 1) * seq_count].reshape(-1, part_width) for k in range(3)
    ]
    grad_gain = jnp.sum(by_scale * (1.0 + scale_all), axis=0)
    d_mod_all = jnp.concatenate([by_shift, by_scale * norm_gain[None], by_gate], axis=1)
    grad_b_ada = jnp.sum(d_mod_all, axis=0).reshape(3, part_width)
    high = d_mod_all.astype(bf16)
    rest = d_mod_all - high.astype(f32)
    middle = rest.astype(bf16)
    split = jnp.concatenate([high, middle, (rest - middle.astype(f32)).astype(bf16)], axis=0)
    grad_w_ada = dot_tokens(split, cond_all).reshape(3, part_width, width)
    block_out = (activations.astype(f32) + per_token(mod_full[:, 2], onehot_loc) * branch).astype(bf16)
    wide_loc = activations.astype(f32)
    centred_loc = wide_loc - jnp.mean(wide_loc, axis=1, keepdims=True)
    inv_std_loc = lax.rsqrt(jnp.mean(centred_loc * centred_loc, axis=1, keepdims=True) + EPSILON)
    normed_loc = centred_loc * inv_std_loc
    scale_loc = per_token(mod_full[:, 1], onehot_loc)
    d_normed = d_xmod * (1.0 + scale_loc) * gain_full[None, :]
    mean_first = jnp.mean(d_normed, axis=1, keepdims=True)
    mean_second = jnp.mean(d_normed * normed_loc, axis=1, keepdims=True)
    grad_input = (
        inv_std_loc * (d_normed - mean_first - normed_loc * mean_second) + grad_out.astype(f32)
    ).astype(bf16)
    return (
        block_out,
        grad_input,
        grad_w_ada,
        grad_b_ada,
        grad_gain,
        grad_w_in_x,
        grad_w_in_z,
        pieces[3].T,
        pieces[4][0],
        pieces[0].T,
        pieces[1],
        pieces[5][0],
        pieces[2].T,
        pieces[6][0],
        grad_w_out,
    )


PROJ_WIRE = bf16
DPROJ_WIRE = bf16


def solution(mesh):
    return jax.shard_map(
        local,
        mesh=mesh,
        in_specs=(
            P(("rows", "chan"), None),
            P("rows", None),
            P("rows", None),
            P(None, "chan", None),
            P(None, "chan"),
            P("chan"),
            P("chan", None),
            P("chan", None),
            P("chan", None),
            P("chan"),
            P("chan", None),
            P(None, "chan"),
            P("chan"),
            P("chan", None),
            P("chan"),
            P("chan", None),
            P(("rows", "chan"), None),
        ),
        out_specs=(
            P(("rows", "chan"), None),
            P(("rows", "chan"), None),
            P(None, "chan", None),
            P(None, "chan"),
            P("chan"),
            P("chan", None),
            P("chan", None),
            P("chan", None),
            P("chan"),
            P("chan", None),
            P(None, "chan"),
            P("chan"),
            P("chan", None),
            P("chan"),
            P("chan", None),
        ),
        check_vma=False,
    )
```

```python
import functools
import math

import jax
import jax.numpy as jnp
from jax import lax
from jax.experimental import pallas as pl
from jax.experimental.pallas import tpu as pltpu
from jax.sharding import PartitionSpec as P

CHUNK = 16
LANES = 128
LOG2E = math.log2(math.e)
f32 = jnp.float32
bf16 = jnp.bfloat16


def scan_kernel(
    n_seq,
    states,
    begins_ref,
    proj_ref,
    act_ref,
    z_ref,
    d_gated_ref,
    w_dt_ref,
    dt_bias_ref,
    an_ref,
    skip_ref,
    gated_ref,
    d_z_ref,
    d_dt_ref,
    d_act_ref,
    ga_ref,
    sums_ref,
    terms_ref,
    b_all,
    c_all,
    pf_all,
    db_all,
    b_blk_all,
    c_blk_all,
    delta_all,
    step_all,
    dm_all,
    exp_all,
):
    tokens, channels = act_ref.shape
    n_pairs = tokens // (2 * CHUNK)
    wide = CHUNK * states
    low_rank = proj_ref.shape[1] - 2 * states
    an = an_ref[...]
    a2 = an * LOG2E
    dot = functools.partial(jnp.dot, preferred_element_type=f32)
    across = functools.partial(
        lax.dot_general, dimension_numbers=(((1,), (1,)), ((), ())), preferred_element_type=f32
    )

    def diagonal(rows):
        r = lax.broadcasted_iota(jnp.int32, (rows, wide), 0) % CHUNK
        return (r == lax.broadcasted_iota(jnp.int32, (rows, wide), 1) // states).astype(f32)

    diag = diagonal(CHUNK)
    half = states // 2
    spot = lax.broadcasted_iota(jnp.int32, (CHUNK, CHUNK * half), 1) // half
    ones_blk = (lax.broadcasted_iota(jnp.int32, (CHUNK, CHUNK * half), 0) == spot).astype(bf16)
    m = lax.broadcasted_iota(jnp.int32, (low_rank + 2 * states, wide), 0)
    q = lax.broadcasted_iota(jnp.int32, (low_rank + 2 * states, wide), 1) % states
    pick_b = (m == low_rank + q).astype(bf16)
    pick_c = (m == low_rank + states + q).astype(bf16)
    tile = pl.program_id(0)

    @pl.when(tile == 0)
    def _():
        many = diagonal(LANES)

        def spread(k, carry):
            base = pl.multiple_of(k * LANES, LANES)
            proj = proj_ref[pl.ds(base, LANES), :]
            low = proj.astype(bf16)
            b_blk_all[pl.ds(base, LANES), :] = (dot(low, pick_b) * many).astype(bf16)
            c_blk_all[pl.ds(base, LANES), :] = (dot(low, pick_c) * many).astype(bf16)
            turned = proj.astype(f32).T
            bt = turned[low_rank : low_rank + states]
            ct = turned[low_rank + states :]
            for i in range(LANES):
                at = pl.ds(pl.multiple_of(base * states + i * states, states), states)
                b_all[at, :] = jnp.broadcast_to(bt[:, i : i + 1], (states, channels))
                c_all[at, :] = jnp.broadcast_to(ct[:, i : i + 1], (states, channels))
            return carry

        lax.fori_loop(0, tokens // LANES, spread, 0, unroll=2)

    def prepare(k, carry):
        here = pl.ds(pl.multiple_of(k * LANES, LANES), LANES)
        dt_raw = dot(proj_ref[here, :].astype(bf16), w_dt_ref[...]) + dt_bias_ref[...]
        delta = jnp.maximum(dt_raw, 0.0) + jnp.log1p(jnp.exp(-jnp.abs(dt_raw)))
        delta_all[here, :] = delta
        step_all[here, :] = delta * act_ref[here, :].astype(f32)
        z = z_ref[here, :]
        dm_all[here, :] = d_gated_ref[here, :] * (z * jax.nn.sigmoid(z))
        return carry

    lax.fori_loop(0, tokens // LANES, prepare, 0, unroll=10 if tokens % (10 * LANES) == 0 else 1)

    def keep_at(t):
        keep = None
        for s in range(1, n_seq):
            k = jnp.where(begins_ref[0, s] == t, 0.0, 1.0).astype(f32)
            keep = k if keep is None else keep * k
        return keep

    def sweep(body, cut, carry):
        plain, masked = functools.partial(body, False), functools.partial(body, True)
        if n_seq == 1:
            return lax.fori_loop(0, n_pairs, plain, carry)
        if n_seq > 2:
            return lax.fori_loop(0, n_pairs, masked, carry)
        carry = lax.fori_loop(0, cut, plain, carry)
        carry = masked(cut, carry)
        return lax.fori_loop(cut + 1, n_pairs, plain, carry)

    def row(ref, t):
        return ref[pl.ds(t, 1), :]

    def forward(masked, pair, carry):
        sf, g = carry
        base = pl.multiple_of(pair * 2 * CHUNK, 2 * CHUNK)
        for i in range(2 * CHUNK):
            at = pl.ds(pl.multiple_of(base * states + i * states, states), states)
            decay = jnp.exp2(row(delta_all, base + i) * a2)
            if masked:
                keep = keep_at(base + i)
                sf = sf * keep
                g = g * keep
            pf = decay * sf
            sf = pf + row(step_all, base + i) * b_all[at, :]
            db = row(dm_all, base + i) * c_all[at, :] + g
            g = decay * db
            pf_all[at, :] = pf
            db_all[at, :] = db
        return sf, g

    zero = jnp.zeros((states, channels), f32)
    first = begins_ref[0, n_seq - 1]
    sweep(forward, first // (2 * CHUNK), (zero, zero))

    def backward(masked, k, carry):
        sb, g, ga = carry
        base = pl.multiple_of((n_pairs - 1 - k) * 2 * CHUNK, 2 * CHUNK)
        for i in range(2 * CHUNK - 1, -1, -1):
            at = pl.ds(pl.multiple_of(base * states + i * states, states), states)
            delta = row(delta_all, base + i)
            decay = jnp.exp2(delta * a2)
            drive = row(step_all, base + i) * b_all[at, :]
            if masked:
                keep = keep_at(base + i + 1)
                sb = sb * keep
                g = g * keep
            pb = decay * sb
            sb = pb + drive
            df = row(dm_all, base + i) * c_all[at, :] + g
            g = decay * df
            pf = pf_all[at, :]
            db = db_all[at, :]
            d_expo = df * pf + db * pb
            ga = ga + d_expo * delta
            pf_all[at, :] = pf + drive + sb
            db_all[at, :] = df + db
            by_n = d_expo * an
            exp_all[pl.ds(pl.multiple_of(base * half + i * half, half), half), :] = by_n[:half] + by_n[half:]
        return sb, g, ga

    cut = n_pairs - 1 - (first - 1) // (2 * CHUNK)
    _, _, ga = sweep(backward, cut, (zero, zero, zero))
    ga_ref[...] = ga

    def finish(k, carry):
        by_bias, by_skip = carry
        base = pl.multiple_of(k * LANES, LANES)
        here = pl.ds(base, LANES)
        low = proj_ref[here, :].astype(bf16)
        act = act_ref[here, :].astype(f32)
        d_mixed = dm_all[here, :]
        dm_low = d_mixed.astype(bf16)
        step_low = step_all[here, :].astype(bf16)
        y, through, expo, dcm, dbm = [], [], [], [], []
        for c in range(LANES // CHUNK):
            at = pl.ds(pl.multiple_of(base * states + c * wide, wide), wide)
            mine = pl.ds(pl.multiple_of(base + c * CHUNK, CHUNK), CHUNK)
            span = slice(c * CHUNK, (c + 1) * CHUNK)
            both = pf_all[at, :].astype(bf16)
            drv = db_all[at, :].astype(bf16)
            y.append(dot(c_blk_all[mine, :], both))
            through.append(dot(b_blk_all[mine, :], drv))
            at = pl.ds(pl.multiple_of(base * half + c * CHUNK * half, CHUNK * half), CHUNK * half)
            expo.append(dot(ones_blk, exp_all[at, :].astype(bf16)))
            dcm.append((across(dm_low[span], both) * diag).astype(bf16))
            dbm.append((across(step_low[span], drv) * diag).astype(bf16))
        whole = lambda parts: jnp.concatenate(parts, axis=0)
        skip = skip_ref[...]
        z = z_ref[here, :]
        sigma = jax.nn.sigmoid(z)
        mixed = whole(y) + skip * act
        gated_ref[here, :] = (mixed * (z * sigma)).astype(bf16)
        d_z_ref[here, :] = (d_gated_ref[here, :] * mixed * (sigma * (1.0 + z * (1.0 - sigma)))).astype(bf16)
        via = whole(through)
        d_act_ref[here, :] = d_mixed * skip + via * delta_all[here, :]
        dt_raw = dot(low, w_dt_ref[...]) + dt_bias_ref[...]
        d_dt_raw = (whole(expo) + via * act) * jax.nn.sigmoid(dt_raw)
        d_dt = d_dt_raw.astype(bf16)
        d_dt_ref[here, :] = d_dt
        terms = across(d_dt, w_dt_ref[...]) + across(whole(dbm), pick_b) + across(whole(dcm), pick_c)

        @pl.when(tile == 0)
        def _():
            terms_ref[here, :] = terms

        @pl.when(tile != 0)
        def _():
            terms_ref[here, :] += terms

        total = lambda v: jnp.sum(v, axis=0, keepdims=True)
        return by_bias + total(d_dt_raw), by_skip + total(d_mixed * act)

    none = jnp.zeros((1, channels), f32)
    by_bias, by_skip = lax.fori_loop(0, tokens // LANES, finish, (none, none), unroll=2)
    sums_ref[0:8, :] = jnp.broadcast_to(by_bias, (8, channels))
    sums_ref[8:16, :] = jnp.broadcast_to(by_skip, (8, channels))


def scans(proj, act_low, z_inner, d_gated, w_dt, dt_bias, a_neg, d_skip, begins):
    tokens, channels = act_low.shape
    states = a_neg.shape[0]
    tile = LANES if channels % LANES == 0 else channels
    wide = CHUNK * states
    w_dt = jnp.pad(w_dt, ((0, 2 * states), (0, 0)))
    col = lambda: pl.BlockSpec((tokens, tile), lambda j: (0, j))
    rows = lambda n: pl.BlockSpec((n, tile), lambda j: (0, j))
    full = lambda: pl.BlockSpec(proj.shape, lambda j: (0, 0))
    if z_inner.shape[1] % tile or tile % LANES:
        z_inner = z_inner[:, -channels:]
    ahead = (z_inner.shape[1] - channels) // tile
    z_col = pl.BlockSpec((tokens, tile), lambda j: (0, ahead + j))
    sds = jax.ShapeDtypeStruct
    return pl.pallas_call(
        functools.partial(scan_kernel, begins.shape[1], states),
        grid=(channels // tile,),
        in_specs=[
            pl.BlockSpec(memory_space=pltpu.SMEM),
            full(),
            col(),
            z_col,
            col(),
            rows(w_dt.shape[0]),
            rows(1),
            rows(states),
            rows(1),
        ],
        out_specs=[col(), col(), col(), col(), rows(states), rows(16), full()],
        out_shape=[
            sds((tokens, channels), bf16),
            sds((tokens, channels), bf16),
            sds((tokens, channels), bf16),
            sds((tokens, channels), f32),
            sds((states, channels), f32),
            sds((16, channels), f32),
            sds(proj.shape, f32),
        ],
        scratch_shapes=[pltpu.VMEM((tokens * states, tile), f32)] * 4
        + [pltpu.VMEM((tokens, wide), bf16)] * 2
        + [pltpu.VMEM((tokens, tile), f32)] * 3
        + [pltpu.VMEM((tokens * states // 2, tile), f32)],
        compiler_params=pltpu.CompilerParams(vmem_limit_bytes=62 * 2**20, dimension_semantics=("arbitrary",)),
        cost_estimate=pl.CostEstimate(
            flops=tokens * channels * states * 60,
            bytes_accessed=tokens * channels * 24,
            transcendentals=2 * tokens * channels * states,
        ),
        name="scan_all",
    )(begins, proj, act_low, z_inner, d_gated, w_dt, dt_bias[None], a_neg, d_skip[None])


EPSILON = 1e-06
HIGHEST = lax.Precision.HIGHEST


def low_dot(left, right):
    return jnp.dot(left, right, preferred_element_type=f32)


def dot_across(left, right):
    return lax.dot_general(left, right, (((1,), (1,)), ((), ())), preferred_element_type=f32)


def dot_tokens(left, right):
    return lax.dot_general(left, right, (((0,), (0,)), ((), ())), preferred_element_type=f32)


def delay_rows(operand, lag):
    if lag == 0:
        return operand
    padding = jnp.zeros((lag,) + operand.shape[1:], operand.dtype)
    return jnp.concatenate([padding, operand[:-lag]], axis=0)


def advance_rows(operand, lag):
    if lag == 0:
        return operand
    padding = jnp.zeros((lag,) + operand.shape[1:], operand.dtype)
    return jnp.concatenate([operand[lag:], padding], axis=0)


def after(x, *others):
    others = tuple(jax.tree.leaves(others))
    return lax.optimization_barrier((x, others))[0] if others else x


class Steps:
    def __init__(self, steps):
        self.steps = steps
        self.result = self.sent = self.arrived = None
        next(steps)

    def go(self, *others):
        if self.result is None:
            try:
                self.sent, self.arrived = self.steps.send(others)
            except StopIteration as stop:
                self.result = stop.value
        return self.arrived

    def end(self, *others):
        while self.result is None:
            self.go(*others)
        return self.result


def silu_slope(operand):
    squash = jax.nn.sigmoid(operand)
    return squash * (1.0 + operand * (1.0 - squash))


class Ring:
    def __init__(self):
        self.n = lax.axis_size("chan")
        self.down = 4 if self.n % 8 == 0 else 1
        self.across = self.n // self.down
        order = [self.at(p) for p in range(self.n)]
        self.right = [(order[k], order[(k + 1) % self.n]) for k in range(self.n)]
        self.left = [(b, a) for a, b in self.right]
        index = lax.axis_index("chan")
        i, j = index // self.across, index % self.across
        back = self.down - 1 - i
        step = jnp.where(back % 2 == 0, j - 1, self.across - 1 - j)
        self.place = jnp.where(j == 0, i, self.down + back * (self.across - 1) + step)

    def at(self, p):
        if self.down == 1:
            return p
        back, step = (p - self.down) // (self.across - 1), (p - self.down) % (self.across - 1)
        if isinstance(p, int):
            column = 1 + step if back % 2 == 0 else self.across - 1 - step
            return p * self.across if p < self.down else (self.down - 1 - back) * self.across + column
        column = jnp.where(back % 2 == 0, 1 + step, self.across - 1 - step)
        return jnp.where(p < self.down, p * self.across, (self.down - 1 - back) * self.across + column)

    def owner(self, away):
        p = self.place + away
        if away > 0:
            p = jnp.where(p >= self.n, p - self.n, p)
        elif away < 0:
            p = jnp.where(p < 0, p + self.n, p)
        return self.at(p)

    def go_right(self, x):
        return lax.ppermute(x, "chan", self.right)

    def go_left(self, x):
        return lax.ppermute(x, "chan", self.left)

    def blocks(self, x):
        half = self.n // 2
        cut = x.shape[0] // 2
        pair = x, x
        found = [(self.owner(0), x)]
        waits = yield
        for step in range(1, half):
            sent = after(pair, waits)
            pair = self.go_right(sent[0]), self.go_left(sent[1])
            found += [(self.owner(-step), pair[0]), (self.owner(step), pair[1])]
            waits = yield sent, pair
        sent = after((pair[0][:cut], pair[1][cut:]), waits)
        pair = self.go_right(sent[0]), self.go_left(sent[1])
        yield sent, pair
        return found + [(self.owner(half), jnp.concatenate(pair, axis=0))]

    def scatter(self, part):
        half = self.n // 2
        rows = part.shape[0] // self.n
        cut = rows // 2
        mine = lambda away: lax.dynamic_slice_in_dim(part, self.owner(away) * rows, rows, 0)
        wide = lambda v: v.astype(f32)
        far = mine(half)
        right, left = yield far[:cut], far[cut:]
        for away in range(half - 1, 0, -1):
            ahead, behind = wide(mine(away)), wide(mine(-away))
            if away == half - 1:
                ahead = jnp.concatenate([ahead[:cut] + wide(right), ahead[cut:]], axis=0)
                behind = jnp.concatenate([behind[:cut], behind[cut:] + wide(left)], axis=0)
            else:
                ahead, behind = ahead + wide(right), behind + wide(left)
            right, left = yield ahead.astype(bf16), behind.astype(bf16)
        return wide(mine(0)) + wide(right) + wide(left)

    def hop(self, sums, *others):
        self.land(self.launch(sums, *others))

    def launch(self, sums, *others):
        sums = [one for one in sums if one.result is None]
        if not sums:
            return sums, None
        join = lambda side: jnp.concatenate([one.pair[side] for one in sums], axis=0)
        right, left = lax.optimization_barrier((join(0), join(1), tuple(jax.tree.leaves(others))))[:2]
        return sums, (self.go_right(right), self.go_left(left))

    def land(self, flight, *others):
        sums, pair = flight
        if not sums:
            return
        right, left = lax.optimization_barrier((pair, tuple(jax.tree.leaves(others))))[0]
        at = 0
        for one in sums:
            rows = one.pair[0].shape[0]
            one.take((right[at : at + rows], left[at : at + rows]))
            at += rows


class Scatter:
    def __init__(self, ring, part):
        self.steps = ring.scatter(part)
        self.result, self.arrived = None, None
        self.pair = next(self.steps)

    def take(self, arrived):
        self.arrived = arrived
        try:
            self.pair = self.steps.send(arrived)
        except StopIteration as stop:
            self.result = stop.value


def is_power(n):
    return n & (n - 1) == 0


def bits_of(n):
    return [1 << b for b in range(n.bit_length() - 1)]


def sum_chan(x, wire):
    n = lax.axis_size("chan")
    index = lax.axis_index("chan")
    waits = yield
    if not is_power(n) or x.shape[0] % (16 * n):
        return lax.psum(after(x, waits), "chan")
    perm = lambda b: [(i, i ^ b) for i in range(n)]
    for b in bits_of(n):
        h = x.shape[0] // 2
        upper = (index // b) % 2
        keep = lax.dynamic_slice_in_dim(x, upper * h, h, 0)
        send = lax.dynamic_slice_in_dim(x, (1 - upper) * h, h, 0).astype(wire)
        send = after(send, waits)
        other = lax.ppermute(send, "chan", perm(b))
        waits = yield send, other
        x = keep + other.astype(f32)
    x = x.astype(wire)
    for b in reversed(bits_of(n)):
        upper = (index // b) % 2
        x = after(x, waits)
        other = lax.ppermute(x, "chan", perm(b))
        waits = yield x, other
        x = jnp.concatenate([jnp.where(upper == 0, x, other), jnp.where(upper == 0, other, x)], axis=0)
    return after(x, waits)


def small_gather(x, axis):
    n = lax.axis_size(axis)
    waits = yield
    if not is_power(n) or n > 8:
        return lax.all_gather(after(x, waits), axis, axis=0)
    index = lax.axis_index(axis)
    x = x[None]
    for b in bits_of(n):
        x = after(x, waits)
        other = lax.ppermute(x, axis, [(i, i ^ b) for i in range(n)])
        waits = yield x, other
        other = after(other, waits)
        lower = (index // b) % 2 == 0
        x = jnp.concatenate([jnp.where(lower, x, other), jnp.where(lower, other, x)], axis=0)
    return x


def small_sum(x, axis):
    n = lax.axis_size(axis)
    waits = yield
    if not is_power(n) or n > 8:
        return lax.psum(after(x, waits), axis)
    for b in bits_of(n):
        x = after(x, waits)
        other = lax.ppermute(x, axis, [(i, i ^ b) for i in range(n)])
        waits = yield x, other
        x = x + after(other, waits)
    return x


def join_kernel(upper_ref, mine_ref, other_ref, out_ref):
    k = pl.program_id(0)

    @pl.when(k == upper_ref[0])
    def _():
        out_ref[...] = mine_ref[...]

    @pl.when(k != upper_ref[0])
    def _():
        out_ref[...] = other_ref[...]


def join_halves(mine, other):
    rows, half = mine.shape
    fixed = lambda: pl.BlockSpec((rows, half), lambda k, upper_ref: (0, 0))
    return pl.pallas_call(
        join_kernel,
        grid_spec=pltpu.PrefetchScalarGridSpec(
            num_scalar_prefetch=1,
            grid=(2,),
            in_specs=[fixed(), fixed()],
            out_specs=pl.BlockSpec((rows, half), lambda k, upper_ref: (0, k)),
        ),
        out_shape=jax.ShapeDtypeStruct((rows, 2 * half), f32),
        compiler_params=pltpu.CompilerParams(vmem_limit_bytes=24 * 2**20, dimension_semantics=("arbitrary",)),
        cost_estimate=pl.CostEstimate(flops=0, bytes_accessed=rows * half * 16, transcendentals=0),
        name="join_halves",
    )((lax.axis_index("rows") % 2).astype(jnp.int32)[None], mine, other)


def sum_grad(left, right, wire):
    n = lax.axis_size("rows")
    waits = yield
    left = after(left, waits)
    if n != 4:
        return lax.psum(dot_tokens(left, right), "rows")
    core = [(0, 1), (1, 0), (2, 3), (3, 2)]
    chip = [(0, 2), (2, 0), (1, 3), (3, 1)]
    low, high = right
    send = dot_tokens(left, high)
    other = lax.ppermute(send, "rows", core)
    waits = yield send, other
    pair = (dot_tokens(after(left, send), low) + after(other, waits)).astype(wire)
    other = lax.ppermute(pair, "rows", chip)
    waits = yield pair, other
    total = pair.astype(f32) + after(other, waits).astype(f32)
    other = lax.ppermute(total, "rows", core)
    waits = yield total, other
    return join_halves(total, after(other, waits))


def core_halves(x):
    if lax.axis_size("rows") != 4:
        return x
    half = x.shape[1] // 2
    upper = lax.axis_index("rows") % 2
    part = lambda which: lax.dynamic_slice_in_dim(x, which * half, half, 1)
    return part(upper), part(1 - upper)


def place_norm_kernel(n_seq, count, owners_ref, begins_ref, mod_ref, *refs):
    blocks, (xmod_ref, normed_ref, held) = refs[:count], refs[-3:]
    rows, width = xmod_ref.shape
    step = 2 * CHUNK if rows % (2 * CHUNK) == 0 else rows
    k = pl.program_id(0)
    base = owners_ref[k] * rows

    def hold(block_ref):
        held[...] = block_ref[...]

    for i in range(count):
        pl.when(k == i)(functools.partial(hold, blocks[i]))
    shift, scale = mod_ref[0:1, :], mod_ref[1:2, :]
    gain = mod_ref[3 * n_seq : 3 * n_seq + 1, :]
    for start in range(0, rows, step):
        here = slice(start, start + step)
        wide = held[here, :].astype(f32)
        centred = wide - jnp.sum(wide, axis=1, keepdims=True) * (1.0 / width)
        square = jnp.sum(centred * centred, axis=1, keepdims=True) * (1.0 / width)
        normed = centred * lax.rsqrt(square + EPSILON)
        token = base + start + lax.broadcasted_iota(jnp.int32, (step, 1), 0)
        add, by = shift, gain * (1.0 + scale)
        for s in range(1, n_seq):
            later = token >= begins_ref[0, s]
            add = jnp.where(later, mod_ref[3 * s : 3 * s + 1, :], add)
            by = jnp.where(later, gain * (1.0 + mod_ref[3 * s + 1 : 3 * s + 2, :]), by)
        xmod_ref[here, :] = (normed * by + add).astype(bf16)
        normed_ref[here, :] = normed.astype(bf16)


def place_gate_kernel(n_seq, count, owners_ref, begins_ref, mod_ref, *refs):
    blocks, (gated_ref, plain_ref) = refs[:count], refs[-2:]
    rows = gated_ref.shape[0]
    step = CHUNK if rows % CHUNK == 0 else rows
    k = pl.program_id(0)
    base = owners_ref[k] * rows

    def fill(block_ref):
        def part(p, carry):
            here = pl.ds(pl.multiple_of(p * step, step), step)
            low = block_ref[here, :]
            token = base + p * step + lax.broadcasted_iota(jnp.int32, (step, 1), 0)
            gate = mod_ref[2:3, :]
            for s in range(1, n_seq):
                gate = jnp.where(token >= begins_ref[0, s], mod_ref[3 * s + 2 : 3 * s + 3, :], gate)
            gated_ref[here, :] = (low.astype(f32) * gate).astype(bf16)
            plain_ref[here, :] = low
            return carry

        lax.fori_loop(0, rows // step, part, 0)

    for i in range(count):
        pl.when(k == i)(functools.partial(fill, blocks[i]))


def place(kernel, blocks, begins, mod, name, total, scratch=False, into=()):
    owners = jnp.stack([owner for owner, _ in blocks]).astype(jnp.int32)
    parts = [block for _, block in blocks]
    rows, width = parts[0].shape
    count = len(parts)
    whole = jax.ShapeDtypeStruct((total, width), bf16)
    held = [pl.BlockSpec(memory_space=pl.ANY)] * len(into)
    out = lambda: pl.BlockSpec((rows, width), lambda k, owners_ref, begins_ref: (owners_ref[k], 0))
    fixed = lambda shape: pl.BlockSpec(shape, lambda k, owners_ref, begins_ref: (0, 0))
    return pl.pallas_call(
        functools.partial(kernel, begins.shape[1], count),
        grid_spec=pltpu.PrefetchScalarGridSpec(
            num_scalar_prefetch=2,
            grid=(count,),
            in_specs=[fixed(mod.shape)] + [fixed((rows, width))] * count + held,
            out_specs=[out(), out()],
            scratch_shapes=[pltpu.VMEM((rows, width), bf16)] if scratch else [],
        ),
        out_shape=[whole, whole],
        input_output_aliases={3 + count + k: k for k in range(len(into))},
        compiler_params=pltpu.CompilerParams(vmem_limit_bytes=28 * 2**20, dimension_semantics=("arbitrary",)),
        cost_estimate=pl.CostEstimate(
            flops=count * rows * width * 20, bytes_accessed=count * rows * width * 6, transcendentals=0
        ),
        name=name,
    )(owners, begins, mod, *parts, *into)


def own_columns(x, part, *others):
    count = x.shape[1] // part

    def kernel(index_ref, x_ref, *refs):
        for p in range(count):

            @pl.when(index_ref[0] == p)
            def _():
                refs[-1][...] = x_ref[:, p * part : (p + 1) * part]

    return pl.pallas_call(
        kernel,
        in_specs=[pl.BlockSpec(memory_space=pltpu.SMEM), pl.BlockSpec(memory_space=pltpu.VMEM)]
        + [pl.BlockSpec(memory_space=pl.ANY)] * len(others),
        out_specs=pl.BlockSpec(memory_space=pltpu.VMEM),
        out_shape=jax.ShapeDtypeStruct((x.shape[0], part), x.dtype),
        name="own_columns",
    )(lax.axis_index("chan").astype(jnp.int32)[None], x, *others)


def sums_kernel(n_seq, begins_ref, share_ref, normed_ref, up_ref, branch_ref, out_ref):
    rows, width = share_ref.shape
    k = pl.program_id(0)

    @pl.when(k == 0)
    def _():
        out_ref[...] = jnp.zeros(out_ref.shape, f32)

    lanes = 2 * LANES if width % (2 * LANES) == 0 else width
    token = k * rows + lax.broadcasted_iota(jnp.int32, (rows, 1), 0)
    for at in range(0, width, lanes):
        cols = slice(at, at + lanes)
        share = share_ref[:, cols].astype(f32)
        terms = [share, share * normed_ref[:, cols].astype(f32)]
        terms.append(up_ref[:, cols].astype(f32) * branch_ref[:, cols].astype(f32))
        for j, term in enumerate(terms):
            rest = jnp.sum(term, axis=0, keepdims=True)
            for s in range(n_seq - 1, 0, -1):
                later = jnp.sum(jnp.where(token >= begins_ref[0, s], term, 0.0), axis=0, keepdims=True)
                at_row = j * n_seq + s
                mine = later if s == n_seq - 1 else later - after_it
                out_ref[at_row : at_row + 1, cols] += mine
                after_it = later
            out_ref[j * n_seq : j * n_seq + 1, cols] += rest - (after_it if n_seq > 1 else 0.0)


def token_sums(share, normed, up, branch, begins):
    tokens, width = share.shape
    n_seq = begins.shape[1]
    rows = LANES
    spec = lambda: pl.BlockSpec((rows, width), lambda k: (k, 0))
    height = 3 * n_seq + (-3 * n_seq % 8)
    return pl.pallas_call(
        functools.partial(sums_kernel, n_seq),
        grid=(tokens // rows,),
        in_specs=[pl.BlockSpec(memory_space=pltpu.SMEM), spec(), spec(), spec(), spec()],
        out_specs=pl.BlockSpec((height, width), lambda k: (0, 0)),
        out_shape=jax.ShapeDtypeStruct((height, width), f32),
        compiler_params=pltpu.CompilerParams(vmem_limit_bytes=32 * 2**20, dimension_semantics=("arbitrary",)),
        cost_estimate=pl.CostEstimate(flops=tokens * width * 12, bytes_accessed=tokens * width * 8, transcendentals=0),
        name="token_sums",
    )(begins, share, normed, up, branch)


def local(
    activations,
    condition,
    seq_lengths,
    w_ada,
    b_ada,
    norm_gain,
    w_in_x,
    w_in_z,
    conv_weight,
    conv_bias,
    w_xproj,
    w_dt,
    dt_bias,
    a_log,
    d_skip,
    w_out,
    grad_out,
):
    ring = Ring()
    tok_loc, width = activations.shape
    low_rank = w_dt.shape[0]
    states = a_log.shape[1]
    channels = a_log.shape[0]
    conv_taps = conv_weight.shape[1]
    tok_count = tok_loc * ring.n
    tok_start = lax.axis_index("chan") * tok_loc
    act_ring = Steps(ring.blocks(activations))
    act_in = [act_ring.go()]
    cond_act = jax.nn.silu(condition.astype(f32)).astype(bf16)
    modulation = (
        jnp.einsum("si,kji->skj", cond_act, w_ada, preferred_element_type=f32) + b_ada[None]
    )
    part_width = norm_gain.shape[0]
    seq_count = seq_lengths.shape[1]
    packed = jnp.concatenate([modulation.reshape(3 * seq_count, part_width), norm_gain[None]], axis=0)
    packing = Steps(small_gather(packed, "chan"))
    packing.go()
    act_in.append(act_ring.go())
    packing.go(act_in[0])
    seq_lengths, conv_weight, conv_bias, w_dt, dt_bias, a_log, d_skip = after(
        (seq_lengths, conv_weight, conv_bias, w_dt, dt_bias, a_log, d_skip), act_in[0]
    )
    w_in = after(jnp.concatenate([w_in_x, w_in_z], axis=0), act_in[0])
    seq_lens = seq_lengths[0]
    seq_ends = jnp.cumsum(seq_lens)
    begins = seq_ends - seq_lens
    position = jnp.arange(tok_count, dtype=jnp.int32)
    member = (position[:, None] >= begins[None, :]) & (position[:, None] < seq_ends[None, :])
    onehot = member.astype(f32)
    in_seq = jnp.sum(onehot * (position[:, None] - begins[None, :]).astype(f32), axis=1)
    per_token = lambda rows, hot: sum(hot[:, s : s + 1] * rows[s][None] for s in range(seq_count))
    a_neg = -jnp.exp(a_log).T
    act_in.append(act_ring.go(w_in, in_seq))
    packing.go(act_in[1])
    far_wait = packing.arrived
    packed = packing.end().transpose(1, 0, 2).reshape(3 * seq_count + 1, width)
    packed = jnp.pad(packed, ((0, -packed.shape[0] % 8), (0, 0)))
    mod_full = packed[: 3 * seq_count].reshape(seq_count, 3, width)
    gain_full = packed[3 * seq_count]
    act_ring.go(far_wait)
    act_blocks = act_ring.end()
    soon = 5 if len(act_blocks) == 8 else 0
    norm = functools.partial(place, place_norm_kernel, begins=begins[None], mod=packed, total=tok_count, scratch=True)
    so_far = tuple(norm(act_blocks[:soon], name="place_norm_soon")) if soon else ()
    up_ring = Steps(ring.blocks(after(grad_out, act_in[-1])))
    up_in = [up_ring.go()]
    xmod, normed = norm(act_blocks[soon:], name="place_norm", into=so_far)
    inner = dot_across(xmod, w_in)
    x_inner = inner[:, :channels]
    xmod_halves = core_halves(after(xmod, inner))
    conv_pre = jnp.zeros_like(x_inner) + conv_bias[None, :]
    for tap_index in range(conv_taps):
        lag = conv_taps - 1 - tap_index
        valid = (in_seq >= lag).astype(f32)[:, None]
        conv_pre = conv_pre + conv_weight[:, tap_index][None, :] * delay_rows(x_inner, lag) * valid
    act_low = jax.nn.silu(conv_pre).astype(bf16)
    up_in.append(up_ring.go())
    adding = Steps(sum_chan(low_dot(act_low, w_xproj), PROJ_WIRE))
    adding.go(up_in[0])
    adding.go()
    adding.go(up_in[1])
    up_in.append(up_ring.go())
    adding.go()
    adding.go(up_in[2])
    up_ring.go()
    proj = adding.end()
    dt_low = proj[:, :low_rank].astype(bf16)
    d_branch_all, whole_up = place(
        place_gate_kernel, up_ring.end(), begins[None], packed, "place_gate", tok_count
    )
    d_gated = dot_across(d_branch_all, w_out)
    gated, d_z_low, d_dt_low, d_act, d_log, bias_skip, proj_terms = scans(
        proj, act_low, inner, d_gated, w_dt, dt_bias, a_neg, d_skip, begins[None]
    )
    adding = Steps(sum_chan(proj_terms, DPROJ_WIRE))
    branch_part = lax.optimization_barrier(low_dot(gated, w_out).astype(bf16))
    branch_sum = Scatter(ring, branch_part)
    adding.go()
    ring.hop([branch_sum])
    out_rows = Steps(sum_grad(gated, core_halves(d_branch_all), bf16))
    in_z_rows = Steps(sum_grad(d_z_low, xmod_halves, bf16))
    out_rows.go(branch_part)
    arrived = adding.arrived
    adding.go(out_rows.sent)
    in_z_rows.go(arrived)
    arrived = adding.arrived
    adding.go(in_z_rows.sent, branch_sum.arrived)
    flight = ring.launch([branch_sum])
    out_rows.go(arrived)
    arrived = adding.arrived
    adding.go(out_rows.sent)
    in_z_rows.go(arrived)
    adding.go(in_z_rows.sent)
    adding.go()
    d_proj = adding.end().astype(bf16)
    ring.land(flight, adding.arrived)
    d_act = d_act + dot_across(d_proj, w_xproj)
    d_conv = d_act * silu_slope(conv_pre)
    d_x_inner = jnp.zeros_like(d_conv)
    tap_grads = []
    for tap_index in range(conv_taps):
        lag = conv_taps - 1 - tap_index
        valid = (in_seq >= lag).astype(f32)[:, None]
        masked = d_conv * valid
        ahead = advance_rows(masked, lag)
        tap_grads.append(jnp.sum(ahead * x_inner, axis=0))
        d_x_inner = d_x_inner + conv_weight[:, tap_index][None, :] * ahead
    d_x_low = d_x_inner.astype(bf16)
    in_x_rows = Steps(sum_grad(d_x_low, xmod_halves, bf16))
    d_xmod_part = (low_dot(d_x_low, w_in_x) + low_dot(d_z_low, w_in_z)).astype(bf16)
    d_xmod_part = lax.optimization_barrier(d_xmod_part)
    in_x_rows.go(d_xmod_part)
    d_xmod_sum = Scatter(ring, d_xmod_part)
    both = [branch_sum, d_xmod_sum]
    ring.hop(both)
    first = d_xmod_sum.arrived
    ring.hop(both)
    share = after(d_xmod_part, first)
    summing = Steps(small_sum(token_sums(share, normed, whole_up, branch_part, begins[None]), "chan"))
    summing.go()
    in_x_rows.go(first)
    out_rows.go(first)
    rows_now = jnp.concatenate([modulation[:, 1], cond_act.astype(f32).reshape(-1, part_width)], axis=0)
    knowing = Steps(small_gather(rows_now, "rows"))
    knowing.go(first)
    d_proj = after(d_proj, first)
    small = jnp.concatenate(
        [
            dot_tokens(d_proj, act_low),
            dot_tokens(dt_low, d_dt_low),
            d_log * a_neg,
            jnp.stack(tap_grads),
            jnp.sum(d_conv, axis=0)[None],
            bias_skip[0:1],
            bias_skip[8:9],
        ],
        axis=0,
    )
    small = jnp.pad(small, ((0, -small.shape[0] % 16), (0, 0)))
    small_rows = Steps(small_sum(small, "rows"))
    small_rows.go()
    second = d_xmod_sum.arrived
    ring.hop(both, summing.sent, in_x_rows.sent, out_rows.sent, small_rows.sent)
    summing.go(second)
    in_z_rows.go(second)
    small_rows.go(second)
    knowing.go(second)
    grad_w_out = out_rows.end(second)
    third = d_xmod_sum.arrived
    ring.hop(both, summing.sent, in_z_rows.sent, small_rows.sent, grad_w_out)
    summing.go(third)
    known = knowing.end(third)
    scale_all = known[:, :seq_count].reshape(-1, part_width)
    cond_all = jnp.tile(known[:, seq_count:].reshape(-1, width).astype(bf16), (3, 1))
    in_x_rows.go(third)
    grad_w_in_z = in_z_rows.end(third)
    grad_w_in_x = in_x_rows.end()
    while d_xmod_sum.result is None:
        ring.hop(both)
    last = d_xmod_sum.arrived
    branch, d_xmod = branch_sum.result, d_xmod_sum.result
    sums = own_columns(summing.end(last), part_width, grad_w_in_z, grad_w_in_x)
    reaching = Steps(small_gather(sums, "rows"))
    reaching.go()
    reaching.go()
    reach = reaching.end()
    small = small_rows.end(last)
    onehot_loc = lax.dynamic_slice_in_dim(onehot, tok_start, tok_loc, 0)
    counts = [w_xproj.shape[1], low_rank, states, conv_taps, 1, 1, 1]
    pieces, at = [], 0
    for count in counts:
        pieces.append(small[at : at + count])
        at += count
    by_shift, by_scale, by_gate = [
        reach[:, k * seq_count : (k + 1) * seq_count].reshape(-1, part_width) for k in range(3)
    ]
    grad_gain = jnp.sum(by_scale * (1.0 + scale_all), axis=0)
    d_mod_all = jnp.concatenate([by_shift, by_scale * norm_gain[None], by_gate], axis=1)
    grad_b_ada = jnp.sum(d_mod_all, axis=0).reshape(3, part_width)
    high = d_mod_all.astype(bf16)
    rest = d_mod_all - high.astype(f32)
    middle = rest.astype(bf16)
    split = jnp.concatenate([high, middle, (rest - middle.astype(f32)).astype(bf16)], axis=0)
    grad_w_ada = dot_tokens(split, cond_all).reshape(3, part_width, width)
    block_out = (activations.astype(f32) + per_token(mod_full[:, 2], onehot_loc) * branch).astype(bf16)
    wide_loc = activations.astype(f32)
    centred_loc = wide_loc - jnp.mean(wide_loc, axis=1, keepdims=True)
    inv_std_loc = lax.rsqrt(jnp.mean(centred_loc * centred_loc, axis=1, keepdims=True) + EPSILON)
    normed_loc = centred_loc * inv_std_loc
    scale_loc = per_token(mod_full[:, 1], onehot_loc)
    d_normed = d_xmod * (1.0 + scale_loc) * gain_full[None, :]
    mean_first = jnp.mean(d_normed, axis=1, keepdims=True)
    mean_second = jnp.mean(d_normed * normed_loc, axis=1, keepdims=True)
    grad_input = (
        inv_std_loc * (d_normed - mean_first - normed_loc * mean_second) + grad_out.astype(f32)
    ).astype(bf16)
    return (
        block_out,
        grad_input,
        grad_w_ada,
        grad_b_ada,
        grad_gain,
        grad_w_in_x,
        grad_w_in_z,
        pieces[3].T,
        pieces[4][0],
        pieces[0].T,
        pieces[1],
        pieces[5][0],
        pieces[2].T,
        pieces[6][0],
        grad_w_out,
    )


PROJ_WIRE = bf16
DPROJ_WIRE = bf16


def solution(mesh):
    return jax.shard_map(
        local,
        mesh=mesh,
        in_specs=(
            P(("rows", "chan"), None),
            P("rows", None),
            P("rows", None),
            P(None, "chan", None),
            P(None, "chan"),
            P("chan"),
            P("chan", None),
            P("chan", None),
            P("chan", None),
            P("chan"),
            P("chan", None),
            P(None, "chan"),
            P("chan"),
            P("chan", None),
            P("chan"),
            P("chan", None),
            P(("rows", "chan"), None),
        ),
        out_specs=(
            P(("rows", "chan"), None),
            P(("rows", "chan"), None),
            P(None, "chan", None),
            P(None, "chan"),
            P("chan"),
            P("chan", None),
            P("chan", None),
            P("chan", None),
            P("chan"),
            P("chan", None),
            P(None, "chan"),
            P("chan"),
            P("chan", None),
            P("chan"),
            P("chan", None),
        ),
        check_vma=False,
    )
```

```python
import functools
import math

import jax
import jax.numpy as jnp
from jax import lax
from jax.experimental import pallas as pl
from jax.experimental.pallas import tpu as pltpu
from jax.sharding import PartitionSpec as P

CHUNK = 16
LANES = 128
LOG2E = math.log2(math.e)
f32 = jnp.float32
bf16 = jnp.bfloat16


def scan_kernel(
    n_seq,
    states,
    begins_ref,
    proj_ref,
    act_ref,
    z_ref,
    d_gated_ref,
    w_dt_ref,
    dt_bias_ref,
    an_ref,
    skip_ref,
    gated_ref,
    d_z_ref,
    d_dt_ref,
    d_act_ref,
    ga_ref,
    sums_ref,
    terms_ref,
    b_all,
    c_all,
    pf_all,
    db_all,
    b_blk_all,
    c_blk_all,
    delta_all,
    step_all,
    dm_all,
    exp_all,
):
    tokens, channels = act_ref.shape
    n_pairs = tokens // (2 * CHUNK)
    wide = CHUNK * states
    low_rank = proj_ref.shape[1] - 2 * states
    an = an_ref[...]
    a2 = an * LOG2E
    dot = functools.partial(jnp.dot, preferred_element_type=f32)
    across = functools.partial(
        lax.dot_general, dimension_numbers=(((1,), (1,)), ((), ())), preferred_element_type=f32
    )

    def diagonal(rows):
        r = lax.broadcasted_iota(jnp.int32, (rows, wide), 0) % CHUNK
        return (r == lax.broadcasted_iota(jnp.int32, (rows, wide), 1) // states).astype(f32)

    diag = diagonal(CHUNK)
    half = states // 2
    spot = lax.broadcasted_iota(jnp.int32, (CHUNK, CHUNK * half), 1) // half
    ones_blk = (lax.broadcasted_iota(jnp.int32, (CHUNK, CHUNK * half), 0) == spot).astype(bf16)
    m = lax.broadcasted_iota(jnp.int32, (low_rank + 2 * states, wide), 0)
    q = lax.broadcasted_iota(jnp.int32, (low_rank + 2 * states, wide), 1) % states
    pick_b = (m == low_rank + q).astype(bf16)
    pick_c = (m == low_rank + states + q).astype(bf16)
    tile = pl.program_id(0)

    @pl.when(tile == 0)
    def _():
        many = diagonal(LANES)

        def spread(k, carry):
            base = pl.multiple_of(k * LANES, LANES)
            proj = proj_ref[pl.ds(base, LANES), :]
            low = proj.astype(bf16)
            b_blk_all[pl.ds(base, LANES), :] = (dot(low, pick_b) * many).astype(bf16)
            c_blk_all[pl.ds(base, LANES), :] = (dot(low, pick_c) * many).astype(bf16)
            turned = proj.astype(f32).T
            bt = turned[low_rank : low_rank + states]
            ct = turned[low_rank + states :]
            for i in range(LANES):
                at = pl.ds(pl.multiple_of(base * states + i * states, states), states)
                b_all[at, :] = jnp.broadcast_to(bt[:, i : i + 1], (states, channels))
                c_all[at, :] = jnp.broadcast_to(ct[:, i : i + 1], (states, channels))
            return carry

        lax.fori_loop(0, tokens // LANES, spread, 0, unroll=5)

    def prepare(k, carry):
        here = pl.ds(pl.multiple_of(k * LANES, LANES), LANES)
        dt_raw = dot(proj_ref[here, :].astype(bf16), w_dt_ref[...]) + dt_bias_ref[...]
        delta = jnp.maximum(dt_raw, 0.0) + jnp.log1p(jnp.exp(-jnp.abs(dt_raw)))
        delta_all[here, :] = delta
        step_all[here, :] = delta * act_ref[here, :].astype(f32)
        z = z_ref[here, :]
        dm_all[here, :] = d_gated_ref[here, :] * (z * jax.nn.sigmoid(z))
        return carry

    lax.fori_loop(0, tokens // LANES, prepare, 0, unroll=10 if tokens % (10 * LANES) == 0 else 1)

    def keep_at(t):
        keep = None
        for s in range(1, n_seq):
            k = jnp.where(begins_ref[0, s] == t, 0.0, 1.0).astype(f32)
            keep = k if keep is None else keep * k
        return keep

    def sweep(body, cut, carry):
        plain, masked = functools.partial(body, False), functools.partial(body, True)
        if n_seq == 1:
            return lax.fori_loop(0, n_pairs, plain, carry)
        if n_seq > 2:
            return lax.fori_loop(0, n_pairs, masked, carry)
        carry = lax.fori_loop(0, cut, plain, carry)
        carry = masked(cut, carry)
        return lax.fori_loop(cut + 1, n_pairs, plain, carry)

    def row(ref, t):
        return ref[pl.ds(t, 1), :]

    def forward(masked, pair, carry):
        sf, g = carry
        base = pl.multiple_of(pair * 2 * CHUNK, 2 * CHUNK)
        for i in range(2 * CHUNK):
            at = pl.ds(pl.multiple_of(base * states + i * states, states), states)
            decay = jnp.exp2(row(delta_all, base + i) * a2)
            if masked:
                keep = keep_at(base + i)
                sf = sf * keep
                g = g * keep
            pf = decay * sf
            sf = pf + row(step_all, base + i) * b_all[at, :]
            db = row(dm_all, base + i) * c_all[at, :] + g
            g = decay * db
            pf_all[at, :] = pf
            db_all[at, :] = db
        return sf, g

    zero = jnp.zeros((states, channels), f32)
    first = begins_ref[0, n_seq - 1]
    sweep(forward, first // (2 * CHUNK), (zero, zero))

    def backward(masked, k, carry):
        sb, g, ga = carry
        base = pl.multiple_of((n_pairs - 1 - k) * 2 * CHUNK, 2 * CHUNK)
        for i in range(2 * CHUNK - 1, -1, -1):
            at = pl.ds(pl.multiple_of(base * states + i * states, states), states)
            delta = row(delta_all, base + i)
            decay = jnp.exp2(delta * a2)
            drive = row(step_all, base + i) * b_all[at, :]
            if masked:
                keep = keep_at(base + i + 1)
                sb = sb * keep
                g = g * keep
            pb = decay * sb
            sb = pb + drive
            df = row(dm_all, base + i) * c_all[at, :] + g
            g = decay * df
            pf = pf_all[at, :]
            db = db_all[at, :]
            d_expo = df * pf + db * pb
            ga = ga + d_expo * delta
            pf_all[at, :] = pf + drive + sb
            db_all[at, :] = df + db
            by_n = d_expo * an
            exp_all[pl.ds(pl.multiple_of(base * half + i * half, half), half), :] = by_n[:half] + by_n[half:]
        return sb, g, ga

    cut = n_pairs - 1 - (first - 1) // (2 * CHUNK)
    _, _, ga = sweep(backward, cut, (zero, zero, zero))
    ga_ref[...] = ga

    def finish(k, carry):
        by_bias, by_skip = carry
        base = pl.multiple_of(k * LANES, LANES)
        here = pl.ds(base, LANES)
        low = proj_ref[here, :].astype(bf16)
        act = act_ref[here, :].astype(f32)
        d_mixed = dm_all[here, :]
        dm_low = d_mixed.astype(bf16)
        step_low = step_all[here, :].astype(bf16)
        y, through, expo, dcm, dbm = [], [], [], [], []
        for c in range(LANES // CHUNK):
            at = pl.ds(pl.multiple_of(base * states + c * wide, wide), wide)
            mine = pl.ds(pl.multiple_of(base + c * CHUNK, CHUNK), CHUNK)
            span = slice(c * CHUNK, (c + 1) * CHUNK)
            both = pf_all[at, :].astype(bf16)
            drv = db_all[at, :].astype(bf16)
            y.append(dot(c_blk_all[mine, :], both))
            through.append(dot(b_blk_all[mine, :], drv))
            at = pl.ds(pl.multiple_of(base * half + c * CHUNK * half, CHUNK * half), CHUNK * half)
            expo.append(dot(ones_blk, exp_all[at, :].astype(bf16)))
            dcm.append((across(dm_low[span], both) * diag).astype(bf16))
            dbm.append((across(step_low[span], drv) * diag).astype(bf16))
        whole = lambda parts: jnp.concatenate(parts, axis=0)
        skip = skip_ref[...]
        z = z_ref[here, :]
        sigma = jax.nn.sigmoid(z)
        mixed = whole(y) + skip * act
        gated_ref[here, :] = (mixed * (z * sigma)).astype(bf16)
        d_z_ref[here, :] = (d_gated_ref[here, :] * mixed * (sigma * (1.0 + z * (1.0 - sigma)))).astype(bf16)
        via = whole(through)
        d_act_ref[here, :] = d_mixed * skip + via * delta_all[here, :]
        dt_raw = dot(low, w_dt_ref[...]) + dt_bias_ref[...]
        d_dt_raw = (whole(expo) + via * act) * jax.nn.sigmoid(dt_raw)
        d_dt = d_dt_raw.astype(bf16)
        d_dt_ref[here, :] = d_dt
        terms = across(d_dt, w_dt_ref[...]) + across(whole(dbm), pick_b) + across(whole(dcm), pick_c)

        @pl.when(tile == 0)
        def _():
            terms_ref[here, :] = terms

        @pl.when(tile != 0)
        def _():
            terms_ref[here, :] += terms

        total = lambda v: jnp.sum(v, axis=0, keepdims=True)
        return by_bias + total(d_dt_raw), by_skip + total(d_mixed * act)

    none = jnp.zeros((1, channels), f32)
    by_bias, by_skip = lax.fori_loop(0, tokens // LANES, finish, (none, none), unroll=2)
    sums_ref[0:8, :] = jnp.broadcast_to(by_bias, (8, channels))
    sums_ref[8:16, :] = jnp.broadcast_to(by_skip, (8, channels))


def scans(proj, act_low, z_inner, d_gated, w_dt, dt_bias, a_neg, d_skip, begins):
    tokens, channels = act_low.shape
    states = a_neg.shape[0]
    tile = LANES if channels % LANES == 0 else channels
    wide = CHUNK * states
    w_dt = jnp.pad(w_dt, ((0, 2 * states), (0, 0)))
    col = lambda: pl.BlockSpec((tokens, tile), lambda j: (0, j))
    rows = lambda n: pl.BlockSpec((n, tile), lambda j: (0, j))
    full = lambda: pl.BlockSpec(proj.shape, lambda j: (0, 0))
    if z_inner.shape[1] % tile or tile % LANES:
        z_inner = z_inner[:, -channels:]
    ahead = (z_inner.shape[1] - channels) // tile
    z_col = pl.BlockSpec((tokens, tile), lambda j: (0, ahead + j))
    sds = jax.ShapeDtypeStruct
    return pl.pallas_call(
        functools.partial(scan_kernel, begins.shape[1], states),
        grid=(channels // tile,),
        in_specs=[
            pl.BlockSpec(memory_space=pltpu.SMEM),
            full(),
            col(),
            z_col,
            col(),
            rows(w_dt.shape[0]),
            rows(1),
            rows(states),
            rows(1),
        ],
        out_specs=[col(), col(), col(), col(), rows(states), rows(16), full()],
        out_shape=[
            sds((tokens, channels), bf16),
            sds((tokens, channels), bf16),
            sds((tokens, channels), bf16),
            sds((tokens, channels), f32),
            sds((states, channels), f32),
            sds((16, channels), f32),
            sds(proj.shape, f32),
        ],
        scratch_shapes=[pltpu.VMEM((tokens * states, tile), f32)] * 4
        + [pltpu.VMEM((tokens, wide), bf16)] * 2
        + [pltpu.VMEM((tokens, tile), f32)] * 3
        + [pltpu.VMEM((tokens * states // 2, tile), f32)],
        compiler_params=pltpu.CompilerParams(vmem_limit_bytes=62 * 2**20, dimension_semantics=("arbitrary",)),
        cost_estimate=pl.CostEstimate(
            flops=tokens * channels * states * 60,
            bytes_accessed=tokens * channels * 24,
            transcendentals=2 * tokens * channels * states,
        ),
        name="scan_all",
    )(begins, proj, act_low, z_inner, d_gated, w_dt, dt_bias[None], a_neg, d_skip[None])


EPSILON = 1e-06
HIGHEST = lax.Precision.HIGHEST


def low_dot(left, right):
    return jnp.dot(left, right, preferred_element_type=f32)


def dot_across(left, right):
    return lax.dot_general(left, right, (((1,), (1,)), ((), ())), preferred_element_type=f32)


def dot_tokens(left, right):
    return lax.dot_general(left, right, (((0,), (0,)), ((), ())), preferred_element_type=f32)


def delay_rows(operand, lag):
    if lag == 0:
        return operand
    padding = jnp.zeros((lag,) + operand.shape[1:], operand.dtype)
    return jnp.concatenate([padding, operand[:-lag]], axis=0)


def advance_rows(operand, lag):
    if lag == 0:
        return operand
    padding = jnp.zeros((lag,) + operand.shape[1:], operand.dtype)
    return jnp.concatenate([operand[lag:], padding], axis=0)


def after(x, *others):
    others = tuple(jax.tree.leaves(others))
    return lax.optimization_barrier((x, others))[0] if others else x


class Steps:
    def __init__(self, steps):
        self.steps = steps
        self.result = self.sent = self.arrived = None
        next(steps)

    def go(self, *others):
        if self.result is None:
            try:
                self.sent, self.arrived = self.steps.send(others)
            except StopIteration as stop:
                self.result = stop.value
        return self.arrived

    def end(self, *others):
        while self.result is None:
            self.go(*others)
        return self.result


def silu_slope(operand):
    squash = jax.nn.sigmoid(operand)
    return squash * (1.0 + operand * (1.0 - squash))


class Ring:
    def __init__(self):
        self.n = lax.axis_size("chan")
        self.down = 4 if self.n % 8 == 0 else 1
        self.across = self.n // self.down
        order = [self.at(p) for p in range(self.n)]
        self.right = [(order[k], order[(k + 1) % self.n]) for k in range(self.n)]
        self.left = [(b, a) for a, b in self.right]
        index = lax.axis_index("chan")
        i, j = index // self.across, index % self.across
        back = self.down - 1 - i
        step = jnp.where(back % 2 == 0, j - 1, self.across - 1 - j)
        self.place = jnp.where(j == 0, i, self.down + back * (self.across - 1) + step)

    def at(self, p):
        if self.down == 1:
            return p
        back, step = (p - self.down) // (self.across - 1), (p - self.down) % (self.across - 1)
        if isinstance(p, int):
            column = 1 + step if back % 2 == 0 else self.across - 1 - step
            return p * self.across if p < self.down else (self.down - 1 - back) * self.across + column
        column = jnp.where(back % 2 == 0, 1 + step, self.across - 1 - step)
        return jnp.where(p < self.down, p * self.across, (self.down - 1 - back) * self.across + column)

    def owner(self, away):
        p = self.place + away
        if away > 0:
            p = jnp.where(p >= self.n, p - self.n, p)
        elif away < 0:
            p = jnp.where(p < 0, p + self.n, p)
        return self.at(p)

    def go_right(self, x):
        return lax.ppermute(x, "chan", self.right)

    def go_left(self, x):
        return lax.ppermute(x, "chan", self.left)

    def blocks(self, x):
        half = self.n // 2
        cut = x.shape[0] // 2
        pair = x, x
        found = [(self.owner(0), x)]
        waits = yield
        for step in range(1, half):
            sent = after(pair, waits)
            pair = self.go_right(sent[0]), self.go_left(sent[1])
            found += [(self.owner(-step), pair[0]), (self.owner(step), pair[1])]
            waits = yield sent, pair
        sent = after((pair[0][:cut], pair[1][cut:]), waits)
        pair = self.go_right(sent[0]), self.go_left(sent[1])
        yield sent, pair
        return found + [(self.owner(half), jnp.concatenate(pair, axis=0))]

    def scatter(self, part):
        half = self.n // 2
        rows = part.shape[0] // self.n
        cut = rows // 2
        mine = lambda away: lax.dynamic_slice_in_dim(part, self.owner(away) * rows, rows, 0)
        wide = lambda v: v.astype(f32)
        far = mine(half)
        right, left = yield far[:cut], far[cut:]
        for away in range(half - 1, 0, -1):
            ahead, behind = wide(mine(away)), wide(mine(-away))
            if away == half - 1:
                ahead = jnp.concatenate([ahead[:cut] + wide(right), ahead[cut:]], axis=0)
                behind = jnp.concatenate([behind[:cut], behind[cut:] + wide(left)], axis=0)
            else:
                ahead, behind = ahead + wide(right), behind + wide(left)
            right, left = yield ahead.astype(bf16), behind.astype(bf16)
        return wide(mine(0)) + wide(right) + wide(left)

    def hop(self, sums, *others):
        self.land(self.launch(sums, *others))

    def launch(self, sums, *others):
        sums = [one for one in sums if one.result is None]
        if not sums:
            return sums, None
        join = lambda side: jnp.concatenate([one.pair[side] for one in sums], axis=0)
        right, left = lax.optimization_barrier((join(0), join(1), tuple(jax.tree.leaves(others))))[:2]
        return sums, (self.go_right(right), self.go_left(left))

    def land(self, flight, *others):
        sums, pair = flight
        if not sums:
            return
        right, left = lax.optimization_barrier((pair, tuple(jax.tree.leaves(others))))[0]
        at = 0
        for one in sums:
            rows = one.pair[0].shape[0]
            one.take((right[at : at + rows], left[at : at + rows]))
            at += rows


class Scatter:
    def __init__(self, ring, part):
        self.steps = ring.scatter(part)
        self.result, self.arrived = None, None
        self.pair = next(self.steps)

    def take(self, arrived):
        self.arrived = arrived
        try:
            self.pair = self.steps.send(arrived)
        except StopIteration as stop:
            self.result = stop.value


def is_power(n):
    return n & (n - 1) == 0


def bits_of(n):
    return [1 << b for b in range(n.bit_length() - 1)]


def sum_chan(x, wire):
    n = lax.axis_size("chan")
    index = lax.axis_index("chan")
    waits = yield
    if not is_power(n) or x.shape[0] % (16 * n):
        return lax.psum(after(x, waits), "chan")
    perm = lambda b: [(i, i ^ b) for i in range(n)]
    for b in bits_of(n):
        h = x.shape[0] // 2
        upper = (index // b) % 2
        keep = lax.dynamic_slice_in_dim(x, upper * h, h, 0)
        send = lax.dynamic_slice_in_dim(x, (1 - upper) * h, h, 0).astype(wire)
        send = after(send, waits)
        other = lax.ppermute(send, "chan", perm(b))
        waits = yield send, other
        x = keep + other.astype(f32)
    x = x.astype(wire)
    for b in reversed(bits_of(n)):
        upper = (index // b) % 2
        x = after(x, waits)
        other = lax.ppermute(x, "chan", perm(b))
        waits = yield x, other
        x = jnp.concatenate([jnp.where(upper == 0, x, other), jnp.where(upper == 0, other, x)], axis=0)
    return after(x, waits)


def small_gather(x, axis):
    n = lax.axis_size(axis)
    waits = yield
    if not is_power(n) or n > 8:
        return lax.all_gather(after(x, waits), axis, axis=0)
    index = lax.axis_index(axis)
    x = x[None]
    for b in bits_of(n):
        x = after(x, waits)
        other = lax.ppermute(x, axis, [(i, i ^ b) for i in range(n)])
        waits = yield x, other
        other = after(other, waits)
        lower = (index // b) % 2 == 0
        x = jnp.concatenate([jnp.where(lower, x, other), jnp.where(lower, other, x)], axis=0)
    return x


def small_sum(x, axis):
    n = lax.axis_size(axis)
    waits = yield
    if not is_power(n) or n > 8:
        return lax.psum(after(x, waits), axis)
    for b in bits_of(n):
        x = after(x, waits)
        other = lax.ppermute(x, axis, [(i, i ^ b) for i in range(n)])
        waits = yield x, other
        x = x + after(other, waits)
    return x


def join_kernel(upper_ref, mine_ref, other_ref, out_ref):
    k = pl.program_id(0)

    @pl.when(k == upper_ref[0])
    def _():
        out_ref[...] = mine_ref[...]

    @pl.when(k != upper_ref[0])
    def _():
        out_ref[...] = other_ref[...]


def join_halves(mine, other):
    rows, half = mine.shape
    fixed = lambda: pl.BlockSpec((rows, half), lambda k, upper_ref: (0, 0))
    return pl.pallas_call(
        join_kernel,
        grid_spec=pltpu.PrefetchScalarGridSpec(
            num_scalar_prefetch=1,
            grid=(2,),
            in_specs=[fixed(), fixed()],
            out_specs=pl.BlockSpec((rows, half), lambda k, upper_ref: (0, k)),
        ),
        out_shape=jax.ShapeDtypeStruct((rows, 2 * half), f32),
        compiler_params=pltpu.CompilerParams(vmem_limit_bytes=24 * 2**20, dimension_semantics=("arbitrary",)),
        cost_estimate=pl.CostEstimate(flops=0, bytes_accessed=rows * half * 16, transcendentals=0),
        name="join_halves",
    )((lax.axis_index("rows") % 2).astype(jnp.int32)[None], mine, other)


def sum_grad(left, right, wire):
    n = lax.axis_size("rows")
    waits = yield
    left = after(left, waits)
    if n != 4:
        return lax.psum(dot_tokens(left, right), "rows")
    core = [(0, 1), (1, 0), (2, 3), (3, 2)]
    chip = [(0, 2), (2, 0), (1, 3), (3, 1)]
    low, high = right
    send = dot_tokens(left, high)
    other = lax.ppermute(send, "rows", core)
    waits = yield send, other
    pair = (dot_tokens(after(left, send), low) + after(other, waits)).astype(wire)
    other = lax.ppermute(pair, "rows", chip)
    waits = yield pair, other
    total = pair.astype(f32) + after(other, waits).astype(f32)
    other = lax.ppermute(total, "rows", core)
    waits = yield total, other
    return join_halves(total, after(other, waits))


def core_halves(x):
    if lax.axis_size("rows") != 4:
        return x
    half = x.shape[1] // 2
    upper = lax.axis_index("rows") % 2
    part = lambda which: lax.dynamic_slice_in_dim(x, which * half, half, 1)
    return part(upper), part(1 - upper)


def place_norm_kernel(n_seq, count, owners_ref, begins_ref, mod_ref, *refs):
    blocks, (xmod_ref, normed_ref, held) = refs[:count], refs[-3:]
    rows, width = xmod_ref.shape
    step = 2 * CHUNK if rows % (2 * CHUNK) == 0 else rows
    k = pl.program_id(0)
    base = owners_ref[k] * rows

    def hold(block_ref):
        held[...] = block_ref[...]

    for i in range(count):
        pl.when(k == i)(functools.partial(hold, blocks[i]))
    shift, scale = mod_ref[0:1, :], mod_ref[1:2, :]
    gain = mod_ref[3 * n_seq : 3 * n_seq + 1, :]
    for start in range(0, rows, step):
        here = slice(start, start + step)
        wide = held[here, :].astype(f32)
        centred = wide - jnp.sum(wide, axis=1, keepdims=True) * (1.0 / width)
        square = jnp.sum(centred * centred, axis=1, keepdims=True) * (1.0 / width)
        normed = centred * lax.rsqrt(square + EPSILON)
        token = base + start + lax.broadcasted_iota(jnp.int32, (step, 1), 0)
        add, by = shift, gain * (1.0 + scale)
        for s in range(1, n_seq):
            later = token >= begins_ref[0, s]
            add = jnp.where(later, mod_ref[3 * s : 3 * s + 1, :], add)
            by = jnp.where(later, gain * (1.0 + mod_ref[3 * s + 1 : 3 * s + 2, :]), by)
        xmod_ref[here, :] = (normed * by + add).astype(bf16)
        normed_ref[here, :] = normed.astype(bf16)


def place_gate_kernel(n_seq, count, owners_ref, begins_ref, mod_ref, *refs):
    blocks, (gated_ref, plain_ref) = refs[:count], refs[-2:]
    rows = gated_ref.shape[0]
    step = CHUNK if rows % CHUNK == 0 else rows
    k = pl.program_id(0)
    base = owners_ref[k] * rows

    def fill(block_ref):
        def part(p, carry):
            here = pl.ds(pl.multiple_of(p * step, step), step)
            low = block_ref[here, :]
            token = base + p * step + lax.broadcasted_iota(jnp.int32, (step, 1), 0)
            gate = mod_ref[2:3, :]
            for s in range(1, n_seq):
                gate = jnp.where(token >= begins_ref[0, s], mod_ref[3 * s + 2 : 3 * s + 3, :], gate)
            gated_ref[here, :] = (low.astype(f32) * gate).astype(bf16)
            plain_ref[here, :] = low
            return carry

        lax.fori_loop(0, rows // step, part, 0)

    for i in range(count):
        pl.when(k == i)(functools.partial(fill, blocks[i]))


def place(kernel, blocks, begins, mod, name, total, scratch=False, into=()):
    owners = jnp.stack([owner for owner, _ in blocks]).astype(jnp.int32)
    parts = [block for _, block in blocks]
    rows, width = parts[0].shape
    count = len(parts)
    whole = jax.ShapeDtypeStruct((total, width), bf16)
    held = [pl.BlockSpec(memory_space=pl.ANY)] * len(into)
    out = lambda: pl.BlockSpec((rows, width), lambda k, owners_ref, begins_ref: (owners_ref[k], 0))
    fixed = lambda shape: pl.BlockSpec(shape, lambda k, owners_ref, begins_ref: (0, 0))
    return pl.pallas_call(
        functools.partial(kernel, begins.shape[1], count),
        grid_spec=pltpu.PrefetchScalarGridSpec(
            num_scalar_prefetch=2,
            grid=(count,),
            in_specs=[fixed(mod.shape)] + [fixed((rows, width))] * count + held,
            out_specs=[out(), out()],
            scratch_shapes=[pltpu.VMEM((rows, width), bf16)] if scratch else [],
        ),
        out_shape=[whole, whole],
        input_output_aliases={3 + count + k: k for k in range(len(into))},
        compiler_params=pltpu.CompilerParams(vmem_limit_bytes=28 * 2**20, dimension_semantics=("arbitrary",)),
        cost_estimate=pl.CostEstimate(
            flops=count * rows * width * 20, bytes_accessed=count * rows * width * 6, transcendentals=0
        ),
        name=name,
    )(owners, begins, mod, *parts, *into)


def own_columns(x, part, *others):
    count = x.shape[1] // part

    def kernel(index_ref, x_ref, *refs):
        for p in range(count):

            @pl.when(index_ref[0] == p)
            def _():
                refs[-1][...] = x_ref[:, p * part : (p + 1) * part]

    return pl.pallas_call(
        kernel,
        in_specs=[pl.BlockSpec(memory_space=pltpu.SMEM), pl.BlockSpec(memory_space=pltpu.VMEM)]
        + [pl.BlockSpec(memory_space=pl.ANY)] * len(others),
        out_specs=pl.BlockSpec(memory_space=pltpu.VMEM),
        out_shape=jax.ShapeDtypeStruct((x.shape[0], part), x.dtype),
        name="own_columns",
    )(lax.axis_index("chan").astype(jnp.int32)[None], x, *others)


def sums_kernel(n_seq, begins_ref, share_ref, normed_ref, up_ref, branch_ref, out_ref):
    rows, width = share_ref.shape
    k = pl.program_id(0)

    @pl.when(k == 0)
    def _():
        out_ref[...] = jnp.zeros(out_ref.shape, f32)

    lanes = 2 * LANES if width % (2 * LANES) == 0 else width
    token = k * rows + lax.broadcasted_iota(jnp.int32, (rows, 1), 0)
    for at in range(0, width, lanes):
        cols = slice(at, at + lanes)
        share = share_ref[:, cols].astype(f32)
        terms = [share, share * normed_ref[:, cols].astype(f32)]
        terms.append(up_ref[:, cols].astype(f32) * branch_ref[:, cols].astype(f32))
        for j, term in enumerate(terms):
            rest = jnp.sum(term, axis=0, keepdims=True)
            for s in range(n_seq - 1, 0, -1):
                later = jnp.sum(jnp.where(token >= begins_ref[0, s], term, 0.0), axis=0, keepdims=True)
                at_row = j * n_seq + s
                mine = later if s == n_seq - 1 else later - after_it
                out_ref[at_row : at_row + 1, cols] += mine
                after_it = later
            out_ref[j * n_seq : j * n_seq + 1, cols] += rest - (after_it if n_seq > 1 else 0.0)


def token_sums(share, normed, up, branch, begins):
    tokens, width = share.shape
    n_seq = begins.shape[1]
    rows = LANES
    spec = lambda: pl.BlockSpec((rows, width), lambda k: (k, 0))
    height = 3 * n_seq + (-3 * n_seq % 8)
    return pl.pallas_call(
        functools.partial(sums_kernel, n_seq),
        grid=(tokens // rows,),
        in_specs=[pl.BlockSpec(memory_space=pltpu.SMEM), spec(), spec(), spec(), spec()],
        out_specs=pl.BlockSpec((height, width), lambda k: (0, 0)),
        out_shape=jax.ShapeDtypeStruct((height, width), f32),
        compiler_params=pltpu.CompilerParams(vmem_limit_bytes=32 * 2**20, dimension_semantics=("arbitrary",)),
        cost_estimate=pl.CostEstimate(flops=tokens * width * 12, bytes_accessed=tokens * width * 8, transcendentals=0),
        name="token_sums",
    )(begins, share, normed, up, branch)


def local(
    activations,
    condition,
    seq_lengths,
    w_ada,
    b_ada,
    norm_gain,
    w_in_x,
    w_in_z,
    conv_weight,
    conv_bias,
    w_xproj,
    w_dt,
    dt_bias,
    a_log,
    d_skip,
    w_out,
    grad_out,
):
    ring = Ring()
    tok_loc, width = activations.shape
    low_rank = w_dt.shape[0]
    states = a_log.shape[1]
    channels = a_log.shape[0]
    conv_taps = conv_weight.shape[1]
    tok_count = tok_loc * ring.n
    tok_start = lax.axis_index("chan") * tok_loc
    act_ring = Steps(ring.blocks(activations))
    act_in = [act_ring.go()]
    cond_act = jax.nn.silu(condition.astype(f32)).astype(bf16)
    modulation = (
        jnp.einsum("si,kji->skj", cond_act, w_ada, preferred_element_type=f32) + b_ada[None]
    )
    part_width = norm_gain.shape[0]
    seq_count = seq_lengths.shape[1]
    packed = jnp.concatenate([modulation.reshape(3 * seq_count, part_width), norm_gain[None]], axis=0)
    packing = Steps(small_gather(packed, "chan"))
    packing.go()
    act_in.append(act_ring.go())
    packing.go(act_in[0])
    seq_lengths, conv_weight, conv_bias, w_dt, dt_bias, a_log, d_skip = after(
        (seq_lengths, conv_weight, conv_bias, w_dt, dt_bias, a_log, d_skip), act_in[0]
    )
    w_in = after(jnp.concatenate([w_in_x, w_in_z], axis=0), act_in[0])
    seq_lens = seq_lengths[0]
    seq_ends = jnp.cumsum(seq_lens)
    begins = seq_ends - seq_lens
    position = jnp.arange(tok_count, dtype=jnp.int32)
    member = (position[:, None] >= begins[None, :]) & (position[:, None] < seq_ends[None, :])
    onehot = member.astype(f32)
    in_seq = jnp.sum(onehot * (position[:, None] - begins[None, :]).astype(f32), axis=1)
    per_token = lambda rows, hot: sum(hot[:, s : s + 1] * rows[s][None] for s in range(seq_count))
    a_neg = -jnp.exp(a_log).T
    act_in.append(act_ring.go(w_in, in_seq))
    packing.go(act_in[1])
    far_wait = packing.arrived
    packed = packing.end().transpose(1, 0, 2).reshape(3 * seq_count + 1, width)
    packed = jnp.pad(packed, ((0, -packed.shape[0] % 8), (0, 0)))
    mod_full = packed[: 3 * seq_count].reshape(seq_count, 3, width)
    gain_full = packed[3 * seq_count]
    act_ring.go(far_wait)
    act_blocks = act_ring.end()
    soon = 5 if len(act_blocks) == 8 else 0
    norm = functools.partial(place, place_norm_kernel, begins=begins[None], mod=packed, total=tok_count, scratch=True)
    so_far = tuple(norm(act_blocks[:soon], name="place_norm_soon")) if soon else ()
    up_ring = Steps(ring.blocks(after(grad_out, act_in[-1])))
    up_in = [up_ring.go()]
    xmod, normed = norm(act_blocks[soon:], name="place_norm", into=so_far)
    inner = dot_across(xmod, w_in)
    x_inner = inner[:, :channels]
    xmod_halves = core_halves(after(xmod, inner))
    conv_pre = jnp.zeros_like(x_inner) + conv_bias[None, :]
    for tap_index in range(conv_taps):
        lag = conv_taps - 1 - tap_index
        valid = (in_seq >= lag).astype(f32)[:, None]
        conv_pre = conv_pre + conv_weight[:, tap_index][None, :] * delay_rows(x_inner, lag) * valid
    act_low = jax.nn.silu(conv_pre).astype(bf16)
    up_in.append(up_ring.go())
    adding = Steps(sum_chan(low_dot(act_low, w_xproj), PROJ_WIRE))
    adding.go(up_in[0])
    adding.go()
    adding.go(up_in[1])
    up_in.append(up_ring.go())
    adding.go()
    adding.go(up_in[2])
    up_ring.go()
    proj = adding.end()
    dt_low = proj[:, :low_rank].astype(bf16)
    d_branch_all, whole_up = place(
        place_gate_kernel, up_ring.end(), begins[None], packed, "place_gate", tok_count
    )
    d_gated = dot_across(d_branch_all, w_out)
    gated, d_z_low, d_dt_low, d_act, d_log, bias_skip, proj_terms = scans(
        proj, act_low, inner, d_gated, w_dt, dt_bias, a_neg, d_skip, begins[None]
    )
    adding = Steps(sum_chan(proj_terms, DPROJ_WIRE))
    branch_part = lax.optimization_barrier(low_dot(gated, w_out).astype(bf16))
    branch_sum = Scatter(ring, branch_part)
    adding.go()
    ring.hop([branch_sum])
    out_rows = Steps(sum_grad(gated, core_halves(d_branch_all), bf16))
    in_z_rows = Steps(sum_grad(d_z_low, xmod_halves, bf16))
    out_rows.go(branch_part)
    arrived = adding.arrived
    adding.go(out_rows.sent)
    in_z_rows.go(arrived)
    arrived = adding.arrived
    adding.go(in_z_rows.sent, branch_sum.arrived)
    flight = ring.launch([branch_sum])
    out_rows.go(arrived)
    arrived = adding.arrived
    adding.go(out_rows.sent)
    in_z_rows.go(arrived)
    adding.go(in_z_rows.sent)
    adding.go()
    d_proj = adding.end().astype(bf16)
    ring.land(flight, adding.arrived)
    d_act = d_act + dot_across(d_proj, w_xproj)
    d_conv = d_act * silu_slope(conv_pre)
    d_x_inner = jnp.zeros_like(d_conv)
    tap_grads = []
    for tap_index in range(conv_taps):
        lag = conv_taps - 1 - tap_index
        valid = (in_seq >= lag).astype(f32)[:, None]
        masked = d_conv * valid
        ahead = advance_rows(masked, lag)
        tap_grads.append(jnp.sum(ahead * x_inner, axis=0))
        d_x_inner = d_x_inner + conv_weight[:, tap_index][None, :] * ahead
    d_x_low = d_x_inner.astype(bf16)
    in_x_rows = Steps(sum_grad(d_x_low, xmod_halves, bf16))
    d_xmod_part = (low_dot(d_x_low, w_in_x) + low_dot(d_z_low, w_in_z)).astype(bf16)
    d_xmod_part = lax.optimization_barrier(d_xmod_part)
    in_x_rows.go(d_xmod_part)
    d_xmod_sum = Scatter(ring, d_xmod_part)
    both = [branch_sum, d_xmod_sum]
    ring.hop(both)
    first = d_xmod_sum.arrived
    ring.hop(both)
    share = after(d_xmod_part, first)
    summing = Steps(small_sum(token_sums(share, normed, whole_up, branch_part, begins[None]), "chan"))
    summing.go()
    in_x_rows.go(first)
    out_rows.go(first)
    rows_now = jnp.concatenate([modulation[:, 1], cond_act.astype(f32).reshape(-1, part_width)], axis=0)
    knowing = Steps(small_gather(rows_now, "rows"))
    knowing.go(first)
    d_proj = after(d_proj, first)
    small = jnp.concatenate(
        [
            dot_tokens(d_proj, act_low),
            dot_tokens(dt_low, d_dt_low),
            d_log * a_neg,
            jnp.stack(tap_grads),
            jnp.sum(d_conv, axis=0)[None],
            bias_skip[0:1],
            bias_skip[8:9],
        ],
        axis=0,
    )
    small = jnp.pad(small, ((0, -small.shape[0] % 16), (0, 0)))
    small_rows = Steps(small_sum(small, "rows"))
    small_rows.go()
    second = d_xmod_sum.arrived
    ring.hop(both, summing.sent, in_x_rows.sent, out_rows.sent, small_rows.sent)
    summing.go(second)
    in_z_rows.go(second)
    small_rows.go(second)
    knowing.go(second)
    grad_w_out = out_rows.end(second)
    third = d_xmod_sum.arrived
    ring.hop(both, summing.sent, in_z_rows.sent, small_rows.sent, grad_w_out)
    summing.go(third)
    known = knowing.end(third)
    scale_all = known[:, :seq_count].reshape(-1, part_width)
    cond_all = jnp.tile(known[:, seq_count:].reshape(-1, width).astype(bf16), (3, 1))
    in_x_rows.go(third)
    grad_w_in_z = in_z_rows.end(third)
    grad_w_in_x = in_x_rows.end()
    while d_xmod_sum.result is None:
        ring.hop(both)
    last = d_xmod_sum.arrived
    branch, d_xmod = branch_sum.result, d_xmod_sum.result
    sums = own_columns(summing.end(last), part_width, grad_w_in_z, grad_w_in_x)
    reaching = Steps(small_gather(sums, "rows"))
    reaching.go()
    reaching.go()
    reach = reaching.end()
    small = small_rows.end(last)
    onehot_loc = lax.dynamic_slice_in_dim(onehot, tok_start, tok_loc, 0)
    counts = [w_xproj.shape[1], low_rank, states, conv_taps, 1, 1, 1]
    pieces, at = [], 0
    for count in counts:
        pieces.append(small[at : at + count])
        at += count
    by_shift, by_scale, by_gate = [
        reach[:, k * seq_count : (k + 1) * seq_count].reshape(-1, part_width) for k in range(3)
    ]
    grad_gain = jnp.sum(by_scale * (1.0 + scale_all), axis=0)
    d_mod_all = jnp.concatenate([by_shift, by_scale * norm_gain[None], by_gate], axis=1)
    grad_b_ada = jnp.sum(d_mod_all, axis=0).reshape(3, part_width)
    high = d_mod_all.astype(bf16)
    rest = d_mod_all - high.astype(f32)
    middle = rest.astype(bf16)
    split = jnp.concatenate([high, middle, (rest - middle.astype(f32)).astype(bf16)], axis=0)
    grad_w_ada = dot_tokens(split, cond_all).reshape(3, part_width, width)
    block_out = (activations.astype(f32) + per_token(mod_full[:, 2], onehot_loc) * branch).astype(bf16)
    wide_loc = activations.astype(f32)
    centred_loc = wide_loc - jnp.mean(wide_loc, axis=1, keepdims=True)
    inv_std_loc = lax.rsqrt(jnp.mean(centred_loc * centred_loc, axis=1, keepdims=True) + EPSILON)
    normed_loc = centred_loc * inv_std_loc
    scale_loc = per_token(mod_full[:, 1], onehot_loc)
    d_normed = d_xmod * (1.0 + scale_loc) * gain_full[None, :]
    mean_first = jnp.mean(d_normed, axis=1, keepdims=True)
    mean_second = jnp.mean(d_normed * normed_loc, axis=1, keepdims=True)
    grad_input = (
        inv_std_loc * (d_normed - mean_first - normed_loc * mean_second) + grad_out.astype(f32)
    ).astype(bf16)
    return (
        block_out,
        grad_input,
        grad_w_ada,
        grad_b_ada,
        grad_gain,
        grad_w_in_x,
        grad_w_in_z,
        pieces[3].T,
        pieces[4][0],
        pieces[0].T,
        pieces[1],
        pieces[5][0],
        pieces[2].T,
        pieces[6][0],
        grad_w_out,
    )


PROJ_WIRE = bf16
DPROJ_WIRE = bf16


def solution(mesh):
    return jax.shard_map(
        local,
        mesh=mesh,
        in_specs=(
            P(("rows", "chan"), None),
            P("rows", None),
            P("rows", None),
            P(None, "chan", None),
            P(None, "chan"),
            P("chan"),
            P("chan", None),
            P("chan", None),
            P("chan", None),
            P("chan"),
            P("chan", None),
            P(None, "chan"),
            P("chan"),
            P("chan", None),
            P("chan"),
            P("chan", None),
            P(("rows", "chan"), None),
        ),
        out_specs=(
            P(("rows", "chan"), None),
            P(("rows", "chan"), None),
            P(None, "chan", None),
            P(None, "chan"),
            P("chan"),
            P("chan", None),
            P("chan", None),
            P("chan", None),
            P("chan"),
            P("chan", None),
            P(None, "chan"),
            P("chan"),
            P("chan", None),
            P("chan"),
            P("chan", None),
        ),
        check_vma=False,
    )
```
